32 devices in a mesh: seq: 16 (over z, x, core), row: 2 (over y).
Axes of the slice: x: 2, y: 2, z: 4, core: 2. Of those that a mesh axis runs over, the one named last changes fastest.
Arguments:
- latents: bfloat16 [2, 16, 1024, 1024], P(None, 'seq', 'row'), may hold values from -6 to 6
- segments: int32 [2, 16, 1024], P(None, 'seq'), may hold values from -1 to 1, as said below
- attention_weights: bfloat16 [3, 1024, 1024], P(None, ('seq', 'row')), may hold values from -0.1875 to 0.1875
- output_weight: bfloat16 [1024, 1024], P(('seq', 'row')), may hold values from -0.75 to 0.75
- hidden_weights: bfloat16 [2, 1024, 1024], P(None, ('seq', 'row')), may hold values from -0.1875 to 0.1875
- gains: bfloat16 [2, 1024], P(None, ('seq', 'row')), may hold values from 0.5 to 1.5
- biases: bfloat16 [7, 1024], P(None, ('seq', 'row')), may hold values from -1 to 1
- cotangent: bfloat16 [2, 16, 1024, 1024], P(None, 'seq', 'row'), may hold values from -6 to 6
Outputs:
- activations: bfloat16 [2, 16, 1024, 1024], P(None, 'seq', 'row')
- latent_grads: float32 [2, 16, 1024, 1024], P(None, 'seq', 'row')
- attention_weight_grads: float32 [3, 1024, 1024], P(None, ('seq', 'row'))
- output_weight_grad: float32 [1024, 1024], P(('seq', 'row'))
- hidden_weight_grads: float32 [2, 1024, 1024], P(None, ('seq', 'row'))
- gain_grads: float32 [2, 1024], P(None, ('seq', 'row'))
- bias_grads: float32 [7, 1024], P(None, ('seq', 'row'))
The draws below stay inside these ranges and needn't reach their ends.
Inputs may be any that keep to these rules, and one draw needn't show every extreme that they name: `segments`: latent sets are runs of consecutive rows of one sequence, numbered from 0 within it; every sequence holds 2 sets, each of 256 to 512 rows, and rows after its last set are padding.
All inputs are finite; a program needn't handle non-finite values.
Results may differ from the reference program's by a relative error of at most 0.012.
Values may be sent and summed in bfloat16 or wider, within the bound.
No kernel may reach another device: no remote copies, remote signals or barrier semaphores. Data moves between devices by JAX's collectives and lax.ppermute only.
A program may use at most 256 MiB of HBM per device.

```python
import math
import jax
import jax.numpy as jnp
from jax import lax

D = 1024
HEADS = 8
SET = 512
LEN = 1024
MB = 2
BATCH = 16


def draw_segments(key, part):
    first_key, second_key = jax.random.split(jax.random.fold_in(key, 17))
    slot_count = LEN // SET
    slot_shape = (MB, BATCH, slot_count)
    coin = jax.random.randint(first_key, slot_shape, 0, 2)
    shorter = jax.random.randint(second_key, slot_shape, SET // 2, SET)
    set_sizes = jnp.where(coin == 0, SET, shorter).astype(jnp.int32)
    set_sizes = set_sizes.at[0, 0, slot_count - 1].set(shorter[0, 0, slot_count - 1])
    set_ends = jnp.cumsum(set_sizes, axis=-1)
    places = jnp.arange(LEN, dtype=jnp.int32)
    passed = (places[None, None, :, None] >= set_ends[:, :, None, :]).astype(jnp.int32)
    identity = jnp.sum(passed, axis=-1)
    return jnp.where(identity < slot_count, identity, -1).astype(jnp.int32)


def levels(rng, extent, pieces, smallest, largest):
    level, own = 1.0, jax.random.fold_in(rng, 6)
    for position, parts in pieces:
        heights = jnp.exp(jax.random.uniform(jax.random.fold_in(own, position), (parts,), jnp.float32, smallest / len(pieces), largest / len(pieces)))
        level = level * jnp.repeat(heights, extent[position] // parts).reshape([-1 if axis == position else 1 for axis in range(len(extent))])
    return level


def scatter_about(rng, extent, scale, bound, cuts=(), held_as=jnp.bfloat16):
    drawn = jax.random.normal(rng, extent, jnp.float32) * scale
    if len(cuts) > 0:
        drawn = levels(rng, extent, cuts, -0.22, 0.18) * drawn
    return jnp.clip(drawn, min=-bound, max=bound).astype(held_as)


def setup_inputs(seed: int = 0) -> dict:
    keys = jax.random.split(jax.random.key(seed), 9)
    return {
        "latents": scatter_about(keys[0], (MB, BATCH, LEN, D), 1.0, 6.0, ((1, 16), (2, 2))),
        "segments": draw_segments(jax.random.fold_in(keys[8], 71), 0),
        "attention_weights": scatter_about(keys[2], (3, D, D), D ** -0.5, 0.1875, ((1, 32),)),
        "output_weight": scatter_about(keys[3], (D, D), (D // 16) ** -0.5, 0.75, ((0, 32),)),
        "hidden_weights": scatter_about(keys[4], (2, D, D), D ** -0.5, 0.1875, ((1, 32),)),
        "gains": jnp.clip(1.0 + 0.1 * jax.random.normal(keys[5], (2, D), jnp.float32), 0.5, 1.5).astype(jnp.bfloat16),
        "biases": scatter_about(keys[6], (7, D), 0.2, 1.0, ((1, 32),)),
        "cotangent": scatter_about(keys[7], (MB, BATCH, LEN, D), 1.0, 6.0, ((1, 16), (2, 2))),
    }


@jax.custom_vjp
def low(v):
    return lax.optimization_barrier(v.astype(jnp.bfloat16)).astype(jnp.float32)

@jax.custom_vjp
def low_back(v):
    return v

def low_keep(v):
    return (low(v), None)

def low_pass(kept, grad):
    return (grad,)

def back_keep(v):
    return (v, None)

def back_low(kept, grad):
    return (low(grad),)
low.defvjp(low_keep, low_pass)
low_back.defvjp(back_keep, back_low)
EPSILON = 1e-05
HIGH = lax.Precision.HIGHEST

def layer_norm(vector, gain_row, offset):
    centre = vector - lax.optimization_barrier(jnp.mean(vector, axis=-1, keepdims=True))
    spread = lax.optimization_barrier(jnp.mean(centre * centre, axis=-1, keepdims=True))
    return centre * lax.rsqrt(spread + EPSILON) * gain_row + offset

def product(left, right):
    return jnp.dot(left, right, precision=HIGH)

def latent_block(inputs, segment_ids, attention_full, output_full, hidden_full, gain_full, bias_full):
    length, features = inputs.shape
    head_size = features // HEADS
    score_scale = 1.0 / math.sqrt(head_size)
    normed_low = low(layer_norm(inputs, gain_full[0], bias_full[0]))
    queries = low(low_back(product(normed_low, attention_full[0]) + bias_full[2]))
    key_rows = low(low_back(product(normed_low, attention_full[1])))
    value_rows = low(low_back(product(normed_low, attention_full[2]) + bias_full[3]))
    key_heads = key_rows.reshape(length, HEADS, head_size)
    value_heads = value_rows.reshape(length, HEADS, head_size)
    block_rows = min(512, length)
    block_count = length // block_rows

    def attend(slices):
        query_block, segment_block = slices
        scores = jnp.einsum('qhd,khd->hqk', query_block, key_heads, precision=HIGH) * score_scale
        same_set = (segment_block[:, None] == segment_ids[None, :])[None]
        scores = low_back(jnp.where(same_set, scores, -1e+30))
        row_max = lax.optimization_barrier(jnp.max(scores, axis=-1, keepdims=True))
        expos = jnp.exp(scores - row_max)
        weights_low = low(expos / lax.optimization_barrier(jnp.sum(expos, axis=-1, keepdims=True)))
        mixture = jnp.einsum('hqk,khd->qhd', weights_low, value_heads, precision=HIGH)
        return low(low_back(mixture.reshape(query_block.shape[0], features)))
    mixture = lax.map(jax.checkpoint(attend), (queries.reshape(block_count, block_rows, HEADS, head_size), segment_ids.reshape(block_count, block_rows)))
    mixture = mixture.reshape(length, features)
    attended = low_back(product(mixture, output_full) + bias_full[4])
    residual_one = inputs + attended
    hidden_low = low(layer_norm(residual_one, gain_full[1], bias_full[1]))
    hidden_pre = low_back(product(hidden_low, hidden_full[0]) + bias_full[5])
    active_low = low(jax.nn.gelu(hidden_pre))
    return residual_one + low_back(product(active_low, hidden_full[1]) + bias_full[6])

def reference(latents, segments, attention_weights, output_weight, hidden_weights, gains, biases, cotangent):
    attention_full = attention_weights.astype(jnp.float32)
    output_full = output_weight.astype(jnp.float32)
    hidden_full = hidden_weights.astype(jnp.float32)
    gain_full = gains.astype(jnp.float32)
    bias_full = biases.astype(jnp.float32)
    row_sets = latents.reshape(-1, LEN, D).astype(jnp.float32)
    segment_sets = segments.reshape(-1, LEN)
    grad_sets = cotangent.reshape(-1, LEN, D).astype(jnp.float32)

    def per_sequence(totals, slices):
        inputs, segment_ids, out_grad = slices

        def forward(rows_in, attn_in, outw_in, hidden_in, gain_in, bias_in):
            return latent_block(rows_in, segment_ids, attn_in, outw_in, hidden_in, gain_in, bias_in)
        result, pullback = jax.vjp(forward, inputs, attention_full, output_full, hidden_full, gain_full, bias_full)
        live_rows = (segment_ids >= 0).astype(jnp.float32)[:, None]
        gradients = pullback(out_grad * live_rows)
        new_totals = (totals[0] + gradients[1], totals[1] + gradients[2], totals[2] + gradients[3], totals[3] + gradients[4], totals[4] + gradients[5])
        return (new_totals, (result.astype(jnp.bfloat16), gradients[0]))
    initial = (jnp.zeros(attention_full.shape, jnp.float32), jnp.zeros(output_full.shape, jnp.float32), jnp.zeros(hidden_full.shape, jnp.float32), jnp.zeros(gain_full.shape, jnp.float32), jnp.zeros(bias_full.shape, jnp.float32))
    totals, (outputs, input_grads) = lax.scan(per_sequence, initial, (row_sets, segment_sets, grad_sets))
    full_shape = latents.shape
    return (outputs.reshape(full_shape), input_grads.reshape(full_shape), totals[0], totals[1], totals[2], totals[3], totals[4])
```

```python
import functools
import math

import jax
import jax.numpy as jnp
from jax import lax
from jax.experimental import pallas as pl
from jax.experimental.pallas import tpu as pltpu
from jax.sharding import PartitionSpec as P

HEADS = 8
EPSILON = 1e-05
AXES = ("seq", "row")
VMEM_LIMIT = 60 << 20
NN = (((1,), (0,)), ((), ()))
NT = (((1,), (1,)), ((), ()))
TN = (((0,), (0,)), ((), ()))
ORDERS = ((16, 1, 8, 4, 2), (16, 1, 4, 8, 2))


def offset_of(order, position):
    offset = 0
    for bit, mask in enumerate(order):
        if position >> bit & 1:
            offset ^= mask
    return offset


def dot(left, right, dims=NN):
    return lax.dot_general(left, right, dims, preferred_element_type=jnp.float32)


def shift(array, mask, count):
    return lax.ppermute(array, AXES, [(i, i ^ mask) for i in range(count)])


def gather_blocks(block, order):
    count = 1 << len(order)
    held = block[None]
    for mask in order[:-1]:
        held = jnp.concatenate([held, shift(held, mask, count)], axis=0)
    return held, shift(held, order[-1], count)


def scatter_blocks(keep, send, order):
    count = 1 << len(order)
    for mask in reversed(order):
        got = shift(send, mask, count)
        half = keep.shape[0] // 2
        if half == 0:
            return keep[0].astype(jnp.float32) + got[0].astype(jnp.float32)
        send = keep[half:] + got[half:]
        keep = keep[:half] + got[:half]


def place_weights(me, order, low_ref, high_ref, weight_ref, column, sem):
    depth = weight_ref.shape[1] // (1 << len(order))
    width = low_ref.shape[-1]
    half = low_ref.shape[0]
    for position in range(2 * half):
        source = low_ref if position < half else high_ref
        owner = me ^ offset_of(order, position)
        rows = pl.ds(pl.multiple_of(owner * depth, depth), depth)
        for matrix in range(3):
            pltpu.make_async_copy(
                source.at[position % half, pl.ds(matrix * depth, depth), :],
                weight_ref.at[matrix, rows, pl.ds(column, width)],
                sem,
            ).start()


def collect_grads(me, order, stage_ref, keep_ref, send_ref, sem):
    half = keep_ref.shape[0]
    depth = stage_ref.shape[1] // (2 * half)
    for position in reversed(range(2 * half)):
        target = keep_ref if position < half else send_ref
        owner = me ^ offset_of(order, position)
        rows = pl.ds(pl.multiple_of(owner * depth, depth), depth)
        for matrix in range(3):
            pltpu.make_async_copy(
                stage_ref.at[matrix, rows, :],
                target.at[position % half, pl.ds(matrix * depth, depth), :],
                sem,
            ).start()


def normalize(rows):
    mean = jnp.mean(rows, axis=-1, keepdims=True)
    centre = rows - mean
    spread = jnp.mean(centre * centre, axis=-1, keepdims=True)
    scale = lax.rsqrt(spread + EPSILON)
    return centre * scale, scale


def column_sum(rows):
    return jnp.sum(rows.astype(jnp.float32), axis=0, keepdims=True)


def project_first_kernel(me_ref, own_ref, other_ref, low_ref, high_ref, vec_ref, normed_ref, qkv_ref, w_ref, sem):
    step = pl.program_id(0)
    width = qkv_ref.shape[-1]

    @pl.when(step == 0)
    def _():
        place_weights(me_ref[0], ORDERS[0], low_ref, high_ref, w_ref, 0, sem)

    rows = jnp.where(step == 0, own_ref[...], other_ref[...]).astype(jnp.float32)
    normed, _ = normalize(rows)
    normed_ref[...] = (normed * vec_ref[0:1] + vec_ref[2:3]).astype(jnp.bfloat16)

    @pl.when(step == 0)
    def _():
        pltpu.make_async_copy(w_ref, w_ref, sem).wait()

    for matrix, bias in ((0, 4), (1, None), (2, 5)):
        out = dot(normed_ref[...], w_ref[matrix])
        if bias is not None:
            out = out + vec_ref[bias : bias + 1, 0:width]
        qkv_ref[matrix] = out.astype(jnp.bfloat16)


def project_next_kernel(me_ref, normed_ref, low_ref, high_ref, vec_ref, qkv_ref, w_ref, sem):
    step = pl.program_id(0)
    width = qkv_ref.shape[-1]

    @pl.when(step == 0)
    def _():
        place_weights(me_ref[0], ORDERS[1], low_ref, high_ref, w_ref, 0, sem)
        pltpu.make_async_copy(w_ref, w_ref, sem).wait()

    for matrix, bias in ((0, 4), (1, None), (2, 5)):
        out = dot(normed_ref[...], w_ref[matrix])
        if bias is not None:
            out = out + vec_ref[bias : bias + 1, width : 2 * width]
        qkv_ref[matrix] = out.astype(jnp.bfloat16)


def key_ranges(length):
    quarter = length // 4
    return ((0, 2 * quarter), (0, length), (quarter, length), (quarter, length))


def attend_kernel(scale, q_ref, k_ref, v_ref, column_ref, row_ref, mix_ref, prob_ref):
    length = q_ref.shape[1]
    quarter = length // 4
    for index, (first, last) in enumerate(key_ranges(length)):
        rows = slice(index * quarter, (index + 1) * quarter)
        scores = dot(q_ref[0, rows, :], k_ref[0, first:last, :], NT)
        same = column_ref[rows, :] == row_ref[:, first:last]
        scores = jnp.where(same, scores, -1e30)
        top = jnp.max(scores, axis=-1, keepdims=True)
        expo = jnp.exp((scores - top) * scale)
        total = jnp.sum(expo, axis=-1, keepdims=True)
        low = (expo * (1.0 / total)).astype(jnp.bfloat16)
        prob_ref[0, rows, first:last] = low
        mix_ref[rows, :] = dot(low, v_ref[0, first:last, :]).astype(jnp.bfloat16)


def attend_back_kernel(scale, q_ref, k_ref, v_ref, prob_ref, mix_ref, mixg_ref, out_ref, key_acc, value_acc):
    length = q_ref.shape[1]
    quarter = length // 4
    key_acc[...] = jnp.zeros_like(key_acc)
    value_acc[...] = jnp.zeros_like(value_acc)
    for index, (first, last) in enumerate(key_ranges(length)):
        rows = slice(index * quarter, (index + 1) * quarter)
        mix_grad = mixg_ref[rows, :]
        centred = jnp.sum(
            mix_grad.astype(jnp.float32) * mix_ref[rows, :].astype(jnp.float32), axis=-1, keepdims=True
        )
        grads = dot(mix_grad, v_ref[0, first:last, :], NT)
        low = prob_ref[0, rows, first:last]
        score_grads = (low.astype(jnp.float32) * (grads - centred)).astype(jnp.bfloat16)
        out_ref[0, rows, :] = (dot(score_grads, k_ref[0, first:last, :]) * scale).astype(jnp.bfloat16)
        key_acc[first:last, :] += dot(score_grads, q_ref[0, rows, :], TN)
        value_acc[first:last, :] += dot(low, mix_grad, TN)
    out_ref[1] = (key_acc[...] * scale).astype(jnp.bfloat16)
    out_ref[2] = value_acc[...].astype(jnp.bfloat16)


def project_back_kernel(order, me_ref, normed_ref, grad_ref, keep_ref, send_ref, sum_ref, stage_ref, sem):
    step = pl.program_id(0)
    stage_ref[step] = dot(normed_ref[...], grad_ref[0], TN).astype(jnp.bfloat16)
    sum_ref[0] = jnp.broadcast_to(column_sum(grad_ref[0]), sum_ref.shape[1:])

    @pl.when(step == 2)
    def _():
        collect_grads(me_ref[0], order, stage_ref, keep_ref, send_ref, sem)
        pltpu.make_async_copy(stage_ref, stage_ref, sem).wait()


def feed_kernel(
    me_ref, x_own_ref, x_other_ref, cot_own_ref, cot_other_ref, mix0_ref, mix1_ref, live_ref, vec_ref,
    low0_ref, high0_ref, low1_ref, high1_ref,
    result_ref, resg_ref, mixg_ref, sum_ref, keep0_ref, send0_ref, keep1_ref, send1_ref,
    w_ref, hid_ref, act_ref, og_ref, pre_ref, res_ref, resid, slope, stage_ref, w_sem, g_sem,
):
    step = pl.program_id(0)
    me = me_ref[0]
    half_rows = x_own_ref.shape[0]
    features = x_own_ref.shape[1]
    width = features // 2

    @pl.when(step == 0)
    def _():
        place_weights(me, ORDERS[0], low0_ref, high0_ref, w_ref, 0, w_sem)
        place_weights(me, ORDERS[1], low1_ref, high1_ref, w_ref, width, w_sem)
        sum_ref[...] = jnp.zeros_like(sum_ref)
        pltpu.make_async_copy(w_ref, w_ref, w_sem).wait()

    @pl.when(step < 2)
    def _():
        place = pl.multiple_of((step ^ (me & 1)) * half_rows, half_rows)
        rows = pl.ds(place, half_rows)
        inputs = jnp.where(step == 0, x_own_ref[...], x_other_ref[...]).astype(jnp.float32)
        attended = dot(mix0_ref[rows, :], w_ref[0, 0:width, :]) + dot(mix1_ref[rows, :], w_ref[0, width:, :])
        resid[...] = inputs + attended + vec_ref[6:7]
        normed, inverse = normalize(resid[...])
        hid_ref[rows, :] = (normed * vec_ref[1:2] + vec_ref[3:4]).astype(jnp.bfloat16)
        pre = dot(hid_ref[rows, :], w_ref[1]) + vec_ref[7:8]
        square = pre * pre
        tanh = jnp.tanh(0.7978845608 * pre * (1.0 + 0.044715 * square))
        act_ref[rows, :] = (0.5 * pre * (1.0 + tanh)).astype(jnp.bfloat16)
        slope[...] = 0.5 * (1.0 + tanh) + (0.5 * 0.7978845608) * pre * (1.0 - tanh * tanh) * (
            1.0 + (3 * 0.044715) * square
        )
        result = resid[...] + dot(act_ref[rows, :], w_ref[2]) + vec_ref[8:9]
        result_ref[0] = result.astype(jnp.bfloat16)
        live = live_ref[rows, :]
        cot = jnp.where(step == 0, cot_own_ref[...], cot_other_ref[...]).astype(jnp.float32)
        og_ref[rows, :] = (cot * live).astype(jnp.bfloat16)
        pre_grad = dot(og_ref[rows, :], w_ref[2], NT) * slope[...]
        pre_ref[rows, :] = pre_grad.astype(jnp.bfloat16)
        normed_grad = dot(pre_ref[rows, :], w_ref[1], NT)
        normed, inverse = normalize(resid[...])
        sum_ref[0:1] += column_sum(normed_grad * normed)
        sum_ref[1:2] += column_sum(normed_grad)
        scaled = normed_grad * vec_ref[1:2]
        resg = og_ref[rows, :].astype(jnp.float32) + inverse * (
            scaled
            - jnp.mean(scaled, axis=-1, keepdims=True)
            - normed * jnp.mean(scaled * normed, axis=-1, keepdims=True)
        )
        resg_ref[0] = resg
        res_ref[rows, :] = resg.astype(jnp.bfloat16)
        mixg_ref[...] = dot(res_ref[rows, :], w_ref[0], NT).astype(jnp.bfloat16)
        sum_ref[2:3] += column_sum(res_ref[rows, :])
        sum_ref[3:4] += column_sum(pre_ref[rows, :])
        sum_ref[4:5] += column_sum(og_ref[rows, :])

    @pl.when(step == 2)
    def _():
        for half, (order, keep_ref, send_ref) in enumerate(
            ((ORDERS[0], keep0_ref, send0_ref), (ORDERS[1], keep1_ref, send1_ref))
        ):
            columns = slice(half * width, (half + 1) * width)
            for part in range(2):
                mix_ref = (mix0_ref, mix1_ref)[part]
                out_rows = slice(part * width, (part + 1) * width)
                stage_ref[half, 0, out_rows, :] = dot(mix_ref[...], res_ref[:, columns], TN).astype(jnp.bfloat16)
            stage_ref[half, 1] = dot(hid_ref[...], pre_ref[:, columns], TN).astype(jnp.bfloat16)
            stage_ref[half, 2] = dot(act_ref[...], og_ref[:, columns], TN).astype(jnp.bfloat16)
            collect_grads(me, order, stage_ref.at[half], keep_ref, send_ref, g_sem.at[half])
        for half in range(2):
            pltpu.make_async_copy(stage_ref.at[half], stage_ref.at[half], g_sem.at[half]).wait()


def finish_kernel(
    me_ref, x_own_ref, x_other_ref, resg_ref, grad0_ref, grad1_ref, vec_ref, low0_ref, high0_ref, low1_ref, high1_ref,
    out_ref, other_ref, sum_ref, w_ref, sem,
):
    step = pl.program_id(0)
    me = me_ref[0]
    width = grad0_ref.shape[-1]

    @pl.when(step == 0)
    def _():
        place_weights(me, ORDERS[0], low0_ref, high0_ref, w_ref, 0, sem)
        place_weights(me, ORDERS[1], low1_ref, high1_ref, w_ref, width, sem)
        sum_ref[...] = jnp.zeros_like(sum_ref)
        pltpu.make_async_copy(w_ref, w_ref, sem).wait()

    normed_grad = None
    for matrix in range(3):
        for part, grad_ref in enumerate((grad0_ref, grad1_ref)):
            term = dot(grad_ref[matrix], w_ref[matrix, :, part * width : (part + 1) * width], NT)
            normed_grad = term if normed_grad is None else normed_grad + term
    rows = jnp.where(step == 1, x_own_ref[...], x_other_ref[...]).astype(jnp.float32)
    normed, inverse = normalize(rows)
    sum_ref[0:1] += column_sum(normed_grad * normed)
    sum_ref[1:2] += column_sum(normed_grad)
    scaled = normed_grad * vec_ref[0:1]
    total = resg_ref[0] + inverse * (
        scaled
        - jnp.mean(scaled, axis=-1, keepdims=True)
        - normed * jnp.mean(scaled * normed, axis=-1, keepdims=True)
    )

    @pl.when(step == 0)
    def _():
        other_ref[...] = total.astype(jnp.bfloat16)

    @pl.when(step == 1)
    def _():
        out_ref[0] = total


def call(kernel, grid, in_specs, out_specs, out_shape, scratch, flops, moved):
    return pl.pallas_call(
        kernel,
        grid_spec=pltpu.PrefetchScalarGridSpec(
            num_scalar_prefetch=1,
            grid=grid,
            in_specs=in_specs,
            out_specs=out_specs,
            scratch_shapes=scratch,
        ),
        out_shape=out_shape,
        compiler_params=pltpu.CompilerParams(
            dimension_semantics=("arbitrary",) * len(grid), vmem_limit_bytes=VMEM_LIMIT
        ),
        cost_estimate=pl.CostEstimate(flops=int(flops), bytes_accessed=int(moved), transcendentals=0),
    )


def struct(shape, dtype=jnp.bfloat16):
    return jax.ShapeDtypeStruct(shape, dtype)


def whole(shape):
    return pl.BlockSpec(shape, lambda *_: (0,) * len(shape))


ANY = pl.BlockSpec(memory_space=pl.ANY)


def whole_sequence(
    latents, segments, attention_weights, output_weight, hidden_weights, gains, biases, cotangent
):
    half_rows, features = latents.shape[2:]
    length = 2 * half_rows
    head_size = features // HEADS
    scale = 1.0 / math.sqrt(head_size)
    width = features // 2
    count = 1 << len(ORDERS[0])
    depth = features // count
    rank = lax.axis_index("row")
    device = lax.axis_index("seq") * 2 + rank
    me = device.astype(jnp.int32).reshape(1)
    bf16, f32 = jnp.bfloat16, jnp.float32

    vectors = jnp.concatenate([gains, biases], axis=0)
    vector_rows = vectors.shape[0]
    padded = jnp.zeros((16, width), bf16).at[:vector_rows, :depth].set(vectors)
    groups = (attention_weights, jnp.concatenate([output_weight[None], hidden_weights], axis=0))
    chunks = []
    for index, group in enumerate(groups):
        for half in range(2):
            block = group[:, :, half * width : (half + 1) * width].reshape(3 * depth, width)
            if index == 0 and half == 0:
                block = jnp.concatenate([block, padded], axis=0)
            chunks.append(gather_blocks(block, ORDERS[half]))
    (al0, ah0), (al1, ah1), (fl0, fh0), (fl1, fh1) = chunks

    offsets = jnp.array([offset_of(ORDERS[0], p) for p in range(count)], jnp.int32)
    owners = jnp.bitwise_xor(device.astype(jnp.int32), offsets)
    choose = (owners[:, None] == jnp.arange(count, dtype=jnp.int32)[None, :]).astype(f32)
    pieces = jnp.concatenate([al0, ah0], axis=0)[:, 3 * depth : 3 * depth + vector_rows, :depth].astype(f32)
    vec = jnp.einsum("pa,pkj->kaj", choose, pieces, precision=lax.Precision.HIGHEST)
    vec = vec.reshape(vector_rows, features)

    x_own = lax.dynamic_index_in_dim(latents[:, 0], rank, 0, keepdims=False)
    x_other = shift(lax.dynamic_index_in_dim(latents[:, 0], 1 - rank, 0, keepdims=False), 1, count)
    cot_own = lax.dynamic_index_in_dim(cotangent[:, 0], rank, 0, keepdims=False)
    cot_other = shift(lax.dynamic_index_in_dim(cotangent[:, 0], 1 - rank, 0, keepdims=False), 1, count)
    segment = lax.dynamic_index_in_dim(segments[:, 0], rank, 0, keepdims=False)
    segment_column = segment[:, None]
    segment_row = segment[None, :]
    live = (segment >= 0).astype(f32)[:, None]

    local = pl.BlockSpec((half_rows, features), lambda i, me: (i ^ (me[0] & 1), 0))
    local3 = pl.BlockSpec((3, half_rows, width), lambda i, me: (0, i ^ (me[0] & 1), 0))
    rows_spec = whole((half_rows, features))
    vec_spec = whole((vector_rows, features))
    w_half = [pltpu.VMEM((3, features, width), bf16), pltpu.SemaphoreType.DMA(())]
    dense = 2.0 * length * features * features

    normed_low, qkv0 = call(
        project_first_kernel, (2,), [rows_spec, rows_spec, ANY, ANY, vec_spec], [local, local3],
        [struct((length, features)), struct((3, length, width))], w_half, 1.5 * dense, 16e6,
    )(me, x_own, x_other, al0, ah0, vec)
    qkv1 = call(
        project_next_kernel, (2,),
        [pl.BlockSpec((half_rows, features), lambda i, me: (i, 0)), ANY, ANY, vec_spec],
        pl.BlockSpec((3, half_rows, width), lambda i, me: (0, i, 0)), struct((3, length, width)), w_half,
        1.5 * dense, 8e6,
    )(me, normed_low, al1, ah1, vec)

    heads = width // head_size
    head_specs = [
        pl.BlockSpec((1, length, head_size), functools.partial(lambda c, h, me: (c, 0, h), c)) for c in range(3)
    ]
    column_block = pl.BlockSpec((length, head_size), lambda h, me: (0, h))
    prob_block = pl.BlockSpec((1, length, length), lambda h, me: (h, 0, 0))

    def attend(qkv):
        return call(
            lambda me_ref, *refs: attend_kernel(scale, *refs), (heads,),
            head_specs + [whole((length, 1)), whole((1, length))], [column_block, prob_block],
            [struct((length, width)), struct((heads, length, length))], [], 4 * dense, 30e6,
        )(me, qkv, qkv, qkv, segment_column, segment_row)

    mix0, prob0 = attend(qkv0)
    mix1, prob1 = attend(qkv1)

    blocks = [struct((count // 2, 3 * depth, width))] * 2
    local_step = pl.BlockSpec((1, half_rows, features), lambda i, me: (jnp.minimum(i, 1), 0, 0))
    result, residual_grad, mix_grad, feed_sums, fk0, fs0, fk1, fs1 = call(
        feed_kernel, (3,),
        [rows_spec] * 4 + [whole((length, width))] * 2 + [whole((length, 1)), vec_spec] + [ANY] * 4,
        [
            local_step, local_step,
            pl.BlockSpec((half_rows, features), lambda i, me: (jnp.minimum(i, 1) ^ (me[0] & 1), 0)),
            whole((8, features)),
        ] + [ANY] * 4,
        [struct((2, half_rows, features)), struct((2, half_rows, features), f32), struct((length, features)),
         struct((8, features), f32)] + blocks + blocks,
        [
            pltpu.VMEM((3, features, features), bf16),
            pltpu.VMEM((length, features), bf16),
            pltpu.VMEM((length, features), bf16),
            pltpu.VMEM((length, features), bf16),
            pltpu.VMEM((length, features), bf16),
            pltpu.VMEM((length, features), bf16),
            pltpu.VMEM((half_rows, features), f32),
            pltpu.VMEM((half_rows, features), f32),
            pltpu.VMEM((2, 3, features, width), bf16),
            pltpu.SemaphoreType.DMA(()),
            pltpu.SemaphoreType.DMA((2,)),
        ],
        9 * dense, 30e6,
    )(me, x_own, x_other, cot_own, cot_other, mix0, mix1, live, vec, fl0, fh0, fl1, fh1)
    feed_grads = [scatter_blocks(fk0, fs0, ORDERS[0]), scatter_blocks(fk1, fs1, ORDERS[1])]

    def attend_back(qkv, prob, mix, half):
        return call(
            lambda me_ref, *refs: attend_back_kernel(scale, *refs), (heads,),
            head_specs + [prob_block, column_block, pl.BlockSpec((length, head_size), lambda h, me: (0, h + half * heads))],
            pl.BlockSpec((3, length, head_size), lambda h, me: (0, 0, h)), struct((3, length, width)),
            [pltpu.VMEM((length, head_size), f32)] * 2, 8 * dense, 30e6,
        )(me, qkv, qkv, qkv, prob, mix, mix_grad)

    def project_back(grad, order):
        return call(
            functools.partial(project_back_kernel, order), (3,),
            [whole((length, features)), pl.BlockSpec((1, length, width), lambda i, me: (i, 0, 0))],
            [ANY, ANY, pl.BlockSpec((1, 8, width), lambda i, me: (i, 0, 0))], blocks + [struct((3, 8, width), f32)],
            [pltpu.VMEM((3, features, width), bf16), pltpu.SemaphoreType.DMA(())], 1.5 * dense, 8e6,
        )(me, normed_low, grad)

    qkv_grad0 = attend_back(qkv0, prob0, mix0, 0)
    ak0, as0, sums0 = project_back(qkv_grad0, ORDERS[0])
    qkv_grad1 = attend_back(qkv1, prob1, mix1, 1)
    ak1, as1, sums1 = project_back(qkv_grad1, ORDERS[1])
    attn_grads = [scatter_blocks(ak0, as0, ORDERS[0]), scatter_blocks(ak1, as1, ORDERS[1])]

    last_first = pl.BlockSpec((1, half_rows, features), lambda i, me: (1 - i, 0, 0))
    grad_rows = pl.BlockSpec((3, half_rows, width), lambda i, me: (0, 1 - (i ^ (me[0] & 1)), 0))
    latent_out, latent_other, last_sums = call(
        finish_kernel, (2,),
        [rows_spec] * 2 + [last_first, grad_rows, grad_rows, vec_spec] + [ANY] * 4,
        [pl.BlockSpec((1, half_rows, features), lambda i, me: (me[0] & 1, 0, 0)), rows_spec, whole((8, features))],
        [struct((2, half_rows, features), f32), struct((half_rows, features)), struct((8, features), f32)],
        [pltpu.VMEM((3, features, features), bf16), pltpu.SemaphoreType.DMA(())], 3 * dense, 20e6,
    )(me, x_own, x_other, residual_grad, qkv_grad0, qkv_grad1, vec, al0, ah0, al1, ah1)

    latent_back = shift(latent_other, 1, count).astype(f32)
    latent_grads = lax.dynamic_update_slice_in_dim(latent_out, latent_back[None], 1 - rank, 0)
    result_back = shift(result[1], 1, count)
    activations = lax.dynamic_update_slice_in_dim(
        jnp.broadcast_to(result[0][None], (2, half_rows, features)), result_back[None], 1 - rank, 0
    )

    qv_sums = jnp.concatenate([sums0[:, 0], sums1[:, 0]], axis=1)
    totals = jnp.concatenate(
        [last_sums[0:1], feed_sums[0:1], last_sums[1:2], feed_sums[1:2], qv_sums[0:1], qv_sums[2:3], feed_sums[2:5]], axis=0
    )
    by_owner = totals.reshape(vector_rows, count, depth)
    pieces = jnp.einsum("pa,kaj->pkj", choose, by_owner, precision=lax.Precision.HIGHEST)
    pieces = pieces.reshape(count, vector_rows * depth)
    vector_grads = scatter_blocks(pieces[: count // 2], pieces[count // 2 :], ORDERS[0])
    vector_grads = vector_grads.reshape(vector_rows, depth)

    attn_out = jnp.concatenate([g.reshape(3, depth, width) for g in attn_grads], axis=2)
    feed_out = jnp.concatenate([g.reshape(3, depth, width) for g in feed_grads], axis=2)
    return (
        activations[:, None],
        latent_grads[:, None],
        attn_out,
        feed_out[0],
        feed_out[1:],
        vector_grads[:2],
        vector_grads[2:],
    )


def layer_norm(vector, gain_row, offset):
    centre = vector - jnp.mean(vector, axis=-1, keepdims=True)
    spread = jnp.mean(centre * centre, axis=-1, keepdims=True)
    return centre * lax.rsqrt(spread + EPSILON) * gain_row + offset


def on_device(
    latents, segments, attention_weights, output_weight, hidden_weights, gains, biases, cotangent
):
    micro_count = latents.shape[0]
    row_count = latents.shape[2]
    features = latents.shape[3]
    head_size = features // HEADS
    score_scale = 1.0 / math.sqrt(head_size)
    own_rank = lax.axis_index("row")
    attn_total = jnp.zeros((3, features, features), jnp.float32)
    output_total = jnp.zeros((features, features), jnp.float32)
    hidden_total = jnp.zeros((2, features, features), jnp.float32)
    gain_total = jnp.zeros((2, features), jnp.float32)
    bias_total = jnp.zeros((7, features), jnp.float32)
    outputs = []
    input_grads = []
    for micro_index in range(micro_count):
        gathered = (
            lax.all_gather(attention_weights, ("seq", "row"), axis=1, tiled=True),
            lax.all_gather(output_weight, ("seq", "row"), axis=0, tiled=True),
            lax.all_gather(hidden_weights, ("seq", "row"), axis=1, tiled=True),
            lax.all_gather(gains, ("seq", "row"), axis=1, tiled=True),
            lax.all_gather(biases, ("seq", "row"), axis=1, tiled=True),
        )
        attention_full, output_full, hidden_full, gain_full, bias_full = gathered
        gain_values = gain_full.astype(jnp.float32)
        bias_values = bias_full.astype(jnp.float32)
        inputs = latents[micro_index, 0].astype(jnp.float32)
        segment_all = segments[micro_index, 0]
        segment_own = lax.dynamic_slice_in_dim(segment_all, own_rank * row_count, row_count)
        normed_one, norm_one_pull = jax.vjp(layer_norm, inputs, gain_values[0], bias_values[0])
        normed_low = normed_one.astype(jnp.bfloat16)
        projected = jnp.einsum(
            "rd,cde->cre", normed_low, attention_full, preferred_element_type=jnp.float32
        )
        queries = (projected[0] + bias_values[2]).astype(jnp.bfloat16)
        own_keys = projected[1].astype(jnp.bfloat16)
        own_values = (projected[2] + bias_values[3]).astype(jnp.bfloat16)
        all_keys, all_values = (
            lax.all_gather(own_keys, "row", axis=0, tiled=True),
            lax.all_gather(own_values, "row", axis=0, tiled=True),
        )
        length = all_keys.shape[0]
        query_heads = queries.reshape(row_count, HEADS, head_size)
        key_heads = all_keys.reshape(length, HEADS, head_size)
        value_heads = all_values.reshape(length, HEADS, head_size)
        same_set = (segment_own[:, None] == segment_all[None, :])[None]
        raw_scores = (
            jnp.einsum("qhd,khd->hqk", query_heads, key_heads, preferred_element_type=jnp.float32)
            * score_scale
        )
        scores = jnp.where(same_set, raw_scores, -1e30)
        row_max = jnp.max(scores, axis=-1, keepdims=True)
        log_total = row_max + jnp.log(jnp.sum(jnp.exp(scores - row_max), axis=-1, keepdims=True))
        weights_low = jnp.exp(scores - log_total).astype(jnp.bfloat16)
        mixture = jnp.einsum(
            "hqk,khd->qhd", weights_low, value_heads, preferred_element_type=jnp.float32
        )
        mixture = mixture.reshape(row_count, features).astype(jnp.bfloat16)
        attended = (
            jnp.dot(mixture, output_full, preferred_element_type=jnp.float32) + bias_values[4]
        )
        residual_one = inputs + attended
        normed_two, norm_two_pull = jax.vjp(
            layer_norm, residual_one, gain_values[1], bias_values[1]
        )
        hidden_low = normed_two.astype(jnp.bfloat16)
        hidden_pre = (
            jnp.dot(hidden_low, hidden_full[0], preferred_element_type=jnp.float32) + bias_values[5]
        )
        activated, gelu_pull = jax.vjp(jax.nn.gelu, hidden_pre)
        active_low = activated.astype(jnp.bfloat16)
        result = residual_one + (
            jnp.dot(active_low, hidden_full[1], preferred_element_type=jnp.float32) + bias_values[6]
        )
        outputs.append(result.astype(jnp.bfloat16))
        live_rows = (segment_own >= 0).astype(jnp.bfloat16)[:, None]
        out_grad = cotangent[micro_index, 0] * live_rows
        out_grad_wide = out_grad.astype(jnp.float32)
        active_grad = jnp.dot(out_grad, hidden_full[1].T, preferred_element_type=jnp.float32)
        pre_grad = gelu_pull(active_grad)[0].astype(jnp.bfloat16)
        normed_two_grad = jnp.dot(pre_grad, hidden_full[0].T, preferred_element_type=jnp.float32)
        residual_part, gain_two, offset_two = norm_two_pull(normed_two_grad)
        residual_grad = out_grad_wide + residual_part
        residual_low = residual_grad.astype(jnp.bfloat16)
        mixture_grad = jnp.dot(residual_low, output_full.T, preferred_element_type=jnp.float32)
        mixture_grad = mixture_grad.astype(jnp.bfloat16).reshape(row_count, HEADS, head_size)
        raw_again = (
            jnp.einsum("qhd,khd->hqk", query_heads, key_heads, preferred_element_type=jnp.float32)
            * score_scale
        )
        weights_wide = jnp.exp(jnp.where(same_set, raw_again, -1e30) - log_total)
        weight_grads = jnp.einsum(
            "qhd,khd->hqk", mixture_grad, value_heads, preferred_element_type=jnp.float32
        )
        centred = jnp.sum(weights_wide * weight_grads, axis=-1, keepdims=True)
        score_grads = (weights_wide * (weight_grads - centred)).astype(jnp.bfloat16)
        query_grad = (
            jnp.einsum("hqk,khd->qhd", score_grads, key_heads, preferred_element_type=jnp.float32)
            * score_scale
        )
        query_grad = query_grad.astype(jnp.bfloat16).reshape(row_count, features)
        weights_again = weights_wide.astype(jnp.bfloat16)
        key_part = (
            jnp.einsum("hqk,qhd->khd", score_grads, query_heads, preferred_element_type=jnp.float32)
            * score_scale
        )
        value_part = jnp.einsum(
            "hqk,qhd->khd", weights_again, mixture_grad, preferred_element_type=jnp.float32
        )
        key_grad, value_grad = (
            lax.psum_scatter(
                key_part.reshape(length, features).astype(jnp.bfloat16),
                "row",
                scatter_dimension=0,
                tiled=True,
            ).astype(jnp.float32),
            lax.psum_scatter(
                value_part.reshape(length, features).astype(jnp.bfloat16),
                "row",
                scatter_dimension=0,
                tiled=True,
            ).astype(jnp.float32),
        )
        key_low = key_grad.astype(jnp.bfloat16)
        value_low = value_grad.astype(jnp.bfloat16)
        projection_grads = jnp.stack([query_grad, key_low, value_low])
        attn_total = attn_total + jnp.einsum(
            "rd,cre->cde", normed_low, projection_grads, preferred_element_type=jnp.float32
        )
        output_total = output_total + jnp.dot(
            mixture.T, residual_low, preferred_element_type=jnp.float32
        )
        hidden_total = hidden_total + jnp.stack(
            [
                jnp.dot(hidden_low.T, pre_grad, preferred_element_type=jnp.float32),
                jnp.dot(active_low.T, out_grad, preferred_element_type=jnp.float32),
            ]
        )
        normed_one_grad = jnp.einsum(
            "cre,cde->rd", projection_grads, attention_full, preferred_element_type=jnp.float32
        )
        input_part, gain_one, offset_one = norm_one_pull(normed_one_grad)
        input_grads.append(residual_grad + input_part)
        gain_total = gain_total + jnp.stack([gain_one, gain_two])
        bias_total = bias_total + jnp.stack(
            [
                offset_one,
                offset_two,
                jnp.sum(query_grad.astype(jnp.float32), axis=0),
                jnp.sum(value_low.astype(jnp.float32), axis=0),
                jnp.sum(residual_low.astype(jnp.float32), axis=0),
                jnp.sum(pre_grad.astype(jnp.float32), axis=0),
                jnp.sum(out_grad_wide, axis=0),
            ]
        )
    attn_grads, output_grads, hidden_grads, gain_grads, bias_grads = (
        lax.psum_scatter(attn_total, ("seq", "row"), scatter_dimension=1, tiled=True),
        lax.psum_scatter(output_total, ("seq", "row"), scatter_dimension=0, tiled=True),
        lax.psum_scatter(hidden_total, ("seq", "row"), scatter_dimension=1, tiled=True),
        lax.psum_scatter(gain_total, ("seq", "row"), scatter_dimension=1, tiled=True),
        lax.psum_scatter(bias_total, ("seq", "row"), scatter_dimension=1, tiled=True),
    )
    return (
        jnp.stack(outputs)[:, None],
        jnp.stack(input_grads)[:, None],
        attn_grads,
        output_grads,
        hidden_grads,
        gain_grads,
        bias_grads,
    )


def solution(mesh):
    def on_mesh(latents, *rest):
        shares_pair = mesh.shape["row"] == latents.shape[0] == 2
        fits = mesh.size == 1 << len(ORDERS[0]) and latents.shape[1] == mesh.shape["seq"]
        return shard_over(whole_sequence if shares_pair and fits else on_device)(latents, *rest)

    def shard_over(function):
        return jax.shard_map(
            function,
            mesh=mesh,
            in_specs=(
                P(None, "seq", "row", None),
                P(None, "seq", None),
                P(None, ("seq", "row"), None),
                P(("seq", "row"), None),
                P(None, ("seq", "row"), None),
                P(None, ("seq", "row")),
                P(None, ("seq", "row")),
                P(None, "seq", "row", None),
            ),
            out_specs=(
                P(None, "seq", "row", None),
                P(None, "seq", "row", None),
                P(None, ("seq", "row"), None),
                P(("seq", "row"), None),
                P(None, ("seq", "row"), None),
                P(None, ("seq", "row")),
                P(None, ("seq", "row")),
            ),
            check_vma=False,
        )

    return on_mesh
```

```python
import functools
import math

import jax
import jax.numpy as jnp
from jax import lax
from jax.experimental import pallas as pl
from jax.experimental.pallas import tpu as pltpu
from jax.sharding import PartitionSpec as P

HEADS = 8
EPSILON = 1e-05
AXES = ("seq", "row")
VMEM_LIMIT = 60 << 20
NN = (((1,), (0,)), ((), ()))
NT = (((1,), (1,)), ((), ()))
TN = (((0,), (0,)), ((), ()))
ORDERS = ((16, 1, 8, 4, 2), (16, 1, 4, 8, 2))


def offset_of(order, position):
    offset = 0
    for bit, mask in enumerate(order):
        if position >> bit & 1:
            offset ^= mask
    return offset


def dot(left, right, dims=NN):
    return lax.dot_general(left, right, dims, preferred_element_type=jnp.float32)


def shift(array, mask, count):
    return lax.ppermute(array, AXES, [(i, i ^ mask) for i in range(count)])


def place_weights(me, order, sources, weight_ref, column, sem):
    depth = weight_ref.shape[1] >> len(order)
    width = sources[0].shape[-1]
    held = sources[0].shape[0]
    for position in range(len(sources) * held):
        owner = me ^ offset_of(order, position)
        rows = pl.ds(pl.multiple_of(owner * depth, depth), depth)
        for matrix in range(3):
            pltpu.make_async_copy(
                sources[position // held].at[position % held, pl.ds(matrix * depth, depth), :],
                weight_ref.at[matrix, rows, pl.ds(column, width)],
                sem,
            ).start()


def collect_grads(me, order, stage_ref, keep_ref, send_ref, sem):
    half = 1 << len(order) - 1
    depth = stage_ref.shape[1] >> len(order)
    for position in reversed(range(2 * half)):
        target = keep_ref if position < half else send_ref
        owner = me ^ offset_of(order, position)
        rows = pl.ds(pl.multiple_of(owner * depth, depth), depth)
        for matrix in range(3):
            place = (position % half * 3 + matrix) * depth
            pltpu.make_async_copy(stage_ref.at[matrix, rows, :], target.at[pl.ds(place, depth), :], sem).start()


def normalize(rows):
    mean = jnp.mean(rows, axis=-1, keepdims=True)
    centre = rows - mean
    spread = jnp.mean(centre * centre, axis=-1, keepdims=True)
    scale = lax.rsqrt(spread + EPSILON)
    return centre * scale, scale


def column_sum(rows):
    return jnp.sum(rows.astype(jnp.float32), axis=0, keepdims=True)


def project_first_kernel(me_ref, own_ref, other_ref, vec_ref, *refs):
    *sources, normed_ref, qkv_ref, w_ref, sem = refs
    step = pl.program_id(0)
    width = qkv_ref.shape[-1]

    @pl.when(step == 0)
    def _():
        place_weights(me_ref[0], ORDERS[0], sources, w_ref, 0, sem)

    rows = jnp.where(step == 0, own_ref[0], other_ref[...]).astype(jnp.float32)
    normed, _ = normalize(rows)
    normed_ref[...] = (normed * vec_ref[0:1] + vec_ref[2:3]).astype(jnp.bfloat16)

    @pl.when(step == 0)
    def _():
        pltpu.make_async_copy(w_ref, w_ref, sem).wait()

    for matrix, bias in ((0, 4), (1, None), (2, 5)):
        out = dot(normed_ref[...], w_ref[matrix])
        if bias is not None:
            out = out + vec_ref[bias : bias + 1, 0:width]
        qkv_ref[matrix] = out.astype(jnp.bfloat16)


def project_next_kernel(me_ref, normed_ref, vec_ref, *refs):
    *sources, qkv_ref, w_ref, sem = refs
    step = pl.program_id(0)
    width = qkv_ref.shape[-1]

    @pl.when(step == 0)
    def _():
        place_weights(me_ref[0], ORDERS[1], sources, w_ref, 0, sem)
        pltpu.make_async_copy(w_ref, w_ref, sem).wait()

    for matrix, bias in ((0, 4), (1, None), (2, 5)):
        out = dot(normed_ref[...], w_ref[matrix])
        if bias is not None:
            out = out + vec_ref[bias : bias + 1, width : 2 * width]
        qkv_ref[matrix] = out.astype(jnp.bfloat16)


def key_ranges(length):
    quarter = length // 4
    return ((0, 2 * quarter), (0, length), (quarter, length), (quarter, length))


def attend_kernel(scale, q_ref, k_ref, v_ref, column_ref, row_ref, mix_ref, prob_ref):
    length = q_ref.shape[1]
    quarter = length // 4
    for index, (first, last) in enumerate(key_ranges(length)):
        rows = slice(index * quarter, (index + 1) * quarter)
        scores = dot(q_ref[0, rows, :], k_ref[0, first:last, :], NT)
        same = column_ref[rows, :] == row_ref[0, :, first:last]
        scores = jnp.where(same, scores, -1e30)
        top = jnp.max(scores, axis=-1, keepdims=True)
        expo = jnp.exp((scores - top) * scale)
        total = jnp.sum(expo, axis=-1, keepdims=True)
        low = (expo * (1.0 / total)).astype(jnp.bfloat16)
        prob_ref[0, rows, first:last] = low
        mix_ref[rows, :] = dot(low, v_ref[0, first:last, :]).astype(jnp.bfloat16)


def attend_back_kernel(scale, q_ref, k_ref, v_ref, prob_ref, mix_ref, mixg_ref, out_ref, key_acc, value_acc):
    length = q_ref.shape[1]
    quarter = length // 4
    key_acc[...] = jnp.zeros_like(key_acc)
    value_acc[...] = jnp.zeros_like(value_acc)
    for index, (first, last) in enumerate(key_ranges(length)):
        rows = slice(index * quarter, (index + 1) * quarter)
        mix_grad = mixg_ref[rows, :]
        centred = jnp.sum(
            mix_grad.astype(jnp.float32) * mix_ref[rows, :].astype(jnp.float32), axis=-1, keepdims=True
        )
        grads = dot(mix_grad, v_ref[0, first:last, :], NT)
        low = prob_ref[0, rows, first:last]
        score_grads = (low.astype(jnp.float32) * (grads - centred)).astype(jnp.bfloat16)
        out_ref[0, rows, :] = (dot(score_grads, k_ref[0, first:last, :]) * scale).astype(jnp.bfloat16)
        key_acc[first:last, :] += dot(score_grads, q_ref[0, rows, :], TN)
        value_acc[first:last, :] += dot(low, mix_grad, TN)
    out_ref[1] = (key_acc[...] * scale).astype(jnp.bfloat16)
    out_ref[2] = value_acc[...].astype(jnp.bfloat16)


def project_back_kernel(half, order, me_ref, normed_ref, grad_ref, *refs):
    sources = refs[:4]
    keep_ref, send_ref, sum_ref, total_ref, stage_ref, w_ref, acc_ref, w_sem, g_sem = refs[4:]
    step = pl.program_id(0)
    lanes = acc_ref.shape[1]

    @pl.when(step == 0)
    def _():
        place_weights(me_ref[0], ORDERS[half], sources, w_ref, 0, w_sem)
        acc_ref[...] = jnp.zeros_like(acc_ref)
        total_ref[...] = jnp.zeros_like(total_ref)

    grads = dot(normed_ref[...], grad_ref[0], TN)
    stage_ref[step] = grads.astype(jnp.bfloat16)

    @pl.when(step == 0)
    def _():
        pltpu.make_async_copy(w_ref, w_ref, w_sem).wait()

    part = acc_ref[...]
    for first in range(0, grads.shape[1], lanes):
        columns = slice(first, first + lanes)
        part = part + grads[:, columns] * w_ref[step, :, columns].astype(jnp.float32)
    acc_ref[...] = part
    column = column_sum(grad_ref[0])
    sum_ref[0] = jnp.broadcast_to(column, sum_ref.shape[1:])
    first, second = halves_of(column)
    rows = lax.broadcasted_iota(jnp.int32, (16, column.shape[1]), 0)
    rows = jnp.where(rows == 0, first, jnp.where(rows == 1, second, 0.0)).astype(jnp.bfloat16)
    total = dot(rows, w_ref[step], NT)
    total_ref[1:2] += total[0:1] + total[1:2]

    @pl.when(step == 2)
    def _():
        collect_grads(me_ref[0], order, stage_ref, keep_ref, send_ref, g_sem)
        first, second = halves_of(acc_ref[...])
        ones = jnp.ones((16, lanes), jnp.bfloat16)
        total = dot(ones, first.astype(jnp.bfloat16), NT) + dot(ones, second.astype(jnp.bfloat16), NT)
        total_ref[0:1] = total[0:1]
        pltpu.make_async_copy(stage_ref, stage_ref, g_sem).wait()


def halves_of(value):
    first = value.astype(jnp.bfloat16).astype(jnp.float32)
    return first, value - first


def feed_kernel(
    me_ref, x_own_ref, x_other_ref, cot_own_ref, cot_other_ref, mix0_ref, mix1_ref, column_ref, vec_ref, *refs
):
    sources = refs[:8]
    result_ref, result_other_ref, resg_ref, mixg_ref, sum_ref, keep_ref, send_ref, *refs = refs[8:]
    w_ref, hid_ref, act_ref, og_ref, pre_ref, res_ref, resid, slope, stage_ref, w_sem, g_sem = refs
    step = pl.program_id(0)
    me = me_ref[0]
    half_rows, features = x_other_ref.shape
    width = features // 2

    @pl.when(step == 0)
    def _():
        for half in range(2):
            place_weights(me, ORDERS[half], sources[4 * half : 4 * half + 4], w_ref, half * width, w_sem)
        sum_ref[...] = jnp.zeros_like(sum_ref)
        pltpu.make_async_copy(w_ref, w_ref, w_sem).wait()

    @pl.when(step < 2)
    def _():
        place = pl.multiple_of((step ^ (me & 1)) * half_rows, half_rows)
        rows = pl.ds(place, half_rows)
        inputs = jnp.where(step == 0, x_own_ref[0], x_other_ref[...]).astype(jnp.float32)
        attended = dot(mix0_ref[rows, :], w_ref[0, 0:width, :]) + dot(mix1_ref[rows, :], w_ref[0, width:, :])
        resid[...] = inputs + attended + vec_ref[6:7]
        normed, inverse = normalize(resid[...])
        hid_ref[rows, :] = (normed * vec_ref[1:2] + vec_ref[3:4]).astype(jnp.bfloat16)
        pre = dot(hid_ref[rows, :], w_ref[1]) + vec_ref[7:8]
        square = pre * pre
        tanh = jnp.tanh(0.7978845608 * pre * (1.0 + 0.044715 * square))
        act_ref[rows, :] = (0.5 * pre * (1.0 + tanh)).astype(jnp.bfloat16)
        slope[...] = 0.5 * (1.0 + tanh) + (0.5 * 0.7978845608) * pre * (1.0 - tanh * tanh) * (
            1.0 + (3 * 0.044715) * square
        )
        result = resid[...] + dot(act_ref[rows, :], w_ref[2]) + vec_ref[8:9]
        result = result.astype(jnp.bfloat16)

        @pl.when(step == 0)
        def _():
            result_ref[0] = result

        @pl.when(step == 1)
        def _():
            result_other_ref[...] = result

        live = (column_ref[rows, :] >= 0).astype(jnp.float32)
        cot = jnp.where(step == 0, cot_own_ref[0], cot_other_ref[...]).astype(jnp.float32)
        og_ref[rows, :] = (cot * live).astype(jnp.bfloat16)
        pre_grad = dot(og_ref[rows, :], w_ref[2], NT) * slope[...]
        pre_ref[rows, :] = pre_grad.astype(jnp.bfloat16)
        normed_grad = dot(pre_ref[rows, :], w_ref[1], NT)
        normed, inverse = normalize(resid[...])
        sum_ref[0:1] += column_sum(normed_grad * normed)
        sum_ref[1:2] += column_sum(normed_grad)
        scaled = normed_grad * vec_ref[1:2]
        resg = og_ref[rows, :].astype(jnp.float32) + inverse * (
            scaled
            - jnp.mean(scaled, axis=-1, keepdims=True)
            - normed * jnp.mean(scaled * normed, axis=-1, keepdims=True)
        )
        resg_ref[0] = resg
        res_ref[rows, :] = resg.astype(jnp.bfloat16)
        mixg_ref[...] = dot(res_ref[rows, :], w_ref[0], NT).astype(jnp.bfloat16)
        sum_ref[2:3] += column_sum(res_ref[rows, :])
        sum_ref[3:4] += column_sum(pre_ref[rows, :])
        sum_ref[4:5] += column_sum(og_ref[rows, :])

    @pl.when(step == 2)
    def _():
        for half in range(2):
            columns = slice(half * width, (half + 1) * width)
            for part in range(2):
                mix_ref = (mix0_ref, mix1_ref)[part]
                out_rows = slice(part * width, (part + 1) * width)
                stage_ref[half, 0, out_rows, :] = dot(mix_ref[...], res_ref[:, columns], TN).astype(jnp.bfloat16)
            stage_ref[half, 1] = dot(hid_ref[...], pre_ref[:, columns], TN).astype(jnp.bfloat16)
            stage_ref[half, 2] = dot(act_ref[...], og_ref[:, columns], TN).astype(jnp.bfloat16)
            wide = pl.ds(half * keep_ref.shape[0] // 2, keep_ref.shape[0] // 2)
            collect_grads(
                me, ORDERS[half], stage_ref.at[half], keep_ref.at[wide], send_ref.at[wide], g_sem.at[half]
            )
        for half in range(2):
            pltpu.make_async_copy(stage_ref.at[half], stage_ref.at[half], g_sem.at[half]).wait()


def finish_kernel(me_ref, x_own_ref, x_other_ref, resg_ref, grad0_ref, grad1_ref, vec_ref, *refs):
    sources = refs[:8]
    out_ref, other_ref, w_ref, sem = refs[8:]
    step = pl.program_id(0)
    me = me_ref[0]
    width = grad0_ref.shape[-1]

    @pl.when(step == 0)
    def _():
        for half in range(2):
            place_weights(me, ORDERS[half], sources[4 * half : 4 * half + 4], w_ref, half * width, sem)
        pltpu.make_async_copy(w_ref, w_ref, sem).wait()

    normed_grad = None
    for matrix in range(3):
        for part, grad_ref in enumerate((grad0_ref, grad1_ref)):
            term = dot(grad_ref[matrix], w_ref[matrix, :, part * width : (part + 1) * width], NT)
            normed_grad = term if normed_grad is None else normed_grad + term
    rows = jnp.where(step == 1, x_own_ref[0], x_other_ref[...]).astype(jnp.float32)
    normed, inverse = normalize(rows)
    scaled = normed_grad * vec_ref[0:1]
    total = resg_ref[0] + inverse * (
        scaled
        - jnp.mean(scaled, axis=-1, keepdims=True)
        - normed * jnp.mean(scaled * normed, axis=-1, keepdims=True)
    )

    @pl.when(step == 0)
    def _():
        other_ref[...] = total.astype(jnp.bfloat16)

    @pl.when(step == 1)
    def _():
        out_ref[0] = total


def pack_first_kernel(me_ref, attention_ref, gain_ref, bias_ref, out_ref):
    matrices, depth, features = attention_ref.shape
    width = features // 2
    out_ref[...] = jnp.zeros_like(out_ref)
    for half in range(2):
        for matrix in range(matrices):
            block = attention_ref[matrix, :, half * width : (half + 1) * width]
            out_ref[0, half, matrix * depth : (matrix + 1) * depth, :] = block
    base = matrices * depth
    gains = gain_ref.shape[0]
    out_ref[0, 0, base : base + gains, 0:depth] = gain_ref[...]
    out_ref[0, 0, base + gains : base + gains + bias_ref.shape[0], 0:depth] = bias_ref[...]


def pack_next_kernel(me_ref, output_ref, hidden_ref, out_ref):
    depth, features = output_ref.shape
    width = features // 2
    for half in range(2):
        columns = slice(half * width, (half + 1) * width)
        out_ref[0, half, 0:depth, :] = output_ref[:, columns]
        out_ref[0, half, depth : 2 * depth, :] = hidden_ref[0, :, columns]
        out_ref[0, half, 2 * depth : 3 * depth, :] = hidden_ref[1, :, columns]


def join_kernel(moves, me_ref, *refs):
    for source, source_index, target, target_index in moves:
        refs[target][target_index] = refs[source][source_index]


def select_kernel(me_ref, rows_ref, out_ref):
    out_ref[...] = rows_ref[0]


def total_of(refs, width):
    total = None
    for ref in refs:
        term = ref[...].astype(jnp.float32).reshape(-1, width)
        total = term if total is None else total + term
    return total


def combine_kernel(sums, me_ref, *refs):
    for first, last, output, row in sums:
        out_ref = refs[output]
        total = total_of(refs[first:last], out_ref.shape[-1])
        out_ref[row : row + total.shape[0], :] = total.astype(out_ref.dtype)


def final_kernel(inputs, me_ref, *refs):
    outs = refs[2 * inputs :]
    depth, features = outs[0].shape[1:]
    width = features // 2
    for half in range(2):
        total = total_of(refs[half * inputs : (half + 1) * inputs], width)
        row = 0
        for out_ref in outs:
            matrices = out_ref.shape[0]
            piece = total[row : row + matrices * depth].reshape(matrices, depth, width)
            out_ref[:, :, half * width : (half + 1) * width] = piece
            row += matrices * depth


def final_vector_kernel(inputs, vectors, me_ref, *refs):
    blocks, terms = refs[: 2 * inputs], refs[2 * inputs : 2 * inputs + vectors]
    out_ref, vector_ref = refs[2 * inputs + vectors :]
    final_kernel(inputs, me_ref, *blocks, out_ref)
    vector_kernel(me_ref, *terms, vector_ref)


def vector_kernel(me_ref, *refs):
    *terms, out_ref = refs
    rows, depth = out_ref.shape
    width = terms[0].shape[-1]
    total = total_of(terms, width)
    lane = lax.broadcasted_iota(jnp.int32, (width, depth), 0)
    column = lax.broadcasted_iota(jnp.int32, (width, depth), 1)
    place = me_ref[0] * depth
    picked = None
    for half in range(2):
        choose = (lane + half * width == column + place).astype(jnp.float32)
        part = lax.dot_general(
            total[half * rows : (half + 1) * rows], choose, NN, precision=lax.Precision.HIGHEST,
            preferred_element_type=jnp.float32,
        )
        picked = part if picked is None else picked + part
    out_ref[...] = picked


def vector_pack_kernel(me_ref, feed_ref, vec_ref, s0_ref, s1_ref, t0_ref, t1_ref, out_ref, row_ref):
    width = out_ref.shape[-1]
    row_ref[...] = jnp.zeros_like(row_ref)
    offset = t0_ref[1:2] + t1_ref[1:2]
    row_ref[0:1] = (t0_ref[0:1] + t1_ref[0:1] - vec_ref[2:3] * offset) / vec_ref[0:1]
    row_ref[1:2] = feed_ref[0:1]
    row_ref[2:3] = offset
    row_ref[3:4] = feed_ref[1:2]
    for half, sums in enumerate((s0_ref, s1_ref)):
        row_ref[4:5, half * width : (half + 1) * width] = sums[0, 0:1]
        row_ref[5:6, half * width : (half + 1) * width] = sums[2, 0:1]
    row_ref[6:9] = feed_ref[2:5]
    for half in range(2):
        out_ref[half * 16 : (half + 1) * 16, :] = row_ref[:, half * width : (half + 1) * width].astype(jnp.bfloat16)


ANY = pl.BlockSpec(memory_space=pl.ANY)
VMEM = pl.BlockSpec(memory_space=pltpu.VMEM)
SMALL_LIMIT = 24 << 20


def call(kernel, me, grid, operands, out_specs, out_shape, scratch=(), flops=1e6, moved=1e6, after=(), limit=VMEM_LIMIT):
    taken = len(operands) + 1
    after = list(after)

    def body(*refs):
        kernel(*refs[:taken], *refs[taken + len(after) :])

    return pl.pallas_call(
        body,
        grid_spec=pltpu.PrefetchScalarGridSpec(
            num_scalar_prefetch=1,
            grid=grid,
            in_specs=[spec for _, spec in operands] + [ANY] * len(after),
            out_specs=out_specs,
            scratch_shapes=list(scratch),
        ),
        out_shape=out_shape,
        compiler_params=pltpu.CompilerParams(
            dimension_semantics=("arbitrary",) * len(grid), vmem_limit_bytes=limit
        ),
        cost_estimate=pl.CostEstimate(flops=int(flops), bytes_accessed=int(moved), transcendentals=0),
    )(me, *[array for array, _ in operands], *after)


def struct(shape, dtype=jnp.bfloat16):
    return jax.ShapeDtypeStruct(shape, dtype)


def whole(shape):
    return pl.BlockSpec(shape, lambda *_: (0,) * len(shape))


def join(me, arrays, moves, shapes, after=(), local=True):
    moves = [(i, source, len(arrays) + o, target) for i, source, o, target in moves]
    place = (lambda shape: VMEM) if local else whole
    return call(
        functools.partial(join_kernel, moves), me, (1,), [(a, place(a.shape)) for a in arrays],
        [place(s) for s in shapes], [struct(s) for s in shapes], after=after, limit=SMALL_LIMIT,
    )


def part(array, start, size, tall):
    return array, pl.BlockSpec((size * tall, array.shape[-1]), lambda i, me: (start // size, 0))


def combine(me, outputs, after=()):
    operands, sums, shapes = [], [], []
    count = sum(len(terms) for group in outputs for terms in group)
    for number, group in enumerate(outputs):
        row = 0
        for terms in group:
            first = len(operands)
            operands.extend(terms)
            sums.append((first, len(operands), count + number, row))
            row += terms[0][1].block_shape[0]
        shapes.append((row, group[0][0][0].shape[-1]))
    return call(
        functools.partial(combine_kernel, sums), me, (1,), operands, [whole(s) for s in shapes],
        [struct(s) for s in shapes], after=after, limit=SMALL_LIMIT,
    )


def final(me, halves, depth, features, counts, vectors=()):
    shapes = [(matrices, depth, features) for matrices in counts]
    kernel = functools.partial(final_kernel, len(halves[0]))
    if vectors:
        kernel = functools.partial(final_vector_kernel, len(halves[0]), len(vectors))
        shapes.append((vectors[0][1].block_shape[0] // 2, depth))
    return call(
        kernel, me, (1,), halves[0] + halves[1] + list(vectors), [whole(s) for s in shapes],
        [struct(s, jnp.float32) for s in shapes], limit=SMALL_LIMIT,
    )


def whole_sequence(
    latents, segments, attention_weights, output_weight, hidden_weights, gains, biases, cotangent
):
    half_rows, features = latents.shape[2:]
    length = 2 * half_rows
    head_size = features // HEADS
    scale = 1.0 / math.sqrt(head_size)
    width = features // 2
    count = 1 << len(ORDERS[0])
    depth = features // count
    rank = lax.axis_index("row")
    device = (lax.axis_index("seq") * 2 + rank).astype(jnp.int32)
    me = device.reshape(1)
    bf16, f32 = jnp.bfloat16, jnp.float32
    dense = 2.0 * length * features * features
    tall = 3 * depth
    vector_rows = gains.shape[0] + biases.shape[0]
    padded = tall + 16

    def move(array, mask):
        return shift(array, mask, count)

    def double(held, got, after=()):
        return join(me, [held, got], [(0, 0, 0, 0), (1, 0, 0, 1)], [(2,) + held.shape[1:]], after)[0]

    def split(held, got, rows, after=(), local=True):
        moves, shapes = [], []
        for half in range(2):
            for source in range(2):
                for block in range(2):
                    moves.append((source, (block, half, slice(0, rows[half])), half, 2 * source + block))
            shapes.append((4, rows[half], width))
        return join(me, [held, got], moves, shapes, after, local)

    def append(held, got, after=(), local=True):
        moves, shapes = [], []
        for half in range(2):
            for source in range(2):
                moves.append((2 * half + source, slice(None), half, slice(4 * source, 4 * source + 4)))
            shapes.append((8,) + held[half].shape[1:])
        return join(me, [held[0], got[0], held[1], got[1]], moves, shapes, after, local)

    z_far, y, z_near, x, core = 16, 1, 8, 4, 2
    pack = lambda kernel, arrays, rows, after: call(
        kernel, me, (1,), [(a, whole(a.shape)) for a in arrays], VMEM,
        struct((1, 2, rows, width)), after=after, limit=SMALL_LIMIT,
    )
    latents_flat = latents[:, 0]
    cotangent_flat = cotangent[:, 0]

    def select(array, after):
        block = (half_rows // 2, features)
        return call(
            select_kernel, me, (2,),
            [(array, pl.BlockSpec((1,) + block, lambda i, me: (1 - (me[0] & 1), i, 0)))],
            pl.BlockSpec(block, lambda i, me: (i, 0)), struct(array.shape[1:]), after=after, limit=SMALL_LIMIT,
        )

    a1 = pack(pack_first_kernel, [attention_weights, gains, biases], padded, [])
    x_send = select(latents_flat, [a1])
    a2 = double(a1, move(a1, z_far), [x_send])
    f1 = pack(pack_next_kernel, [output_weight, hidden_weights], tall, [a2])
    a4 = split(a2, move(a2, y), (padded, tall), [f1])
    x_other = move(x_send, y)
    cot_send = select(cotangent_flat, a4)
    f2 = double(f1, move(f1, z_far), a4)
    a8 = append(a4, (move(a4[0], z_near), move(a4[1], x)), [f2, cot_send])
    a_core = [move(a, core) for a in a8]
    f4 = split(f2, move(f2, y), (tall, tall), [*a8, x_other], local=False)
    a_far = (move(a8[0], x), move(a8[1], z_near))
    a_far_core = [move(a, core) for a in a_far]
    attn_sources = [[a8[h], a_far[h], a_core[h], a_far_core[h]] for h in range(2)]

    offsets = jnp.array([offset_of(ORDERS[0], p) for p in range(count)], jnp.int32)
    owners = jnp.bitwise_xor(device, offsets)
    choose = (owners[:, None] == jnp.arange(count, dtype=jnp.int32)[None, :]).astype(f32)
    pieces = jnp.concatenate([a[:, tall : tall + vector_rows, :depth] for a in attn_sources[0]], axis=0).astype(f32)
    vec = jnp.einsum("pa,pkj->kaj", choose, pieces, precision=lax.Precision.HIGHEST)
    vec = vec.reshape(vector_rows, features)

    segment_row = segments
    segment_column = lax.dynamic_index_in_dim(segments[:, 0], rank, 0, keepdims=False)[:, None]

    own = pl.BlockSpec((1, half_rows, features), lambda i, me: (me[0] & 1, 0, 0))
    local = pl.BlockSpec((half_rows, features), lambda i, me: (i ^ (me[0] & 1), 0))
    local3 = pl.BlockSpec((3, half_rows, width), lambda i, me: (0, i ^ (me[0] & 1), 0))
    rows_spec = whole((half_rows, features))
    vec_op = (vec, whole((vector_rows, features)))
    w_half = [pltpu.VMEM((3, features, width), bf16), pltpu.SemaphoreType.DMA(())]

    normed_low, qkv0 = call(
        project_first_kernel, me, (2,),
        [(latents_flat, own), (x_other, rows_spec), vec_op] + [(a, ANY) for a in attn_sources[0]], [local, local3],
        [struct((length, features)), struct((3, length, width))], w_half, 1.5 * dense, 16e6, f4,
    )
    cot_other = move(cot_send, y)
    f8 = append(f4, (move(f4[0], z_near), move(f4[1], x)), [normed_low], local=False)
    f_core = [move(a, core) for a in f8]
    f_far = (move(f8[0], x), move(f8[1], z_near))
    qkv1 = call(
        project_next_kernel, me, (2,),
        [(normed_low, pl.BlockSpec((half_rows, features), lambda i, me: (i, 0))), vec_op]
        + [(a, ANY) for a in attn_sources[1]],
        pl.BlockSpec((3, half_rows, width), lambda i, me: (0, i, 0)), struct((3, length, width)), w_half,
        1.5 * dense, 8e6, f8,
    )

    heads = width // head_size
    head_specs = [
        pl.BlockSpec((1, length, head_size), functools.partial(lambda c, h, me: (c, 0, h), c)) for c in range(3)
    ]
    column_block = pl.BlockSpec((length, head_size), lambda h, me: (0, h))
    prob_block = pl.BlockSpec((1, length, length), lambda h, me: (h, 0, 0))
    segment_spec = pl.BlockSpec((1, 1, length), lambda h, me: (me[0] & 1, 0, 0))

    def attend(qkv, after):
        return call(
            lambda me_ref, *refs: attend_kernel(scale, *refs), me, (heads,),
            [(qkv, s) for s in head_specs] + [(segment_column, whole((length, 1))), (segment_row, segment_spec)],
            [column_block, prob_block], [struct((length, width)), struct((heads, length, length))], [],
            4 * dense, 30e6, after,
        )

    mix0, prob0 = attend(qkv0, [qkv1])
    f_far_core = [move(a, core) for a in f_far]
    feed_sources = [[f8[h], f_far[h], f_core[h], f_far_core[h]] for h in range(2)]
    mix1, prob1 = attend(qkv1, [mix0])

    keeps = [struct((count * tall, width))] * 2
    result_own, result_other, residual_grad, mix_grad, feed_sums, fk, fs = call(
        feed_kernel, me, (3,),
        [(latents_flat, own), (x_other, rows_spec), (cotangent_flat, own), (cot_other, rows_spec),
         (mix0, whole((length, width))), (mix1, whole((length, width))), (segment_column, whole((length, 1))), vec_op]
        + [(a, ANY) for a in feed_sources[0] + feed_sources[1]],
        [
            own, rows_spec,
            pl.BlockSpec((1, half_rows, features), lambda i, me: (jnp.minimum(i, 1), 0, 0)),
            pl.BlockSpec((half_rows, features), lambda i, me: (jnp.minimum(i, 1) ^ (me[0] & 1), 0)),
            whole((8, features)),
        ] + [ANY] * 2,
        [struct((2, half_rows, features)), struct((half_rows, features)), struct((2, half_rows, features), f32),
         struct((length, features)), struct((8, features), f32)] + keeps,
        [pltpu.VMEM((3, features, features), bf16)] + [pltpu.VMEM((length, features), bf16)] * 5
        + [pltpu.VMEM((half_rows, features), f32)] * 2
        + [pltpu.VMEM((2, 3, features, width), bf16), pltpu.SemaphoreType.DMA(()), pltpu.SemaphoreType.DMA((2,))],
        9 * dense, 30e6,
    )
    f_c = move(fs, core)
    result_back = move(result_other, y)

    def attend_back(qkv, prob, mix, half, after):
        return call(
            lambda me_ref, *refs: attend_back_kernel(scale, *refs), me, (heads,),
            [(qkv, s) for s in head_specs] + [(prob, prob_block), (mix, column_block),
             (mix_grad, pl.BlockSpec((length, head_size), lambda h, me: (0, h + half * heads)))],
            pl.BlockSpec((3, length, head_size), lambda h, me: (0, 0, h)), struct((3, length, width)),
            [pltpu.VMEM((length, head_size), f32)] * 2, 8 * dense, 30e6, after,
        )

    def project_back(grad, half, order, after):
        return call(
            functools.partial(project_back_kernel, half, order), me, (3,),
            [(normed_low, whole((length, features))), (grad, pl.BlockSpec((1, length, width), lambda i, me: (i, 0, 0)))]
            + [(a, ANY) for a in attn_sources[half]],
            [ANY, ANY, pl.BlockSpec((1, 8, width), lambda i, me: (i, 0, 0)), whole((8, features))],
            [struct((count // 2 * tall, width))] * 2 + [struct((3, 8, width), f32), struct((8, features), f32)],
            [pltpu.VMEM((3, features, width), bf16), pltpu.VMEM((3, features, width), bf16),
             pltpu.VMEM((features, 128), f32), pltpu.SemaphoreType.DMA(()), pltpu.SemaphoreType.DMA(())],
            1.5 * dense, 8e6, after,
        )

    half_count = count // 2
    blocks = lambda array, start, size: part(array, start, size, tall)
    qkv_grad0 = attend_back(qkv0, prob0, mix0, 0, [])
    feed_first = lambda start, size, h: [blocks(a, h * half_count + start, size) for a in (fk, f_c)]
    fs0, fs1 = combine(me, [[feed_first(8, 8, 0)], [feed_first(8, 8, 1)]], [qkv_grad0])
    f_s2 = (move(fs0, x), move(fs1, z_near))
    ak0, as0, sums0, totals0 = project_back(qkv_grad0, 0, ORDERS[1], [fs0, fs1])
    a0_c = move(as0, core)
    qkv_grad1 = attend_back(qkv1, prob1, mix1, 1, [totals0])
    terms = [feed_first(4, 4, h) + [blocks(f_s2[h], 4, 4)] for h in range(2)]
    ft0, ft1, at0 = combine(me, [[terms[0]], [terms[1]], [[blocks(ak0, 8, 8), blocks(a0_c, 8, 8)]]], [qkv_grad1])
    f_s3 = (move(ft0, z_near), move(ft1, x))
    a0_s2 = move(at0, z_near)
    ak1, as1, sums1, totals1 = project_back(qkv_grad1, 1, ORDERS[0], [ft0, ft1, at0])
    a1_c = move(as1, core)
    vectors = call(
        vector_pack_kernel, me, (1,),
        [(feed_sums, whole((8, features))), vec_op] + [(a, whole((3, 8, width))) for a in (sums0, sums1)]
        + [(a, whole((8, features))) for a in (totals0, totals1)],
        whole((32, width)), struct((32, width)), [pltpu.VMEM((16, features), f32)], limit=SMALL_LIMIT,
    )
    vectors_c = move(vectors, core)
    feed_terms = lambda start, size: [
        feed_first(start, size, h) + [blocks(f_s2[h], start, size), blocks(f_s3[h], start, size)] for h in range(2)
    ]
    fu, = combine(me, [feed_terms(2, 2)], [vectors])
    f_y = move(fu, y)

    last_first = pl.BlockSpec((1, half_rows, features), lambda i, me: (1 - i, 0, 0))
    grad_rows = pl.BlockSpec((3, half_rows, width), lambda i, me: (0, 1 - (i ^ (me[0] & 1)), 0))
    latent_out, latent_other = call(
        finish_kernel, me, (2,),
        [(latents_flat, own), (x_other, rows_spec), (residual_grad, last_first), (qkv_grad0, grad_rows),
         (qkv_grad1, grad_rows), vec_op] + [(a, ANY) for a in attn_sources[0] + attn_sources[1]],
        [own, rows_spec], [struct((2, half_rows, features), f32), struct((half_rows, features))],
        [pltpu.VMEM((3, features, features), bf16), pltpu.SemaphoreType.DMA(())], 3 * dense, 20e6, [fu],
    )
    latent_back = move(latent_other, y)
    vector_part = lambda array, row: (array, pl.BlockSpec((32, width), lambda i, me: (row // 32, 0)))
    vector_terms = [vector_part(vectors, 0), vector_part(vectors_c, 0)]
    a0_second = [blocks(ak0, 4, 4), blocks(a0_c, 4, 4), blocks(a0_s2, 4, 4)]
    fv, at1, au0 = combine(
        me,
        [
            [t + [blocks(f_y, 2 * h + 1, 1)] for h, t in enumerate(feed_terms(1, 1))],
            [[blocks(ak1, 8, 8), blocks(a1_c, 8, 8)], vector_terms],
            [a0_second],
        ],
        [latent_other],
    )
    a1_s2 = move(at1, x)
    a0_s3 = move(au0, x)
    f_z = move(fv, z_far)
    vector_terms = vector_terms + [vector_part(a1_s2, 8 * tall)]
    au1, = combine(me, [[[blocks(ak1, 4, 4), blocks(a1_c, 4, 4), blocks(a1_s2, 4, 4)], vector_terms]])
    a1_s3 = move(au1, z_near)
    vector_terms = vector_terms + [vector_part(a1_s3, 4 * tall)]
    attn_terms = lambda start, size: [
        [blocks(a, start, size) for a in (ak0, a0_c, a0_s2, a0_s3)],
        [blocks(a, start, size) for a in (ak1, a1_c, a1_s2, a1_s3)],
    ]
    av, = combine(me, [attn_terms(2, 2) + [vector_terms]])
    a_y = move(av, y)
    vector_terms = vector_terms + [vector_part(a_y, 4 * tall)]
    aw, = combine(me, [[t + [blocks(a_y, 2 * h + 1, 1)] for h, t in enumerate(attn_terms(1, 1))] + [vector_terms]])
    a_z = move(aw, z_far)
    vector_terms = vector_terms + [vector_part(a_z, 2 * tall)]
    output_grad, hidden_grads = final(
        me, [t + [blocks(f_y, 2 * h, 1), blocks(f_z, h, 1)] for h, t in enumerate(feed_terms(0, 1))], depth, features,
        (1, 2),
    )
    attn_out, vector_grads = final(
        me, [t + [blocks(a_y, 2 * h, 1), blocks(a_z, h, 1)] for h, t in enumerate(attn_terms(0, 1))], depth, features,
        (3,), vector_terms,
    )

    latent_grads = lax.dynamic_update_slice_in_dim(latent_out, latent_back.astype(f32)[None], 1 - rank, 0)
    activations = lax.dynamic_update_slice_in_dim(result_own, result_back[None], 1 - rank, 0)
    return (
        activations[:, None],
        latent_grads[:, None],
        attn_out,
        output_grad[0],
        hidden_grads,
        vector_grads[:2],
        vector_grads[2:vector_rows],
    )


def layer_norm(vector, gain_row, offset):
    centre = vector - jnp.mean(vector, axis=-1, keepdims=True)
    spread = jnp.mean(centre * centre, axis=-1, keepdims=True)
    return centre * lax.rsqrt(spread + EPSILON) * gain_row + offset


def on_device(
    latents, segments, attention_weights, output_weight, hidden_weights, gains, biases, cotangent
):
    micro_count = latents.shape[0]
    row_count = latents.shape[2]
    features = latents.shape[3]
    head_size = features // HEADS
    score_scale = 1.0 / math.sqrt(head_size)
    own_rank = lax.axis_index("row")
    attn_total = jnp.zeros((3, features, features), jnp.float32)
    output_total = jnp.zeros((features, features), jnp.float32)
    hidden_total = jnp.zeros((2, features, features), jnp.float32)
    gain_total = jnp.zeros((2, features), jnp.float32)
    bias_total = jnp.zeros((7, features), jnp.float32)
    outputs = []
    input_grads = []
    for micro_index in range(micro_count):
        gathered = (
            lax.all_gather(attention_weights, ("seq", "row"), axis=1, tiled=True),
            lax.all_gather(output_weight, ("seq", "row"), axis=0, tiled=True),
            lax.all_gather(hidden_weights, ("seq", "row"), axis=1, tiled=True),
            lax.all_gather(gains, ("seq", "row"), axis=1, tiled=True),
            lax.all_gather(biases, ("seq", "row"), axis=1, tiled=True),
        )
        attention_full, output_full, hidden_full, gain_full, bias_full = gathered
        gain_values = gain_full.astype(jnp.float32)
        bias_values = bias_full.astype(jnp.float32)
        inputs = latents[micro_index, 0].astype(jnp.float32)
        segment_all = segments[micro_index, 0]
        segment_own = lax.dynamic_slice_in_dim(segment_all, own_rank * row_count, row_count)
        normed_one, norm_one_pull = jax.vjp(layer_norm, inputs, gain_values[0], bias_values[0])
        normed_low = normed_one.astype(jnp.bfloat16)
        projected = jnp.einsum(
            "rd,cde->cre", normed_low, attention_full, preferred_element_type=jnp.float32
        )
        queries = (projected[0] + bias_values[2]).astype(jnp.bfloat16)
        own_keys = projected[1].astype(jnp.bfloat16)
        own_values = (projected[2] + bias_values[3]).astype(jnp.bfloat16)
        all_keys, all_values = (
            lax.all_gather(own_keys, "row", axis=0, tiled=True),
            lax.all_gather(own_values, "row", axis=0, tiled=True),
        )
        length = all_keys.shape[0]
        query_heads = queries.reshape(row_count, HEADS, head_size)
        key_heads = all_keys.reshape(length, HEADS, head_size)
        value_heads = all_values.reshape(length, HEADS, head_size)
        same_set = (segment_own[:, None] == segment_all[None, :])[None]
        raw_scores = (
            jnp.einsum("qhd,khd->hqk", query_heads, key_heads, preferred_element_type=jnp.float32)
            * score_scale
        )
        scores = jnp.where(same_set, raw_scores, -1e30)
        row_max = jnp.max(scores, axis=-1, keepdims=True)
        log_total = row_max + jnp.log(jnp.sum(jnp.exp(scores - row_max), axis=-1, keepdims=True))
        weights_low = jnp.exp(scores - log_total).astype(jnp.bfloat16)
        mixture = jnp.einsum(
            "hqk,khd->qhd", weights_low, value_heads, preferred_element_type=jnp.float32
        )
        mixture = mixture.reshape(row_count, features).astype(jnp.bfloat16)
        attended = (
            jnp.dot(mixture, output_full, preferred_element_type=jnp.float32) + bias_values[4]
        )
        residual_one = inputs + attended
        normed_two, norm_two_pull = jax.vjp(
            layer_norm, residual_one, gain_values[1], bias_values[1]
        )
        hidden_low = normed_two.astype(jnp.bfloat16)
        hidden_pre = (
            jnp.dot(hidden_low, hidden_full[0], preferred_element_type=jnp.float32) + bias_values[5]
        )
        activated, gelu_pull = jax.vjp(jax.nn.gelu, hidden_pre)
        active_low = activated.astype(jnp.bfloat16)
        result = residual_one + (
            jnp.dot(active_low, hidden_full[1], preferred_element_type=jnp.float32) + bias_values[6]
        )
        outputs.append(result.astype(jnp.bfloat16))
        live_rows = (segment_own >= 0).astype(jnp.bfloat16)[:, None]
        out_grad = cotangent[micro_index, 0] * live_rows
        out_grad_wide = out_grad.astype(jnp.float32)
        active_grad = jnp.dot(out_grad, hidden_full[1].T, preferred_element_type=jnp.float32)
        pre_grad = gelu_pull(active_grad)[0].astype(jnp.bfloat16)
        normed_two_grad = jnp.dot(pre_grad, hidden_full[0].T, preferred_element_type=jnp.float32)
        residual_part, gain_two, offset_two = norm_two_pull(normed_two_grad)
        residual_grad = out_grad_wide + residual_part
        residual_low = residual_grad.astype(jnp.bfloat16)
        mixture_grad = jnp.dot(residual_low, output_full.T, preferred_element_type=jnp.float32)
        mixture_grad = mixture_grad.astype(jnp.bfloat16).reshape(row_count, HEADS, head_size)
        raw_again = (
            jnp.einsum("qhd,khd->hqk", query_heads, key_heads, preferred_element_type=jnp.float32)
            * score_scale
        )
        weights_wide = jnp.exp(jnp.where(same_set, raw_again, -1e30) - log_total)
        weight_grads = jnp.einsum(
            "qhd,khd->hqk", mixture_grad, value_heads, preferred_element_type=jnp.float32
        )
        centred = jnp.sum(weights_wide * weight_grads, axis=-1, keepdims=True)
        score_grads = (weights_wide * (weight_grads - centred)).astype(jnp.bfloat16)
        query_grad = (
            jnp.einsum("hqk,khd->qhd", score_grads, key_heads, preferred_element_type=jnp.float32)
            * score_scale
        )
        query_grad = query_grad.astype(jnp.bfloat16).reshape(row_count, features)
        weights_again = weights_wide.astype(jnp.bfloat16)
        key_part = (
            jnp.einsum("hqk,qhd->khd", score_grads, query_heads, preferred_element_type=jnp.float32)
            * score_scale
        )
        value_part = jnp.einsum(
            "hqk,qhd->khd", weights_again, mixture_grad, preferred_element_type=jnp.float32
        )
        key_grad, value_grad = (
            lax.psum_scatter(
                key_part.reshape(length, features).astype(jnp.bfloat16),
                "row",
                scatter_dimension=0,
                tiled=True,
            ).astype(jnp.float32),
            lax.psum_scatter(
                value_part.reshape(length, features).astype(jnp.bfloat16),
                "row",
                scatter_dimension=0,
                tiled=True,
            ).astype(jnp.float32),
        )
        key_low = key_grad.astype(jnp.bfloat16)
        value_low = value_grad.astype(jnp.bfloat16)
        projection_grads = jnp.stack([query_grad, key_low, value_low])
        attn_total = attn_total + jnp.einsum(
            "rd,cre->cde", normed_low, projection_grads, preferred_element_type=jnp.float32
        )
        output_total = output_total + jnp.dot(
            mixture.T, residual_low, preferred_element_type=jnp.float32
        )
        hidden_total = hidden_total + jnp.stack(
            [
                jnp.dot(hidden_low.T, pre_grad, preferred_element_type=jnp.float32),
                jnp.dot(active_low.T, out_grad, preferred_element_type=jnp.float32),
            ]
        )
        normed_one_grad = jnp.einsum(
            "cre,cde->rd", projection_grads, attention_full, preferred_element_type=jnp.float32
        )
        input_part, gain_one, offset_one = norm_one_pull(normed_one_grad)
        input_grads.append(residual_grad + input_part)
        gain_total = gain_total + jnp.stack([gain_one, gain_two])
        bias_total = bias_total + jnp.stack(
            [
                offset_one,
                offset_two,
                jnp.sum(query_grad.astype(jnp.float32), axis=0),
                jnp.sum(value_low.astype(jnp.float32), axis=0),
                jnp.sum(residual_low.astype(jnp.float32), axis=0),
                jnp.sum(pre_grad.astype(jnp.float32), axis=0),
                jnp.sum(out_grad_wide, axis=0),
            ]
        )
    attn_grads, output_grads, hidden_grads, gain_grads, bias_grads = (
        lax.psum_scatter(attn_total, ("seq", "row"), scatter_dimension=1, tiled=True),
        lax.psum_scatter(output_total, ("seq", "row"), scatter_dimension=0, tiled=True),
        lax.psum_scatter(hidden_total, ("seq", "row"), scatter_dimension=1, tiled=True),
        lax.psum_scatter(gain_total, ("seq", "row"), scatter_dimension=1, tiled=True),
        lax.psum_scatter(bias_total, ("seq", "row"), scatter_dimension=1, tiled=True),
    )
    return (
        jnp.stack(outputs)[:, None],
        jnp.stack(input_grads)[:, None],
        attn_grads,
        output_grads,
        hidden_grads,
        gain_grads,
        bias_grads,
    )


def solution(mesh):
    def on_mesh(latents, *rest):
        shares_pair = mesh.shape["row"] == latents.shape[0] == 2
        fits = mesh.size == 1 << len(ORDERS[0]) and latents.shape[1] == mesh.shape["seq"]
        return shard_over(whole_sequence if shares_pair and fits else on_device)(latents, *rest)

    def shard_over(function):
        return jax.shard_map(
            function,
            mesh=mesh,
            in_specs=(
                P(None, "seq", "row", None),
                P(None, "seq", None),
                P(None, ("seq", "row"), None),
                P(("seq", "row"), None),
                P(None, ("seq", "row"), None),
                P(None, ("seq", "row")),
                P(None, ("seq", "row")),
                P(None, "seq", "row", None),
            ),
            out_specs=(
                P(None, "seq", "row", None),
                P(None, "seq", "row", None),
                P(None, ("seq", "row"), None),
                P(("seq", "row"), None),
                P(None, ("seq", "row"), None),
                P(None, ("seq", "row")),
                P(None, ("seq", "row")),
            ),
            check_vma=False,
        )

    return on_mesh
```

```python
import functools
import math

import jax
import jax.numpy as jnp
from jax import lax
from jax.experimental import pallas as pl
from jax.experimental.pallas import tpu as pltpu
from jax.sharding import PartitionSpec as P

HEADS = 8
EPSILON = 1e-05
AXES = ("seq", "row")
VMEM_LIMIT = 64 << 20
NN = (((1,), (0,)), ((), ()))
NT = (((1,), (1,)), ((), ()))
TN = (((0,), (0,)), ((), ()))
ORDERS = ((16, 1, 8, 4, 2), (16, 1, 4, 8, 2))


def offset_of(order, position):
    offset = 0
    for bit, mask in enumerate(order):
        if position >> bit & 1:
            offset ^= mask
    return offset


def dot(left, right, dims=NN):
    return lax.dot_general(left, right, dims, preferred_element_type=jnp.float32)


def shift(array, mask, count):
    return lax.ppermute(array, AXES, [(i, i ^ mask) for i in range(count)])


def place_weights(me, order, sources, weight_ref, column, sem):
    depth = weight_ref.shape[1] >> len(order)
    width = sources[0].shape[-1]
    held = sources[0].shape[0]
    for position in range(len(sources) * held):
        owner = me ^ offset_of(order, position)
        rows = pl.ds(pl.multiple_of(owner * depth, depth), depth)
        for matrix in range(3):
            pltpu.make_async_copy(
                sources[position // held].at[position % held, pl.ds(matrix * depth, depth), :],
                weight_ref.at[matrix, rows, pl.ds(column, width)],
                sem,
            ).start()


def collect_grads(me, order, stage_ref, keep_ref, send_ref, sem):
    half = 1 << len(order) - 1
    depth = stage_ref.shape[1] >> len(order)
    for position in reversed(range(2 * half)):
        target = keep_ref if position < half else send_ref
        owner = me ^ offset_of(order, position)
        rows = pl.ds(pl.multiple_of(owner * depth, depth), depth)
        for matrix in range(3):
            place = (position % half * 3 + matrix) * depth
            pltpu.make_async_copy(stage_ref.at[matrix, rows, :], target.at[pl.ds(place, depth), :], sem).start()


def normalize(rows):
    mean = jnp.mean(rows, axis=-1, keepdims=True)
    centre = rows - mean
    spread = jnp.mean(centre * centre, axis=-1, keepdims=True)
    scale = lax.rsqrt(spread + EPSILON)
    return centre * scale, scale


def column_sum(rows):
    return jnp.sum(rows.astype(jnp.float32), axis=0, keepdims=True)


def project(normed_ref, w_ref, vec_ref, qkv_ref, column):
    width = qkv_ref.shape[-1]
    for matrix, bias in ((0, 4), (1, None), (2, 5)):
        out = dot(normed_ref[...], w_ref[matrix])
        if bias is not None:
            out = out + vec_ref[bias : bias + 1, column : column + width]
        qkv_ref[matrix] = out.astype(jnp.bfloat16)


def project_first_kernel(me_ref, own_ref, first_ref, second_ref, *refs):
    *sources, normed_ref, qkv_ref, vec_ref, other_ref, weight_ref, w_ref, block_ref, w_sem, v_sem = refs
    step = pl.program_id(0)
    me = me_ref[0]
    depth = w_ref.shape[1] >> len(ORDERS[0])
    rows = block_ref.shape[1]

    @pl.when(step == 0)
    def _():
        held = sources[0].shape[0]
        for position in range(len(sources) * held):
            pltpu.make_async_copy(
                sources[position // held].at[position % held, pl.ds(3 * depth, rows), pl.ds(0, block_ref.shape[2])],
                block_ref.at[me ^ offset_of(ORDERS[0], position)],
                v_sem,
            ).start()
        place_weights(me, ORDERS[0], sources, w_ref, 0, w_sem)
        other_ref[0 : first_ref.shape[0], :] = first_ref[...]
        other_ref[first_ref.shape[0] :, :] = second_ref[...]
        pltpu.make_async_copy(block_ref, block_ref, v_sem).wait()
        for owner in range(block_ref.shape[0]):
            vec_ref[:, owner * depth : (owner + 1) * depth] = block_ref[owner, :, 0:depth].astype(jnp.float32)

    inputs = jnp.where(step == 0, own_ref[0], other_ref[...]).astype(jnp.float32)
    normed, _ = normalize(inputs)
    normed_ref[...] = (normed * vec_ref[0:1] + vec_ref[2:3]).astype(jnp.bfloat16)

    @pl.when(step == 0)
    def _():
        pltpu.make_async_copy(w_ref, w_ref, w_sem).wait()
        pltpu.make_async_copy(w_ref, weight_ref, w_sem).start()

    project(normed_ref, w_ref, vec_ref, qkv_ref, 0)

    @pl.when(step == 1)
    def _():
        pltpu.make_async_copy(w_ref, weight_ref, w_sem).wait()


def project_next_kernel(me_ref, normed_ref, vec_ref, *refs):
    *sources, qkv_ref, weight_ref, w_ref, sem = refs
    step = pl.program_id(0)

    @pl.when(step == 0)
    def _():
        place_weights(me_ref[0], ORDERS[1], sources, w_ref, 0, sem)
        pltpu.make_async_copy(w_ref, w_ref, sem).wait()
        pltpu.make_async_copy(w_ref, weight_ref, sem).start()

    project(normed_ref, w_ref, vec_ref, qkv_ref, qkv_ref.shape[-1])

    @pl.when(step == 1)
    def _():
        pltpu.make_async_copy(w_ref, weight_ref, sem).wait()


def key_ranges(length):
    quarter = length // 4
    return ((0, 2 * quarter), (0, length), (quarter, length), (quarter, length))


def attend_kernel(scale, q_ref, k_ref, v_ref, column_ref, row_ref, mix_ref, prob_ref):
    length = q_ref.shape[1]
    quarter = length // 4
    for index, (first, last) in enumerate(key_ranges(length)):
        rows = slice(index * quarter, (index + 1) * quarter)
        scores = dot(q_ref[0, rows, :], k_ref[0, first:last, :], NT)
        same = column_ref[rows, :] == row_ref[0, :, first:last]
        scores = jnp.where(same, scores, -1e30)
        top = jnp.max(scores, axis=-1, keepdims=True)
        expo = jnp.exp((scores - top) * scale)
        total = jnp.sum(expo, axis=-1, keepdims=True)
        low = (expo * (1.0 / total)).astype(jnp.bfloat16)
        prob_ref[0, rows, first:last] = low
        mix_ref[rows, :] = dot(low, v_ref[0, first:last, :]).astype(jnp.bfloat16)


def attend_back_kernel(scale, q_ref, k_ref, v_ref, prob_ref, mix_ref, mixg_ref, out_ref, key_acc, value_acc):
    length = q_ref.shape[1]
    quarter = length // 4
    key_acc[...] = jnp.zeros_like(key_acc)
    value_acc[...] = jnp.zeros_like(value_acc)
    for index, (first, last) in enumerate(key_ranges(length)):
        rows = slice(index * quarter, (index + 1) * quarter)
        mix_grad = mixg_ref[rows, :]
        centred = jnp.sum(
            mix_grad.astype(jnp.float32) * mix_ref[rows, :].astype(jnp.float32), axis=-1, keepdims=True
        )
        grads = dot(mix_grad, v_ref[0, first:last, :], NT)
        low = prob_ref[0, rows, first:last]
        score_grads = (low.astype(jnp.float32) * (grads - centred)).astype(jnp.bfloat16)
        out_ref[0, rows, :] = (dot(score_grads, k_ref[0, first:last, :]) * scale).astype(jnp.bfloat16)
        key_acc[first:last, :] += dot(score_grads, q_ref[0, rows, :], TN)
        value_acc[first:last, :] += dot(low, mix_grad, TN)
    out_ref[1] = (key_acc[...] * scale).astype(jnp.bfloat16)
    out_ref[2] = value_acc[...].astype(jnp.bfloat16)


def project_back_kernel(order, me_ref, normed_ref, grad_ref, keep_ref, send_ref, sum_ref, stage_ref, sem):
    step = pl.program_id(0)
    stage_ref[step] = dot(normed_ref[...], grad_ref[0], TN).astype(jnp.bfloat16)
    sum_ref[0] = jnp.broadcast_to(column_sum(grad_ref[0]), sum_ref.shape[1:])

    @pl.when(step == 2)
    def _():
        collect_grads(me_ref[0], order, stage_ref, keep_ref, send_ref, sem)
        pltpu.make_async_copy(stage_ref, stage_ref, sem).wait()


def feed_kernel(
    me_ref, x_own_ref, x_other_ref, cot_own_ref, cot_other_ref, mix0_ref, mix1_ref, column_ref, vec_ref, *refs
):
    sources = refs[:8]
    result_ref, result_other_ref, resg_ref, mixg_ref, sum_ref, keep_ref, send_ref, *refs = refs[8:]
    w_ref, hid_ref, act_ref, og_ref, pre_ref, res_ref, resid, slope, stage_ref, w_sem, g_sem = refs
    step = pl.program_id(0)
    me = me_ref[0]
    half_rows, features = x_other_ref.shape
    width = features // 2

    @pl.when(step == 0)
    def _():
        for half in range(2):
            place_weights(me, ORDERS[half], sources[4 * half : 4 * half + 4], w_ref, half * width, w_sem)
        sum_ref[...] = jnp.zeros_like(sum_ref)
        pltpu.make_async_copy(w_ref, w_ref, w_sem).wait()

    @pl.when(step < 2)
    def _():
        place = pl.multiple_of((step ^ (me & 1)) * half_rows, half_rows)
        rows = pl.ds(place, half_rows)
        inputs = jnp.where(step == 0, x_own_ref[0], x_other_ref[...]).astype(jnp.float32)
        attended = dot(mix0_ref[rows, :], w_ref[0, 0:width, :]) + dot(mix1_ref[rows, :], w_ref[0, width:, :])
        resid[...] = inputs + attended + vec_ref[6:7]
        normed, inverse = normalize(resid[...])
        hid_ref[rows, :] = (normed * vec_ref[1:2] + vec_ref[3:4]).astype(jnp.bfloat16)
        pre = dot(hid_ref[rows, :], w_ref[1]) + vec_ref[7:8]
        square = pre * pre
        tanh = jnp.tanh(0.7978845608 * pre * (1.0 + 0.044715 * square))
        act_ref[rows, :] = (0.5 * pre * (1.0 + tanh)).astype(jnp.bfloat16)
        slope[...] = 0.5 * (1.0 + tanh) + (0.5 * 0.7978845608) * pre * (1.0 - tanh * tanh) * (
            1.0 + (3 * 0.044715) * square
        )
        result = resid[...] + dot(act_ref[rows, :], w_ref[2]) + vec_ref[8:9]
        result = result.astype(jnp.bfloat16)

        @pl.when(step == 0)
        def _():
            result_ref[0] = result

        @pl.when(step == 1)
        def _():
            result_other_ref[...] = result

        live = (column_ref[rows, :] >= 0).astype(jnp.float32)
        cot = jnp.where(step == 0, cot_own_ref[0], cot_other_ref[...]).astype(jnp.float32)
        og_ref[rows, :] = (cot * live).astype(jnp.bfloat16)
        pre_grad = dot(og_ref[rows, :], w_ref[2], NT) * slope[...]
        pre_ref[rows, :] = pre_grad.astype(jnp.bfloat16)
        normed_grad = dot(pre_ref[rows, :], w_ref[1], NT)
        normed, inverse = normalize(resid[...])
        sum_ref[0:1] += column_sum(normed_grad * normed)
        sum_ref[1:2] += column_sum(normed_grad)
        scaled = normed_grad * vec_ref[1:2]
        resg = og_ref[rows, :].astype(jnp.float32) + inverse * (
            scaled
            - jnp.mean(scaled, axis=-1, keepdims=True)
            - normed * jnp.mean(scaled * normed, axis=-1, keepdims=True)
        )
        resg_ref[0] = resg
        res_ref[rows, :] = resg.astype(jnp.bfloat16)
        mixg_ref[...] = dot(res_ref[rows, :], w_ref[0], NT).astype(jnp.bfloat16)
        sum_ref[2:3] += column_sum(res_ref[rows, :])
        sum_ref[3:4] += column_sum(pre_ref[rows, :])
        sum_ref[4:5] += column_sum(og_ref[rows, :])

    @pl.when(step == 2)
    def _():
        for half in range(2):
            columns = slice(half * width, (half + 1) * width)
            for part in range(2):
                mix_ref = (mix0_ref, mix1_ref)[part]
                out_rows = slice(part * width, (part + 1) * width)
                stage_ref[half, 0, out_rows, :] = dot(mix_ref[...], res_ref[:, columns], TN).astype(jnp.bfloat16)
            stage_ref[half, 1] = dot(hid_ref[...], pre_ref[:, columns], TN).astype(jnp.bfloat16)
            stage_ref[half, 2] = dot(act_ref[...], og_ref[:, columns], TN).astype(jnp.bfloat16)
            wide = pl.ds(half * keep_ref.shape[0] // 2, keep_ref.shape[0] // 2)
            collect_grads(
                me, ORDERS[half], stage_ref.at[half], keep_ref.at[wide], send_ref.at[wide], g_sem.at[half]
            )
        for half in range(2):
            pltpu.make_async_copy(stage_ref.at[half], stage_ref.at[half], g_sem.at[half]).wait()


def finish_kernel(me_ref, x_ref, resg_ref, grad0_ref, grad1_ref, w0_ref, w1_ref, vec_ref, out_ref, sum_ref, acc_ref):
    step = pl.program_id(0)
    term = dot(grad0_ref[0], w0_ref[0], NT) + dot(grad1_ref[0], w1_ref[0], NT)

    @pl.when(step == 0)
    def _():
        acc_ref[...] = term

    @pl.when(step == 1)
    def _():
        acc_ref[...] += term

    @pl.when(step == 2)
    def _():
        normed_grad = acc_ref[...] + term
        normed, inverse = normalize(x_ref[...].reshape(acc_ref.shape).astype(jnp.float32))
        sum_ref[...] = jnp.zeros_like(sum_ref)
        sum_ref[0:1] = column_sum(normed_grad * normed)
        sum_ref[1:2] = column_sum(normed_grad)
        scaled = normed_grad * vec_ref[0:1]
        total = resg_ref[0] + inverse * (
            scaled
            - jnp.mean(scaled, axis=-1, keepdims=True)
            - normed * jnp.mean(scaled * normed, axis=-1, keepdims=True)
        )
        out_ref[...] = total.reshape(out_ref.shape).astype(out_ref.dtype)


def pack_first_kernel(me_ref, attention_ref, gain_ref, bias_ref, out_ref, gain_rows, bias_rows, sems):
    matrices, depth, features = attention_ref.shape
    width = features // 2
    base = matrices * depth
    small = [
        pltpu.make_async_copy(gain_ref, gain_rows, sems.at[0]), pltpu.make_async_copy(bias_ref, bias_rows, sems.at[1])
    ]
    copies = [
        pltpu.make_async_copy(
            attention_ref.at[matrix, :, pl.ds(half * width, width)],
            out_ref.at[0, half, pl.ds(matrix * depth, depth), :],
            sems.at[2 + half * matrices + matrix],
        )
        for half in range(2)
        for matrix in range(matrices)
    ]
    for copy in small + copies:
        copy.start()
    out_ref[0, :, base:, :] = jnp.zeros_like(out_ref[0, :, base:, :])
    for copy in small:
        copy.wait()
    gains = gain_ref.shape[0]
    out_ref[0, 0, base : base + gains, 0:depth] = gain_rows[...]
    out_ref[0, 0, base + gains : base + gains + bias_ref.shape[0], 0:depth] = bias_rows[...]
    for copy in copies:
        copy.wait()


def pack_next_kernel(me_ref, output_ref, hidden_ref, out_ref, sems):
    depth, features = output_ref.shape
    width = features // 2
    copies = []
    for half in range(2):
        columns = pl.ds(half * width, width)
        sources = [output_ref.at[:, columns]] + [hidden_ref.at[matrix, :, columns] for matrix in range(2)]
        for matrix, source in enumerate(sources):
            target = out_ref.at[0, half, pl.ds(matrix * depth, depth), :]
            copies.append(pltpu.make_async_copy(source, target, sems.at[len(copies)]))
    for copy in copies:
        copy.start()
    for copy in copies:
        copy.wait()


def join_kernel(moves, me_ref, *refs):
    for source, source_index, target, target_index in moves:
        refs[target][target_index] = refs[source][source_index]


def join_out_kernel(moves, me_ref, *refs):
    *refs, sems = refs
    copies = [
        pltpu.make_async_copy(refs[source].at[source_index], refs[target].at[target_index], sems.at[number])
        for number, (source, source_index, target, target_index) in enumerate(moves)
    ]
    for copy in copies:
        copy.start()
    for copy in copies:
        copy.wait()


def select_kernel(me_ref, rows_ref, *refs):
    row = 0
    for out_ref in refs[:-1]:
        out_ref[...] = rows_ref[0, row : row + out_ref.shape[0], :]
        row += out_ref.shape[0]
    refs[-1][...] = jnp.zeros_like(refs[-1])


def total_of(refs, width):
    total = None
    for ref in refs:
        term = ref[...].astype(jnp.float32).reshape(-1, width)
        total = term if total is None else total + term
    return total


def combine_kernel(sums, me_ref, *refs):
    for first, last, output, row in sums:
        out_ref = refs[output]
        total = total_of(refs[first:last], out_ref.shape[-1])
        out_ref[row : row + total.shape[0], :] = total.astype(out_ref.dtype)


def final_kernel(inputs, me_ref, *refs):
    outs = refs[2 * inputs :]
    depth, features = outs[0].shape[1:]
    width = features // 2
    for half in range(2):
        total = total_of(refs[half * inputs : (half + 1) * inputs], width)
        row = 0
        for out_ref in outs:
            matrices = out_ref.shape[0]
            piece = total[row : row + matrices * depth].reshape(matrices, depth, width)
            out_ref[:, :, half * width : (half + 1) * width] = piece
            row += matrices * depth


def final_vector_kernel(inputs, vectors, me_ref, *refs):
    blocks, terms = refs[: 2 * inputs], refs[2 * inputs : 2 * inputs + vectors]
    out_ref, vector_ref = refs[2 * inputs + vectors :]
    final_kernel(inputs, me_ref, *blocks, out_ref)
    vector_kernel(me_ref, *terms, vector_ref)


def vector_kernel(me_ref, *refs):
    *terms, out_ref = refs
    rows, depth = out_ref.shape
    width = terms[0].shape[-1]
    total = total_of(terms, width)
    lane = lax.broadcasted_iota(jnp.int32, (width, depth), 0)
    column = lax.broadcasted_iota(jnp.int32, (width, depth), 1)
    place = me_ref[0] * depth
    picked = None
    for half in range(2):
        choose = (lane + half * width == column + place).astype(jnp.float32)
        part = lax.dot_general(
            total[half * rows : (half + 1) * rows], choose, NN, precision=lax.Precision.HIGHEST,
            preferred_element_type=jnp.float32,
        )
        picked = part if picked is None else picked + part
    out_ref[...] = picked


def vector_pack_kernel(me_ref, feed_ref, last0_ref, last1_ref, s0_ref, s1_ref, out_ref, row_ref):
    width = out_ref.shape[-1]
    row_ref[...] = jnp.zeros_like(row_ref)
    row_ref[0:1] = last0_ref[0:1] + last1_ref[0:1]
    row_ref[1:2] = feed_ref[0:1]
    row_ref[2:3] = last0_ref[1:2] + last1_ref[1:2]
    row_ref[3:4] = feed_ref[1:2]
    for half, sums in enumerate((s0_ref, s1_ref)):
        row_ref[4:5, half * width : (half + 1) * width] = sums[0, 0:1]
        row_ref[5:6, half * width : (half + 1) * width] = sums[2, 0:1]
    row_ref[6:9] = feed_ref[2:5]
    for half in range(2):
        out_ref[half * 16 : (half + 1) * 16, :] = row_ref[:, half * width : (half + 1) * width].astype(jnp.bfloat16)


ANY = pl.BlockSpec(memory_space=pl.ANY)
VMEM = pl.BlockSpec(memory_space=pltpu.VMEM)
HBM = pl.BlockSpec(memory_space=pltpu.HBM)
SMALL_LIMIT = 24 << 20


def call(kernel, me, grid, operands, out_specs, out_shape, scratch=(), flops=1e6, moved=1e6, after=(), limit=VMEM_LIMIT):
    taken = len(operands) + 1
    after = list(after)
    ordered = ANY if limit == SMALL_LIMIT else HBM

    def body(*refs):
        kernel(*refs[:taken], *refs[taken + len(after) :])

    return pl.pallas_call(
        body,
        grid_spec=pltpu.PrefetchScalarGridSpec(
            num_scalar_prefetch=1,
            grid=grid,
            in_specs=[spec for _, spec in operands] + [ordered] * len(after),
            out_specs=out_specs,
            scratch_shapes=list(scratch),
        ),
        out_shape=out_shape,
        compiler_params=pltpu.CompilerParams(
            dimension_semantics=("arbitrary",) * len(grid), vmem_limit_bytes=limit
        ),
        cost_estimate=pl.CostEstimate(flops=int(flops), bytes_accessed=int(moved), transcendentals=0),
    )(me, *[array for array, _ in operands], *after)


def struct(shape, dtype=jnp.bfloat16):
    return jax.ShapeDtypeStruct(shape, dtype)


def whole(shape):
    return pl.BlockSpec(shape, lambda *_: (0,) * len(shape))


def join(me, arrays, moves, shapes, after=(), kind="local"):
    moves = [(i, source, len(arrays) + o, target) for i, source, o, target in moves]
    place = whole if kind == "far" else lambda shape: VMEM
    kernel = functools.partial(join_out_kernel if kind == "out" else join_kernel, moves)
    return call(
        kernel, me, (1,), [(a, place(a.shape)) for a in arrays],
        [HBM if kind == "out" else place(s) for s in shapes], [struct(s) for s in shapes],
        [pltpu.SemaphoreType.DMA((len(moves),))] if kind == "out" else [], after=after,
        limit=VMEM_LIMIT if kind == "far" else SMALL_LIMIT,
    )


def part(array, start, size, tall):
    return array, pl.BlockSpec((size * tall, array.shape[-1]), lambda i, me: (start // size, 0))


def combine(me, outputs, after=()):
    operands, sums, shapes = [], [], []
    count = sum(len(terms) for group in outputs for terms in group)
    for number, group in enumerate(outputs):
        row = 0
        for terms in group:
            first = len(operands)
            operands.extend(terms)
            sums.append((first, len(operands), count + number, row))
            row += terms[0][1].block_shape[0]
        shapes.append((row, group[0][0][0].shape[-1]))
    return call(
        functools.partial(combine_kernel, sums), me, (1,), operands, [whole(s) for s in shapes],
        [struct(s) for s in shapes], after=after,
    )


def final(me, halves, depth, features, counts, vectors=()):
    shapes = [(matrices, depth, features) for matrices in counts]
    kernel = functools.partial(final_kernel, len(halves[0]))
    if vectors:
        kernel = functools.partial(final_vector_kernel, len(halves[0]), len(vectors))
        shapes.append((vectors[0][1].block_shape[0] // 2, depth))
    return call(
        kernel, me, (1,), halves[0] + halves[1] + list(vectors), [whole(s) for s in shapes],
        [struct(s, jnp.float32) for s in shapes],
    )


def whole_sequence(
    latents, segments, attention_weights, output_weight, hidden_weights, gains, biases, cotangent
):
    half_rows, features = latents.shape[2:]
    length = 2 * half_rows
    head_size = features // HEADS
    scale = 1.0 / math.sqrt(head_size)
    width = features // 2
    count = 1 << len(ORDERS[0])
    depth = features // count
    rank = lax.axis_index("row")
    device = (lax.axis_index("seq") * 2 + rank).astype(jnp.int32)
    me = device.reshape(1)
    bf16, f32 = jnp.bfloat16, jnp.float32
    dense = 2.0 * length * features * features
    tall = 3 * depth
    vector_rows = gains.shape[0] + biases.shape[0]
    padded = tall + 16

    def move(array, mask):
        return shift(array, mask, count)

    def double(held, got, after=()):
        return join(me, [held, got], [(0, 0, 0, 0), (1, 0, 0, 1)], [(2,) + held.shape[1:]], after)[0]

    def split(held, got, rows, after=(), kind="local"):
        moves, shapes = [], []
        for half in range(2):
            for source in range(2):
                for block in range(2):
                    moves.append((source, (block, half, pl.ds(0, rows[half])), half, 2 * source + block))
            shapes.append((4, rows[half], width))
        return join(me, [held, got], moves, shapes, after, kind)

    def append(held, got, after=(), kind="out"):
        moves, shapes = [], []
        for half in range(2):
            for source in range(2):
                moves.append((2 * half + source, pl.ds(0, 4), half, pl.ds(4 * source, 4)))
            shapes.append((8,) + held[half].shape[1:])
        return join(me, [held[0], got[0], held[1], got[1]], moves, shapes, after, kind)

    z_far, y, z_near, x, core = 16, 1, 8, 4, 2
    def pack(kernel, arrays, rows, scratch, after=()):
        return call(
            kernel, me, (1,), [(a, HBM) for a in arrays], VMEM, struct((1, 2, rows, width)), scratch, after=after,
            limit=SMALL_LIMIT,
        )

    latents_flat = latents[:, 0]
    cotangent_flat = cotangent[:, 0]

    def select(array, parts, after):
        shapes = [(half_rows // parts, features)] * parts
        return call(
            select_kernel, me, (1,),
            [(array, pl.BlockSpec((1, half_rows, features), lambda i, me: (1 - (me[0] & 1), 0, 0)))],
            [whole(shape) for shape in shapes] + [VMEM], [struct(shape) for shape in shapes] + [struct((8, 128), f32)],
            after=after, limit=SMALL_LIMIT,
        )

    sems = lambda number: pltpu.SemaphoreType.DMA((number,))
    a1 = pack(
        pack_first_kernel, [attention_weights, gains, biases], padded,
        [pltpu.VMEM(gains.shape, bf16), pltpu.VMEM(biases.shape, bf16), sems(8)],
    )
    *x_send, x_token = select(latents_flat, 2, [a1])
    a2 = double(a1, move(a1, z_far), [x_token])
    f1 = pack(pack_next_kernel, [output_weight, hidden_weights], tall, [sems(6)], [a2])
    a4 = split(a2, move(a2, y), (padded, tall), [f1])
    x_first = move(x_send[0], y)
    cot_send, cot_token = select(cotangent_flat, 1, a4)
    f2 = double(f1, move(f1, z_far), [a4[0], cot_token])
    a8 = append(a4, (move(a4[0], z_near), move(a4[1], x)), [f2, x_first])
    a_core = [move(a, core) for a in a8]
    x_second = move(x_send[1], y)
    f4 = split(f2, move(f2, y), (tall, tall), a8, "out")
    a_far = join(
        me, [move(a8[0], x), move(a8[1], z_near)], [(h, pl.ds(0, 8), h, pl.ds(0, 8)) for h in range(2)],
        [a.shape for a in a8], [f4[0], x_second], "out",
    )
    a_far_core = [move(a, core) for a in a_far]
    attn_sources = [[a8[h], a_far[h], a_core[h], a_far_core[h]] for h in range(2)]

    segment_row = segments
    segment_column = lax.dynamic_index_in_dim(segments[:, 0], rank, 0, keepdims=False)[:, None]

    own = pl.BlockSpec((1, half_rows, features), lambda i, me: (me[0] & 1, 0, 0))
    local = pl.BlockSpec((half_rows, features), lambda i, me: (i ^ (me[0] & 1), 0))
    local3 = pl.BlockSpec((3, half_rows, width), lambda i, me: (0, i ^ (me[0] & 1), 0))
    rows_spec = whole((half_rows, features))
    w_scratch = pltpu.VMEM((3, features, width), bf16)
    w_struct = struct((3, features, width))
    normed_low, qkv0, vec, x_other, weight0 = call(
        project_first_kernel, me, (2,),
        [(latents_flat, own)] + [(a, whole(a.shape)) for a in (x_first, x_second)] + [(a, ANY) for a in attn_sources[0]],
        [local, local3, whole((16, features)), rows_spec, ANY],
        [struct((length, features)), struct((3, length, width)), struct((16, features), f32),
         struct((half_rows, features)), w_struct],
        [w_scratch, pltpu.VMEM((count, 16, 128), bf16), pltpu.SemaphoreType.DMA(()), pltpu.SemaphoreType.DMA(())],
        1.5 * dense, 16e6, f4,
    )
    vec_op = (vec, whole((16, features)))
    cot_other = move(cot_send, y)
    f8 = append(f4, (move(f4[0], z_near), move(f4[1], x)), [vec], "far")
    f_core = [move(a, core) for a in f8]
    f_far = (move(f8[0], x), move(f8[1], z_near))
    qkv1, weight1 = call(
        project_next_kernel, me, (2,),
        [(normed_low, pl.BlockSpec((half_rows, features), lambda i, me: (i, 0))), vec_op]
        + [(a, ANY) for a in attn_sources[1]],
        [pl.BlockSpec((3, half_rows, width), lambda i, me: (0, i, 0)), ANY], [struct((3, length, width)), w_struct],
        [w_scratch, pltpu.SemaphoreType.DMA(())], 1.5 * dense, 8e6, f8,
    )

    heads = width // head_size
    head_specs = [
        pl.BlockSpec((1, length, head_size), functools.partial(lambda c, h, me: (c, 0, h), c)) for c in range(3)
    ]
    column_block = pl.BlockSpec((length, head_size), lambda h, me: (0, h))
    prob_block = pl.BlockSpec((1, length, length), lambda h, me: (h, 0, 0))
    segment_spec = pl.BlockSpec((1, 1, length), lambda h, me: (me[0] & 1, 0, 0))

    def attend(qkv, after):
        return call(
            lambda me_ref, *refs: attend_kernel(scale, *refs), me, (heads,),
            [(qkv, s) for s in head_specs] + [(segment_column, whole((length, 1))), (segment_row, segment_spec)],
            [column_block, prob_block], [struct((length, width)), struct((heads, length, length))], [],
            4 * dense, 30e6, after,
        )

    mix0, prob0 = attend(qkv0, [qkv1])
    f_far_core = [move(a, core) for a in f_far]
    feed_sources = [[f8[h], f_far[h], f_core[h], f_far_core[h]] for h in range(2)]
    mix1, prob1 = attend(qkv1, [mix0])

    keeps = [struct((count * tall, width))] * 2
    result_own, result_other, residual_grad, mix_grad, feed_sums, fk, fs = call(
        feed_kernel, me, (3,),
        [(latents_flat, own), (x_other, rows_spec), (cotangent_flat, own), (cot_other, rows_spec),
         (mix0, whole((length, width))), (mix1, whole((length, width))), (segment_column, whole((length, 1))), vec_op]
        + [(a, ANY) for a in feed_sources[0] + feed_sources[1]],
        [
            own, rows_spec,
            pl.BlockSpec((1, half_rows, features), lambda i, me: (jnp.minimum(i, 1), 0, 0)),
            pl.BlockSpec((half_rows, features), lambda i, me: (jnp.minimum(i, 1) ^ (me[0] & 1), 0)),
            whole((8, features)),
        ] + [ANY] * 2,
        [struct((2, half_rows, features)), struct((half_rows, features)), struct((2, half_rows, features), f32),
         struct((length, features)), struct((8, features), f32)] + keeps,
        [pltpu.VMEM((3, features, features), bf16)] + [pltpu.VMEM((length, features), bf16)] * 5
        + [pltpu.VMEM((half_rows, features), f32)] * 2
        + [pltpu.VMEM((2, 3, features, width), bf16), pltpu.SemaphoreType.DMA(()), pltpu.SemaphoreType.DMA((2,))],
        9 * dense, 30e6,
    )
    f_c = move(fs, core)
    result_back = move(result_other, y)

    def attend_back(qkv, prob, mix, half, after):
        return call(
            lambda me_ref, *refs: attend_back_kernel(scale, *refs), me, (heads,),
            [(qkv, s) for s in head_specs] + [(prob, prob_block), (mix, column_block),
             (mix_grad, pl.BlockSpec((length, head_size), lambda h, me: (0, h + half * heads)))],
            pl.BlockSpec((3, length, head_size), lambda h, me: (0, 0, h)), struct((3, length, width)),
            [pltpu.VMEM((length, head_size), f32)] * 2, 8 * dense, 30e6, after,
        )

    def project_back(grad, order, after):
        return call(
            functools.partial(project_back_kernel, order), me, (3,),
            [(normed_low, whole((length, features))), (grad, pl.BlockSpec((1, length, width), lambda i, me: (i, 0, 0)))],
            [ANY, ANY, pl.BlockSpec((1, 8, width), lambda i, me: (i, 0, 0))],
            [struct((count // 2 * tall, width))] * 2 + [struct((3, 8, width), f32)],
            [w_scratch, pltpu.SemaphoreType.DMA(())], 1.5 * dense, 8e6, after,
        )

    def finish(rows, index, flip, out_spec, out_struct, after):
        block = lambda me: (me[0] & 1) ^ flip
        grad_spec = pl.BlockSpec((1, half_rows, width), lambda i, me: (i, block(me), 0))
        w_spec = pl.BlockSpec((1, features, width), lambda i, me: (i, 0, 0))
        return call(
            finish_kernel, me, (3,),
            [rows, (residual_grad, pl.BlockSpec((1, half_rows, features), lambda i, me: (index, 0, 0))),
             (qkv_grad0, grad_spec), (qkv_grad1, grad_spec), (weight0, w_spec), (weight1, w_spec), vec_op],
            [out_spec, whole((8, features))], [out_struct, struct((8, features), f32)],
            [pltpu.VMEM((half_rows, features), f32)], 8 * dense, 20e6, after,
        )

    half_count = count // 2
    blocks = lambda array, start, size: part(array, start, size, tall)
    vector_part = lambda array, row: (array, pl.BlockSpec((32, width), lambda i, me: (row // 32, 0)))
    feed_first = lambda start, size, h: [blocks(a, h * half_count + start, size) for a in (fk, f_c)]
    qkv_grad0 = attend_back(qkv0, prob0, mix0, 0, [])
    fs0, fs1 = combine(me, [[feed_first(8, 8, 0)], [feed_first(8, 8, 1)]], [qkv_grad0])
    f_s2 = (move(fs0, x), move(fs1, z_near))
    ak0, as0, sums0 = project_back(qkv_grad0, ORDERS[0], [fs0, fs1])
    a0_c = move(as0, core)
    qkv_grad1 = attend_back(qkv1, prob1, mix1, 1, [ak0])
    terms = [feed_first(4, 4, h) + [blocks(f_s2[h], 4, 4)] for h in range(2)]
    ft0, ft1, at0 = combine(me, [[terms[0]], [terms[1]], [[blocks(ak0, 8, 8), blocks(a0_c, 8, 8)]]], [qkv_grad1])
    f_s3 = (move(ft0, z_near), move(ft1, x))
    a0_s2 = move(at0, x)
    ak1, as1, sums1 = project_back(qkv_grad1, ORDERS[1], [ft0, ft1, at0, result_back])
    a1_c = move(as1, core)
    feed_terms = lambda start, size: [
        feed_first(start, size, h) + [blocks(f_s2[h], start, size), blocks(f_s3[h], start, size)] for h in range(2)
    ]
    fu, = combine(me, [feed_terms(2, 2)], [ak1])
    f_y = move(fu, y)
    latent_other, sums_other = finish((x_other, rows_spec), 1, 1, rows_spec, struct((half_rows, features)), [fu])
    latent_back = move(latent_other, y)
    at1, = combine(me, [[[blocks(ak1, 8, 8), blocks(a1_c, 8, 8)]]], [latent_other])
    a1_s2 = move(at1, z_near)
    latent_out, sums_own = finish((latents_flat, own), 0, 0, own, struct((2, half_rows, features), f32), [at1])
    vectors = call(
        vector_pack_kernel, me, (1,),
        [(a, whole((8, features))) for a in (feed_sums, sums_own, sums_other)]
        + [(a, whole((3, 8, width))) for a in (sums0, sums1)],
        whole((32, width)), struct((32, width)), [pltpu.VMEM((16, features), f32)], after=[f_y],
    )
    vectors_c = move(vectors, core)
    vector_terms = [vector_part(vectors, 0), vector_part(vectors_c, 0)]
    vectors_z = move(combine(me, [[vector_terms]])[0], z_near)
    vector_terms = vector_terms + [vector_part(vectors_z, 0)]
    au0, au1 = combine(
        me,
        [
            [[blocks(ak0, 4, 4), blocks(a0_c, 4, 4), blocks(a0_s2, 4, 4)]],
            [[blocks(ak1, 4, 4), blocks(a1_c, 4, 4), blocks(a1_s2, 4, 4)], vector_terms],
        ],
    )
    a0_s3 = move(au0, z_near)
    a1_s3 = move(au1, x)
    vector_terms = vector_terms + [vector_part(a1_s3, 4 * tall)]
    attn_terms = lambda start, size: [
        [blocks(a, start, size) for a in (ak0, a0_c, a0_s2, a0_s3)],
        [blocks(a, start, size) for a in (ak1, a1_c, a1_s2, a1_s3)],
    ]
    av, fv = combine(
        me,
        [
            attn_terms(2, 2) + [vector_terms],
            [t + [blocks(f_y, 2 * h + 1, 1)] for h, t in enumerate(feed_terms(1, 1))],
        ],
    )
    a_y = move(av, y)
    f_z = move(fv, z_far)
    vector_terms = vector_terms + [vector_part(a_y, 4 * tall)]
    aw, = combine(me, [[t + [blocks(a_y, 2 * h + 1, 1)] for h, t in enumerate(attn_terms(1, 1))] + [vector_terms]])
    a_z = move(aw, z_far)
    vector_terms = vector_terms + [vector_part(a_z, 2 * tall)]
    output_grad, hidden_grads = final(
        me, [t + [blocks(f_y, 2 * h, 1), blocks(f_z, h, 1)] for h, t in enumerate(feed_terms(0, 1))], depth, features,
        (1, 2),
    )
    attn_out, vector_grads = final(
        me, [t + [blocks(a_y, 2 * h, 1), blocks(a_z, h, 1)] for h, t in enumerate(attn_terms(0, 1))], depth, features,
        (3,), vector_terms,
    )

    latent_grads = lax.dynamic_update_slice_in_dim(latent_out, latent_back.astype(f32)[None], 1 - rank, 0)
    activations = lax.dynamic_update_slice_in_dim(result_own, result_back[None], 1 - rank, 0)
    return (
        activations[:, None],
        latent_grads[:, None],
        attn_out,
        output_grad[0],
        hidden_grads,
        vector_grads[:2],
        vector_grads[2:vector_rows],
    )


def layer_norm(vector, gain_row, offset):
    centre = vector - jnp.mean(vector, axis=-1, keepdims=True)
    spread = jnp.mean(centre * centre, axis=-1, keepdims=True)
    return centre * lax.rsqrt(spread + EPSILON) * gain_row + offset


def on_device(
    latents, segments, attention_weights, output_weight, hidden_weights, gains, biases, cotangent
):
    micro_count = latents.shape[0]
    row_count = latents.shape[2]
    features = latents.shape[3]
    head_size = features // HEADS
    score_scale = 1.0 / math.sqrt(head_size)
    own_rank = lax.axis_index("row")
    attn_total = jnp.zeros((3, features, features), jnp.float32)
    output_total = jnp.zeros((features, features), jnp.float32)
    hidden_total = jnp.zeros((2, features, features), jnp.float32)
    gain_total = jnp.zeros((2, features), jnp.float32)
    bias_total = jnp.zeros((7, features), jnp.float32)
    outputs = []
    input_grads = []
    for micro_index in range(micro_count):
        gathered = (
            lax.all_gather(attention_weights, ("seq", "row"), axis=1, tiled=True),
            lax.all_gather(output_weight, ("seq", "row"), axis=0, tiled=True),
            lax.all_gather(hidden_weights, ("seq", "row"), axis=1, tiled=True),
            lax.all_gather(gains, ("seq", "row"), axis=1, tiled=True),
            lax.all_gather(biases, ("seq", "row"), axis=1, tiled=True),
        )
        attention_full, output_full, hidden_full, gain_full, bias_full = gathered
        gain_values = gain_full.astype(jnp.float32)
        bias_values = bias_full.astype(jnp.float32)
        inputs = latents[micro_index, 0].astype(jnp.float32)
        segment_all = segments[micro_index, 0]
        segment_own = lax.dynamic_slice_in_dim(segment_all, own_rank * row_count, row_count)
        normed_one, norm_one_pull = jax.vjp(layer_norm, inputs, gain_values[0], bias_values[0])
        normed_low = normed_one.astype(jnp.bfloat16)
        projected = jnp.einsum(
            "rd,cde->cre", normed_low, attention_full, preferred_element_type=jnp.float32
        )
        queries = (projected[0] + bias_values[2]).astype(jnp.bfloat16)
        own_keys = projected[1].astype(jnp.bfloat16)
        own_values = (projected[2] + bias_values[3]).astype(jnp.bfloat16)
        all_keys, all_values = (
            lax.all_gather(own_keys, "row", axis=0, tiled=True),
            lax.all_gather(own_values, "row", axis=0, tiled=True),
        )
        length = all_keys.shape[0]
        query_heads = queries.reshape(row_count, HEADS, head_size)
        key_heads = all_keys.reshape(length, HEADS, head_size)
        value_heads = all_values.reshape(length, HEADS, head_size)
        same_set = (segment_own[:, None] == segment_all[None, :])[None]
        raw_scores = (
            jnp.einsum("qhd,khd->hqk", query_heads, key_heads, preferred_element_type=jnp.float32)
            * score_scale
        )
        scores = jnp.where(same_set, raw_scores, -1e30)
        row_max = jnp.max(scores, axis=-1, keepdims=True)
        log_total = row_max + jnp.log(jnp.sum(jnp.exp(scores - row_max), axis=-1, keepdims=True))
        weights_low = jnp.exp(scores - log_total).astype(jnp.bfloat16)
        mixture = jnp.einsum(
            "hqk,khd->qhd", weights_low, value_heads, preferred_element_type=jnp.float32
        )
        mixture = mixture.reshape(row_count, features).astype(jnp.bfloat16)
        attended = (
            jnp.dot(mixture, output_full, preferred_element_type=jnp.float32) + bias_values[4]
        )
        residual_one = inputs + attended
        normed_two, norm_two_pull = jax.vjp(
            layer_norm, residual_one, gain_values[1], bias_values[1]
        )
        hidden_low = normed_two.astype(jnp.bfloat16)
        hidden_pre = (
            jnp.dot(hidden_low, hidden_full[0], preferred_element_type=jnp.float32) + bias_values[5]
        )
        activated, gelu_pull = jax.vjp(jax.nn.gelu, hidden_pre)
        active_low = activated.astype(jnp.bfloat16)
        result = residual_one + (
            jnp.dot(active_low, hidden_full[1], preferred_element_type=jnp.float32) + bias_values[6]
        )
        outputs.append(result.astype(jnp.bfloat16))
        live_rows = (segment_own >= 0).astype(jnp.bfloat16)[:, None]
        out_grad = cotangent[micro_index, 0] * live_rows
        out_grad_wide = out_grad.astype(jnp.float32)
        active_grad = jnp.dot(out_grad, hidden_full[1].T, preferred_element_type=jnp.float32)
        pre_grad = gelu_pull(active_grad)[0].astype(jnp.bfloat16)
        normed_two_grad = jnp.dot(pre_grad, hidden_full[0].T, preferred_element_type=jnp.float32)
        residual_part, gain_two, offset_two = norm_two_pull(normed_two_grad)
        residual_grad = out_grad_wide + residual_part
        residual_low = residual_grad.astype(jnp.bfloat16)
        mixture_grad = jnp.dot(residual_low, output_full.T, preferred_element_type=jnp.float32)
        mixture_grad = mixture_grad.astype(jnp.bfloat16).reshape(row_count, HEADS, head_size)
        raw_again = (
            jnp.einsum("qhd,khd->hqk", query_heads, key_heads, preferred_element_type=jnp.float32)
            * score_scale
        )
        weights_wide = jnp.exp(jnp.where(same_set, raw_again, -1e30) - log_total)
        weight_grads = jnp.einsum(
            "qhd,khd->hqk", mixture_grad, value_heads, preferred_element_type=jnp.float32
        )
        centred = jnp.sum(weights_wide * weight_grads, axis=-1, keepdims=True)
        score_grads = (weights_wide * (weight_grads - centred)).astype(jnp.bfloat16)
        query_grad = (
            jnp.einsum("hqk,khd->qhd", score_grads, key_heads, preferred_element_type=jnp.float32)
            * score_scale
        )
        query_grad = query_grad.astype(jnp.bfloat16).reshape(row_count, features)
        weights_again = weights_wide.astype(jnp.bfloat16)
        key_part = (
            jnp.einsum("hqk,qhd->khd", score_grads, query_heads, preferred_element_type=jnp.float32)
            * score_scale
        )
        value_part = jnp.einsum(
            "hqk,qhd->khd", weights_again, mixture_grad, preferred_element_type=jnp.float32
        )
        key_grad, value_grad = (
            lax.psum_scatter(
                key_part.reshape(length, features).astype(jnp.bfloat16),
                "row",
                scatter_dimension=0,
                tiled=True,
            ).astype(jnp.float32),
            lax.psum_scatter(
                value_part.reshape(length, features).astype(jnp.bfloat16),
                "row",
                scatter_dimension=0,
                tiled=True,
            ).astype(jnp.float32),
        )
        key_low = key_grad.astype(jnp.bfloat16)
        value_low = value_grad.astype(jnp.bfloat16)
        projection_grads = jnp.stack([query_grad, key_low, value_low])
        attn_total = attn_total + jnp.einsum(
            "rd,cre->cde", normed_low, projection_grads, preferred_element_type=jnp.float32
        )
        output_total = output_total + jnp.dot(
            mixture.T, residual_low, preferred_element_type=jnp.float32
        )
        hidden_total = hidden_total + jnp.stack(
            [
                jnp.dot(hidden_low.T, pre_grad, preferred_element_type=jnp.float32),
                jnp.dot(active_low.T, out_grad, preferred_element_type=jnp.float32),
            ]
        )
        normed_one_grad = jnp.einsum(
            "cre,cde->rd", projection_grads, attention_full, preferred_element_type=jnp.float32
        )
        input_part, gain_one, offset_one = norm_one_pull(normed_one_grad)
        input_grads.append(residual_grad + input_part)
        gain_total = gain_total + jnp.stack([gain_one, gain_two])
        bias_total = bias_total + jnp.stack(
            [
                offset_one,
                offset_two,
                jnp.sum(query_grad.astype(jnp.float32), axis=0),
                jnp.sum(value_low.astype(jnp.float32), axis=0),
                jnp.sum(residual_low.astype(jnp.float32), axis=0),
                jnp.sum(pre_grad.astype(jnp.float32), axis=0),
                jnp.sum(out_grad_wide, axis=0),
            ]
        )
    attn_grads, output_grads, hidden_grads, gain_grads, bias_grads = (
        lax.psum_scatter(attn_total, ("seq", "row"), scatter_dimension=1, tiled=True),
        lax.psum_scatter(output_total, ("seq", "row"), scatter_dimension=0, tiled=True),
        lax.psum_scatter(hidden_total, ("seq", "row"), scatter_dimension=1, tiled=True),
        lax.psum_scatter(gain_total, ("seq", "row"), scatter_dimension=1, tiled=True),
        lax.psum_scatter(bias_total, ("seq", "row"), scatter_dimension=1, tiled=True),
    )
    return (
        jnp.stack(outputs)[:, None],
        jnp.stack(input_grads)[:, None],
        attn_grads,
        output_grads,
        hidden_grads,
        gain_grads,
        bias_grads,
    )


def solution(mesh):
    def on_mesh(latents, *rest):
        shares_pair = mesh.shape["row"] == latents.shape[0] == 2
        fits = mesh.size == 1 << len(ORDERS[0]) and latents.shape[1] == mesh.shape["seq"]
        return shard_over(whole_sequence if shares_pair and fits else on_device)(latents, *rest)

    def shard_over(function):
        return jax.shard_map(
            function,
            mesh=mesh,
            in_specs=(
                P(None, "seq", "row", None),
                P(None, "seq", None),
                P(None, ("seq", "row"), None),
                P(("seq", "row"), None),
                P(None, ("seq", "row"), None),
                P(None, ("seq", "row")),
                P(None, ("seq", "row")),
                P(None, "seq", "row", None),
            ),
            out_specs=(
                P(None, "seq", "row", None),
                P(None, "seq", "row", None),
                P(None, ("seq", "row"), None),
                P(("seq", "row"), None),
                P(None, ("seq", "row"), None),
                P(None, ("seq", "row")),
                P(None, ("seq", "row")),
            ),
            check_vma=False,
        )

    return on_mesh
```

```python
import functools
import math

import jax
import jax.numpy as jnp
from jax import lax
from jax.experimental import pallas as pl
from jax.experimental.pallas import tpu as pltpu
from jax.sharding import PartitionSpec as P

HEADS = 8
EPSILON = 1e-05
AXES = ("seq", "row")
VMEM_LIMIT = 64 << 20
NN = (((1,), (0,)), ((), ()))
NT = (((1,), (1,)), ((), ()))
TN = (((0,), (0,)), ((), ()))
ORDERS = ((16, 1, 8, 4, 2), (16, 1, 4, 8, 2))


def offset_of(order, position):
    offset = 0
    for bit, mask in enumerate(order):
        if position >> bit & 1:
            offset ^= mask
    return offset


def dot(left, right, dims=NN):
    return lax.dot_general(left, right, dims, preferred_element_type=jnp.float32)


def shift(array, mask, count):
    return lax.ppermute(array, AXES, [(i, i ^ mask) for i in range(count)])


def place_weights(me, order, sources, weight_ref, column, sem):
    depth = weight_ref.shape[1] >> len(order)
    width = sources[0].shape[-1]
    held = sources[0].shape[0]
    for position in range(len(sources) * held):
        owner = me ^ offset_of(order, position)
        rows = pl.ds(pl.multiple_of(owner * depth, depth), depth)
        for matrix in range(3):
            pltpu.make_async_copy(
                sources[position // held].at[position % held, pl.ds(matrix * depth, depth), :],
                weight_ref.at[matrix, rows, pl.ds(column, width)],
                sem,
            ).start()


def normalize(rows):
    mean = jnp.mean(rows, axis=-1, keepdims=True)
    centre = rows - mean
    spread = jnp.mean(centre * centre, axis=-1, keepdims=True)
    scale = lax.rsqrt(spread + EPSILON)
    return centre * scale, scale


def column_sum(rows):
    return jnp.sum(rows.astype(jnp.float32), axis=0, keepdims=True)


def project(normed_ref, w_ref, vec_ref, qkv_ref, column):
    width = qkv_ref.shape[-1]
    for matrix, bias in ((0, 4), (1, None), (2, 5)):
        out = dot(normed_ref[...], w_ref[matrix])
        if bias is not None:
            out = out + vec_ref[bias : bias + 1, column : column + width]
        qkv_ref[matrix] = out.astype(jnp.bfloat16)


def project_first_kernel(me_ref, own_ref, first_ref, second_ref, *refs):
    *sources, normed_ref, qkv_ref, vec_ref, other_ref, weight_ref, w_ref, block_ref, w_sem, v_sem = refs
    step = pl.program_id(0)
    me = me_ref[0]
    depth = w_ref.shape[1] >> len(ORDERS[0])
    rows = block_ref.shape[1]

    @pl.when(step == 0)
    def _():
        held = sources[0].shape[0]
        for position in range(len(sources) * held):
            pltpu.make_async_copy(
                sources[position // held].at[position % held, pl.ds(3 * depth, rows), pl.ds(0, block_ref.shape[2])],
                block_ref.at[me ^ offset_of(ORDERS[0], position)],
                v_sem,
            ).start()
        place_weights(me, ORDERS[0], sources, w_ref, 0, w_sem)
        other_ref[0 : first_ref.shape[0], :] = first_ref[...]
        other_ref[first_ref.shape[0] :, :] = second_ref[...]
        pltpu.make_async_copy(block_ref, block_ref, v_sem).wait()
        for owner in range(block_ref.shape[0]):
            vec_ref[:, owner * depth : (owner + 1) * depth] = block_ref[owner, :, 0:depth].astype(jnp.float32)

    inputs = jnp.where(step == 0, own_ref[0], other_ref[...]).astype(jnp.float32)
    normed, _ = normalize(inputs)
    normed_ref[...] = (normed * vec_ref[0:1] + vec_ref[2:3]).astype(jnp.bfloat16)

    @pl.when(step == 0)
    def _():
        pltpu.make_async_copy(w_ref, w_ref, w_sem).wait()
        pltpu.make_async_copy(w_ref, weight_ref, w_sem).start()

    project(normed_ref, w_ref, vec_ref, qkv_ref, 0)

    @pl.when(step == 1)
    def _():
        pltpu.make_async_copy(w_ref, weight_ref, w_sem).wait()


def project_next_kernel(me_ref, normed_ref, vec_ref, *refs):
    *sources, qkv_ref, weight_ref, w_ref, sem = refs
    step = pl.program_id(0)

    @pl.when(step == 0)
    def _():
        place_weights(me_ref[0], ORDERS[1], sources, w_ref, 0, sem)
        pltpu.make_async_copy(w_ref, w_ref, sem).wait()
        pltpu.make_async_copy(w_ref, weight_ref, sem).start()

    project(normed_ref, w_ref, vec_ref, qkv_ref, qkv_ref.shape[-1])

    @pl.when(step == 1)
    def _():
        pltpu.make_async_copy(w_ref, weight_ref, sem).wait()


def key_ranges(length):
    quarter = length // 4
    return ((0, 2 * quarter), (0, length), (quarter, length), (quarter, length))


def attend_kernel(scale, q_ref, k_ref, v_ref, column_ref, row_ref, mix_ref, prob_ref, inverse_ref):
    length = q_ref.shape[1]
    tile = length // 8
    ranges = [(row, *key_ranges(length)[2 * row // (length // 2)]) for row in range(0, length, tile)]

    def score(index):
        row, first, last = ranges[index]
        return dot(q_ref[0, row : row + tile, :], k_ref[0, first:last, :], NT)

    def mix(index, low, inverse):
        row, first, last = ranges[index]
        mix_ref[row : row + tile, :] = (dot(low, v_ref[0, first:last, :]) * inverse).astype(jnp.bfloat16)

    scores, before = score(0), None
    for index, (row, first, last) in enumerate(ranges):
        following = score(index + 1) if index + 1 < len(ranges) else None
        rows = slice(row, row + tile)
        same = column_ref[rows, :] == row_ref[0, :, first:last]
        scores = jnp.where(same, scores, -1e30)
        top = jnp.max(scores, axis=-1, keepdims=True)
        expo = jnp.exp2((scores - top) * (scale * math.log2(math.e)))
        low = expo.astype(jnp.bfloat16)
        inverse = 1.0 / jnp.sum(expo, axis=-1, keepdims=True)
        prob_ref[0, rows, first:last] = low
        inverse_ref[0, rows, :] = jnp.broadcast_to(inverse, (tile, inverse_ref.shape[2]))
        if before is not None:
            mix(*before)
        before, scores = (index, low, inverse), following
    mix(*before)


def attend_back_kernel(
    scale, q_ref, k_ref, v_ref, prob_ref, mix_ref, mixg_ref, inverse_ref, out_ref, key_acc, value_acc
):
    length = q_ref.shape[1]
    quarter = length // 4
    key_acc[...] = jnp.zeros_like(key_acc)
    value_acc[...] = jnp.zeros_like(value_acc)
    mix_grad = (mixg_ref[...].astype(jnp.float32) * inverse_ref[0]).astype(jnp.bfloat16)
    centred = jnp.sum(mix_grad.astype(jnp.float32) * mix_ref[...].astype(jnp.float32), axis=-1, keepdims=True)
    ranges = key_ranges(length)

    def grads_of(index):
        first, last = ranges[index]
        return dot(mix_grad[index * quarter : (index + 1) * quarter], v_ref[0, first:last, :], NT)

    def spread(index, score_grads, low):
        first, last = ranges[index]
        rows = slice(index * quarter, (index + 1) * quarter)
        out_ref[0, rows, :] = (dot(score_grads, k_ref[0, first:last, :]) * scale).astype(jnp.bfloat16)
        key_acc[first:last, :] += dot(score_grads, q_ref[0, rows, :], TN)
        value_acc[first:last, :] += dot(low, mix_grad[rows], TN)

    grads, before = grads_of(0), None
    for index, (first, last) in enumerate(ranges):
        following = grads_of(index + 1) if index + 1 < len(ranges) else None
        rows = slice(index * quarter, (index + 1) * quarter)
        low = prob_ref[0, rows, first:last]
        score_grads = (low.astype(jnp.float32) * (grads - centred[rows])).astype(jnp.bfloat16)
        if before is not None:
            spread(*before)
        before, grads = (index, score_grads, low), following
    spread(*before)
    out_ref[1] = (key_acc[...] * scale).astype(jnp.bfloat16)
    out_ref[2] = value_acc[...].astype(jnp.bfloat16)


def project_back_kernel(order, me_ref, normed_ref, grad_ref, keep_ref, send_ref, sum_ref, stage_ref, sems):
    step = pl.program_id(0)
    stage_ref[step] = dot(normed_ref[...], grad_ref[0], TN).astype(jnp.bfloat16)
    for matrix in range(3):

        @pl.when(step == matrix)
        def _():
            stage = stage_ref.at[matrix]
            collect_matrix(me_ref[0], order, stage, matrix, keep_ref, send_ref, 0, sems.at[matrix])

    sum_ref[0] = jnp.broadcast_to(column_sum(grad_ref[0]), sum_ref.shape[1:])

    @pl.when(step == 2)
    def _():
        for matrix in range(3):
            stage = stage_ref.at[matrix]
            pltpu.make_async_copy(stage, stage, sems.at[matrix]).wait()


def place_matrix(me, order, sources, matrix, weight_ref, column, sem):
    depth = weight_ref.shape[1] >> len(order)
    width = sources[0].shape[-1]
    held = sources[0].shape[0]
    for position in range(len(sources) * held):
        owner = me ^ offset_of(order, position)
        rows = pl.ds(pl.multiple_of(owner * depth, depth), depth)
        pltpu.make_async_copy(
            sources[position // held].at[position % held, pl.ds(matrix * depth, depth), :],
            weight_ref.at[matrix, rows, pl.ds(column, width)],
            sem,
        ).start()


def collect_matrix(me, order, stage_ref, matrix, keep_ref, send_ref, base, sem):
    half = 1 << len(order) - 1
    depth = stage_ref.shape[0] >> len(order)
    for position in reversed(range(2 * half)):
        target = keep_ref if position < half else send_ref
        owner = me ^ offset_of(order, position)
        rows = pl.ds(pl.multiple_of(owner * depth, depth), depth)
        place = base + (position % half * 3 + matrix) * depth
        pltpu.make_async_copy(stage_ref.at[rows, :], target.at[pl.ds(place, depth), :], sem).start()


def feed_kernel(
    me_ref, x_own_ref, x_other_ref, cot_own_ref, cot_other_ref, mix0_ref, mix1_ref, column_ref, vec_ref, *refs
):
    sources = refs[:8]
    result_ref, result_other_ref, resg_ref, mixg_ref, sum_ref, keep_ref, send_ref, *refs = refs[8:]
    (
        w_ref, x_ref, cot_ref, mix_ref, hid_ref, act_ref, og_ref, pre_ref, res_ref, resid_ref, slope_ref,
        out_ref, resg_out, mixg_out, stage_ref, w_sem, in_sem, out_sem, g_sem,
    ) = refs
    me = me_ref[0]
    rank = me & 1
    half_rows, features = x_other_ref.shape
    width = features // 2
    places = [pl.multiple_of((half ^ rank) * half_rows, half_rows) for half in range(2)]
    rows = [pl.ds(place, half_rows) for place in places]

    def weights(matrix):
        for half in range(2):
            place_matrix(me, ORDERS[half], sources[4 * half : 4 * half + 4], matrix, w_ref, half * width, w_sem.at[matrix])

    def weights_here(matrix):
        pltpu.make_async_copy(w_ref.at[matrix], w_ref.at[matrix], w_sem.at[matrix]).wait()

    mix_in = [
        pltpu.make_async_copy(ref, mix_ref.at[:, pl.ds(half * width, width)], in_sem.at[half])
        for half, ref in enumerate((mix0_ref, mix1_ref))
    ]
    x_in = [
        pltpu.make_async_copy(ref, x_ref.at[half], in_sem.at[2 + half])
        for half, ref in enumerate((x_own_ref.at[rank], x_other_ref))
    ]
    cot_in = [
        pltpu.make_async_copy(ref, cot_ref.at[half], in_sem.at[4 + half])
        for half, ref in enumerate((cot_own_ref.at[rank], cot_other_ref))
    ]
    for copy in mix_in:
        copy.start()
    weights(0)
    x_in[0].start()
    x_in[1].start()
    weights(1)
    cot_in[0].start()
    cot_in[1].start()
    weights(2)
    sums = [jnp.zeros((1, features), jnp.float32)] * 5
    out_copies = []

    def attend_out(half):
        x_in[half].wait()
        resid_ref[half] = x_ref[half].astype(jnp.float32) + dot(mix_ref[rows[half], :], w_ref[0]) + vec_ref[6:7]

    def norm_two(half):
        normed, _ = normalize(resid_ref[half])
        hid_ref[half] = (normed * vec_ref[1:2] + vec_ref[3:4]).astype(jnp.bfloat16)

    def first(half):
        return dot(hid_ref[half], w_ref[1]) + vec_ref[7:8]

    def gelu(half, pre):
        square = pre * pre
        tanh = jnp.tanh(0.7978845608 * pre * (1.0 + 0.044715 * square))
        upper = 0.5 * (1.0 + tanh)
        act_ref[half] = (pre * upper).astype(jnp.bfloat16)
        slope_ref[half] = upper * (
            1.0 + pre * (1.0 - tanh) * (0.7978845608 + (3 * 0.044715 * 0.7978845608) * square)
        )

    def mask(half):
        cot_in[half].wait()
        live = (column_ref[rows[half], :] >= 0).astype(jnp.float32)
        og_ref[half] = (cot_ref[half].astype(jnp.float32) * live).astype(jnp.bfloat16)

    def second(half):
        result = resid_ref[half] + dot(act_ref[half], w_ref[2]) + vec_ref[8:9]
        out_ref[half] = result.astype(jnp.bfloat16)
        target = (result_ref.at[rank], result_other_ref)[half]
        out_copies.append(pltpu.make_async_copy(out_ref.at[half], target, out_sem.at[half]))
        out_copies[-1].start()

    def second_back(half):
        return dot(og_ref[half], w_ref[2], NT)

    def gelu_back(half, grad):
        pre_ref[half] = (grad * slope_ref[half]).astype(jnp.bfloat16)
        sums[3] = sums[3] + column_sum(pre_ref[half])
        sums[4] = sums[4] + column_sum(og_ref[half])

    def first_back(half):
        return dot(pre_ref[half], w_ref[1], NT)

    def norm_back(half, grad):
        normed, inverse = normalize(resid_ref[half])
        sums[0] = sums[0] + column_sum(grad * normed)
        sums[1] = sums[1] + column_sum(grad)
        scaled = grad * vec_ref[1:2]
        resg = og_ref[half].astype(jnp.float32) + inverse * (
            scaled
            - jnp.mean(scaled, axis=-1, keepdims=True)
            - normed * jnp.mean(scaled * normed, axis=-1, keepdims=True)
        )
        resg_out[half] = resg
        res_ref[rows[half], :] = resg.astype(jnp.bfloat16)
        sums[2] = sums[2] + column_sum(resg.astype(jnp.bfloat16))

    def out_back(half):
        mixg_out[half] = dot(res_ref[rows[half], :], w_ref[0], NT).astype(jnp.bfloat16)
        for source, target, number in (
            (resg_out.at[half], resg_ref.at[half], 2 + half), (mixg_out.at[half], mixg_ref.at[rows[half]], 4 + half)
        ):
            out_copies.append(pltpu.make_async_copy(source, target, out_sem.at[number]))
            out_copies[-1].start()

    def weight_grad(matrix, half):
        columns = slice(half * width, (half + 1) * width)
        if matrix == 0:
            total = dot(mix_ref[...], res_ref[:, columns], TN)
        else:
            left, right = ((hid_ref, pre_ref), (act_ref, og_ref))[matrix - 1]
            total = dot(left[0], right[0, :, columns], TN) + dot(left[1], right[1, :, columns], TN)
        stage = stage_ref.at[half, matrix]
        stage_ref[half, matrix] = total.astype(jnp.bfloat16)
        collect_matrix(
            me, ORDERS[half], stage, matrix, keep_ref, send_ref, half * keep_ref.shape[0] // 2, g_sem.at[half, matrix]
        )

    for copy in mix_in:
        copy.wait()
    weights_here(0)
    attend_out(0)
    attend_out(1)
    norm_two(0)
    weights_here(1)
    pre0 = first(0)
    norm_two(1)
    pre1 = first(1)
    gelu(0, pre0)
    mask(0)
    weights_here(2)
    second(0)
    grad0 = second_back(0)
    gelu(1, pre1)
    mask(1)
    second(1)
    grad1 = second_back(1)
    gelu_back(0, grad0)
    grad0 = first_back(0)
    gelu_back(1, grad1)
    weight_grad(2, 0)
    grad1 = first_back(1)
    norm_back(0, grad0)
    weight_grad(2, 1)
    out_back(0)
    weight_grad(1, 0)
    norm_back(1, grad1)
    weight_grad(1, 1)
    out_back(1)
    weight_grad(0, 0)
    weight_grad(0, 1)
    sum_ref[...] = jnp.zeros_like(sum_ref)
    for row, value in enumerate(sums):
        sum_ref[row : row + 1] = value
    for copy in out_copies:
        copy.wait()
    for half in range(2):
        for matrix in range(3):
            stage = stage_ref.at[half, matrix]
            pltpu.make_async_copy(stage, stage, g_sem.at[half, matrix]).wait()


def finish_kernel(me_ref, x_ref, resg_ref, grad0_ref, grad1_ref, w0_ref, w1_ref, vec_ref, out_ref, sum_ref, acc_ref):
    step = pl.program_id(0)
    term = dot(grad0_ref[0], w0_ref[0], NT) + dot(grad1_ref[0], w1_ref[0], NT)

    @pl.when(step == 0)
    def _():
        acc_ref[...] = term

    @pl.when(step == 1)
    def _():
        acc_ref[...] += term

    @pl.when(step == 2)
    def _():
        normed_grad = acc_ref[...] + term
        normed, inverse = normalize(x_ref[...].reshape(acc_ref.shape).astype(jnp.float32))
        sum_ref[...] = jnp.zeros_like(sum_ref)
        sum_ref[0:1] = column_sum(normed_grad * normed)
        sum_ref[1:2] = column_sum(normed_grad)
        scaled = normed_grad * vec_ref[0:1]
        total = resg_ref[0] + inverse * (
            scaled
            - jnp.mean(scaled, axis=-1, keepdims=True)
            - normed * jnp.mean(scaled * normed, axis=-1, keepdims=True)
        )
        out_ref[...] = total.reshape(out_ref.shape).astype(out_ref.dtype)


def double_first_kernel(me_ref, own_ref, own_vec_ref, got_ref, got_vec_ref, out_ref):
    matrices, depth, features = own_ref.shape
    width = features // 2
    base = matrices * depth
    out_ref[:, :, base:, :] = jnp.zeros_like(out_ref[:, :, base:, :])
    for block, (part, vectors) in enumerate(((own_ref, own_vec_ref), (got_ref, got_vec_ref))):
        for half in range(2):
            for matrix in range(matrices):
                rows = slice(matrix * depth, (matrix + 1) * depth)
                out_ref[block, half, rows, :] = part[matrix, :, half * width : (half + 1) * width]
        out_ref[block, 0, base : base + vectors.shape[0], 0:depth] = vectors[...]


def pack_next_kernel(me_ref, output_ref, hidden_ref, out_ref, sems):
    depth, features = output_ref.shape
    width = features // 2
    copies = []
    for half in range(2):
        columns = pl.ds(half * width, width)
        sources = [output_ref.at[:, columns]] + [hidden_ref.at[matrix, :, columns] for matrix in range(2)]
        for matrix, source in enumerate(sources):
            target = out_ref.at[0, half, pl.ds(matrix * depth, depth), :]
            copies.append(pltpu.make_async_copy(source, target, sems.at[len(copies)]))
    for copy in copies:
        copy.start()
    for copy in copies:
        copy.wait()


def join_kernel(moves, me_ref, *refs):
    for source, source_index, target, target_index in moves:
        refs[target][target_index] = refs[source][source_index]


def join_out_kernel(moves, me_ref, *refs):
    *refs, sems = refs
    copies = [
        pltpu.make_async_copy(refs[source].at[source_index], refs[target].at[target_index], sems.at[number])
        for number, (source, source_index, target, target_index) in enumerate(moves)
    ]
    for copy in copies:
        copy.start()
    for copy in copies:
        copy.wait()


def select_kernel(me_ref, rows_ref, *refs):
    row = 0
    for out_ref in refs[:-1]:
        out_ref[...] = rows_ref[0, row : row + out_ref.shape[0], :]
        row += out_ref.shape[0]
    refs[-1][...] = jnp.zeros_like(refs[-1])


def total_of(refs, width):
    total = None
    for ref in refs:
        term = ref[...].astype(jnp.float32).reshape(-1, width)
        total = term if total is None else total + term
    return total


def combine_kernel(sums, me_ref, *refs):
    for first, last, output, row in sums:
        out_ref = refs[output]
        total = total_of(refs[first:last], out_ref.shape[-1])
        out_ref[row : row + total.shape[0], :] = total.astype(out_ref.dtype)


def final_kernel(inputs, me_ref, *refs):
    outs = refs[2 * inputs :]
    depth, features = outs[0].shape[1:]
    width = features // 2
    for half in range(2):
        total = total_of(refs[half * inputs : (half + 1) * inputs], width)
        row = 0
        for out_ref in outs:
            matrices = out_ref.shape[0]
            piece = total[row : row + matrices * depth].reshape(matrices, depth, width)
            out_ref[:, :, half * width : (half + 1) * width] = piece
            row += matrices * depth


def final_vector_kernel(inputs, vectors, me_ref, *refs):
    blocks, terms = refs[: 2 * inputs], refs[2 * inputs : 2 * inputs + vectors]
    out_ref, gain_ref, bias_ref = refs[2 * inputs + vectors :]
    final_kernel(inputs, me_ref, *blocks, out_ref)
    picked = own_columns(me_ref, terms, gain_ref.shape[1])
    gains = gain_ref.shape[0]
    gain_ref[...] = picked[0:gains]
    bias_ref[...] = picked[gains : gains + bias_ref.shape[0]]


def own_columns(me_ref, terms, depth):
    rows = terms[0].shape[0] // 2
    width = terms[0].shape[-1]
    total = total_of(terms, width)
    lane = lax.broadcasted_iota(jnp.int32, (width, depth), 0)
    column = lax.broadcasted_iota(jnp.int32, (width, depth), 1)
    place = me_ref[0] * depth
    picked = None
    for half in range(2):
        choose = (lane + half * width == column + place).astype(jnp.float32)
        part = lax.dot_general(
            total[half * rows : (half + 1) * rows], choose, NN, precision=lax.Precision.HIGHEST,
            preferred_element_type=jnp.float32,
        )
        picked = part if picked is None else picked + part
    return picked


def vector_pack_kernel(me_ref, feed_ref, last0_ref, last1_ref, s0_ref, s1_ref, out_ref, row_ref):
    width = out_ref.shape[-1]
    row_ref[...] = jnp.zeros_like(row_ref)
    row_ref[0:1] = last0_ref[0:1] + last1_ref[0:1]
    row_ref[1:2] = feed_ref[0:1]
    row_ref[2:3] = last0_ref[1:2] + last1_ref[1:2]
    row_ref[3:4] = feed_ref[1:2]
    for half, sums in enumerate((s0_ref, s1_ref)):
        row_ref[4:5, half * width : (half + 1) * width] = sums[0, 0:1]
        row_ref[5:6, half * width : (half + 1) * width] = sums[2, 0:1]
    row_ref[6:9] = feed_ref[2:5]
    for half in range(2):
        out_ref[half * 16 : (half + 1) * 16, :] = row_ref[:, half * width : (half + 1) * width].astype(jnp.bfloat16)


ANY = pl.BlockSpec(memory_space=pl.ANY)
VMEM = pl.BlockSpec(memory_space=pltpu.VMEM)
HBM = pl.BlockSpec(memory_space=pltpu.HBM)
SMALL_LIMIT = 24 << 20


def call(kernel, me, grid, operands, out_specs, out_shape, scratch=(), flops=1e6, moved=1e6, after=(), limit=VMEM_LIMIT):
    taken = len(operands) + 1
    after = list(after)
    ordered = ANY if limit == SMALL_LIMIT else HBM

    def body(*refs):
        kernel(*refs[:taken], *refs[taken + len(after) :])

    return pl.pallas_call(
        body,
        grid_spec=pltpu.PrefetchScalarGridSpec(
            num_scalar_prefetch=1,
            grid=grid,
            in_specs=[spec for _, spec in operands] + [ordered] * len(after),
            out_specs=out_specs,
            scratch_shapes=list(scratch),
        ),
        out_shape=out_shape,
        compiler_params=pltpu.CompilerParams(
            dimension_semantics=("arbitrary",) * len(grid), vmem_limit_bytes=limit
        ),
        cost_estimate=pl.CostEstimate(flops=int(flops), bytes_accessed=int(moved), transcendentals=0),
    )(me, *[array for array, _ in operands], *after)


def struct(shape, dtype=jnp.bfloat16):
    return jax.ShapeDtypeStruct(shape, dtype)


def whole(shape):
    return pl.BlockSpec(shape, lambda *_: (0,) * len(shape))


def join(me, arrays, moves, shapes, after=(), kind="local"):
    moves = [(i, source, len(arrays) + o, target) for i, source, o, target in moves]
    place = whole if kind == "far" else lambda shape: VMEM
    kernel = functools.partial(join_out_kernel if kind == "out" else join_kernel, moves)
    return call(
        kernel, me, (1,), [(a, place(a.shape)) for a in arrays],
        [HBM if kind == "out" else place(s) for s in shapes], [struct(s) for s in shapes],
        [pltpu.SemaphoreType.DMA((len(moves),))] if kind == "out" else [], after=after,
        limit=VMEM_LIMIT if kind == "far" else SMALL_LIMIT,
    )


def part(array, start, size, tall):
    return array, pl.BlockSpec((size * tall, array.shape[-1]), lambda i, me: (start // size, 0))


def combine(me, outputs, after=()):
    operands, sums, shapes = [], [], []
    count = sum(len(terms) for group in outputs for terms in group)
    for number, group in enumerate(outputs):
        row = 0
        for terms in group:
            first = len(operands)
            operands.extend(terms)
            sums.append((first, len(operands), count + number, row))
            row += terms[0][1].block_shape[0]
        shapes.append((row, group[0][0][0].shape[-1]))
    return call(
        functools.partial(combine_kernel, sums), me, (1,), operands, [whole(s) for s in shapes],
        [struct(s) for s in shapes], after=after,
    )


def final(me, halves, depth, features, counts, vectors=()):
    shapes = [(matrices, depth, features) for matrices in counts]
    kernel = functools.partial(final_kernel, len(halves[0]))
    if vectors:
        kernel = functools.partial(final_vector_kernel, len(halves[0]), len(vectors))
        shapes.extend([(2, depth), (7, depth)])
    return call(
        kernel, me, (1,), halves[0] + halves[1] + list(vectors), [whole(s) for s in shapes],
        [struct(s, jnp.float32) for s in shapes],
    )


def whole_sequence(
    latents, segments, attention_weights, output_weight, hidden_weights, gains, biases, cotangent
):
    half_rows, features = latents.shape[2:]
    length = 2 * half_rows
    head_size = features // HEADS
    scale = 1.0 / math.sqrt(head_size)
    width = features // 2
    count = 1 << len(ORDERS[0])
    depth = features // count
    rank = lax.axis_index("row")
    device = (lax.axis_index("seq") * 2 + rank).astype(jnp.int32)
    me = device.reshape(1)
    bf16, f32 = jnp.bfloat16, jnp.float32
    dense = 2.0 * length * features * features
    tall = 3 * depth
    vector_rows = gains.shape[0] + biases.shape[0]
    padded = tall + 16

    def move(array, mask):
        return shift(array, mask, count)

    def double(held, got, after=()):
        return join(me, [held, got], [(0, 0, 0, 0), (1, 0, 0, 1)], [(2,) + held.shape[1:]], after)[0]

    def split(held, got, rows, after=(), kind="local"):
        moves, shapes = [], []
        for half in range(2):
            for source in range(2):
                for block in range(2):
                    moves.append((source, (block, half, pl.ds(0, rows[half])), half, 2 * source + block))
            shapes.append((4, rows[half], width))
        return join(me, [held, got], moves, shapes, after, kind)

    def append(held, got, after=(), kind="out"):
        moves, shapes = [], []
        for half in range(2):
            for source in range(2):
                moves.append((2 * half + source, pl.ds(0, 4), half, pl.ds(4 * source, 4)))
            shapes.append((8,) + held[half].shape[1:])
        return join(me, [held[0], got[0], held[1], got[1]], moves, shapes, after, kind)

    z_far, y, z_near, x, core = 16, 1, 8, 4, 2
    def pack(kernel, arrays, rows, scratch, after=()):
        return call(
            kernel, me, (1,), [(a, HBM) for a in arrays], VMEM, struct((1, 2, rows, width)), scratch, after=after,
            limit=SMALL_LIMIT,
        )

    latents_flat = latents[:, 0]
    cotangent_flat = cotangent[:, 0]

    def select(array, parts, after):
        shapes = [(half_rows * share // sum(parts), features) for share in parts]
        return call(
            select_kernel, me, (1,),
            [(array, pl.BlockSpec((1, half_rows, features), lambda i, me: (1 - (me[0] & 1), 0, 0)))],
            [whole(shape) for shape in shapes] + [VMEM], [struct(shape) for shape in shapes] + [struct((8, 128), f32)],
            after=after, limit=SMALL_LIMIT,
        )

    sems = lambda number: pltpu.SemaphoreType.DMA((number,))
    vectors_own = jnp.concatenate([gains, biases], axis=0)
    a1_got = (move(attention_weights, z_far), move(vectors_own, z_far))
    *x_send, x_token = select(latents_flat, (5, 3), [])
    a2 = call(
        double_first_kernel, me, (1,),
        [(a, VMEM) for a in (attention_weights, vectors_own, *a1_got)], VMEM, struct((2, 2, padded, width)),
        after=[x_token], limit=SMALL_LIMIT,
    )
    f1 = pack(pack_next_kernel, [output_weight, hidden_weights], tall, [sems(6)], [a2])
    a4 = split(a2, move(a2, y), (padded, tall), [f1])
    x_first = move(x_send[0], y)
    cot_send, cot_token = select(cotangent_flat, (1,), a4)
    f2 = double(f1, move(f1, z_far), [a4[0], cot_token])
    a8 = append(a4, (move(a4[0], z_near), move(a4[1], x)), [f2, x_first])
    a_core = [move(a, core) for a in a8]
    x_second = move(x_send[1], y)
    f4 = split(f2, move(f2, y), (tall, tall), a8, "out")
    a_far = join(
        me, [move(a8[0], x), move(a8[1], z_near)], [(h, pl.ds(0, 8), h, pl.ds(0, 8)) for h in range(2)],
        [a.shape for a in a8], [f4[0], x_second], "out",
    )
    a_far_core = [move(a, core) for a in a_far]
    attn_sources = [[a8[h], a_far[h], a_core[h], a_far_core[h]] for h in range(2)]

    segment_row = segments
    segment_column = lax.dynamic_index_in_dim(segments[:, 0], rank, 0, keepdims=False)[:, None]

    own = pl.BlockSpec((1, half_rows, features), lambda i, me: (me[0] & 1, 0, 0))
    local = pl.BlockSpec((half_rows, features), lambda i, me: (i ^ (me[0] & 1), 0))
    local3 = pl.BlockSpec((3, half_rows, width), lambda i, me: (0, i ^ (me[0] & 1), 0))
    rows_spec = whole((half_rows, features))
    w_scratch = pltpu.VMEM((3, features, width), bf16)
    w_struct = struct((3, features, width))
    normed_low, qkv0, vec, x_other, weight0 = call(
        project_first_kernel, me, (2,),
        [(latents_flat, own)] + [(a, whole(a.shape)) for a in (x_first, x_second)] + [(a, ANY) for a in attn_sources[0]],
        [local, local3, whole((16, features)), rows_spec, ANY],
        [struct((length, features)), struct((3, length, width)), struct((16, features), f32),
         struct((half_rows, features)), w_struct],
        [w_scratch, pltpu.VMEM((count, 16, 128), bf16), pltpu.SemaphoreType.DMA(()), pltpu.SemaphoreType.DMA(())],
        1.5 * dense, 16e6, f4,
    )
    vec_op = (vec, whole((16, features)))
    cot_other = move(cot_send, y)
    f8 = append(f4, (move(f4[0], z_near), move(f4[1], x)), [vec], "far")
    f_core = [move(a, core) for a in f8]
    f_far = (move(f8[0], x), move(f8[1], z_near))
    qkv1, weight1 = call(
        project_next_kernel, me, (2,),
        [(normed_low, pl.BlockSpec((half_rows, features), lambda i, me: (i, 0))), vec_op]
        + [(a, ANY) for a in attn_sources[1]],
        [pl.BlockSpec((3, half_rows, width), lambda i, me: (0, i, 0)), ANY], [struct((3, length, width)), w_struct],
        [w_scratch, pltpu.SemaphoreType.DMA(())], 1.5 * dense, 8e6, f8,
    )

    heads = width // head_size
    head_specs = [
        pl.BlockSpec((1, length, head_size), functools.partial(lambda c, h, me: (c, 0, h), c)) for c in range(3)
    ]
    column_block = pl.BlockSpec((length, head_size), lambda h, me: (0, h))
    prob_block = pl.BlockSpec((1, length, length), lambda h, me: (h, 0, 0))
    inverse_block = pl.BlockSpec((1, length, head_size), lambda h, me: (h, 0, 0))
    segment_spec = pl.BlockSpec((1, 1, length), lambda h, me: (me[0] & 1, 0, 0))

    def attend(qkv, after):
        return call(
            lambda me_ref, *refs: attend_kernel(scale, *refs), me, (heads,),
            [(qkv, s) for s in head_specs] + [(segment_column, whole((length, 1))), (segment_row, segment_spec)],
            [column_block, prob_block, inverse_block],
            [struct((length, width)), struct((heads, length, length)), struct((heads, length, head_size), f32)], [],
            4 * dense, 30e6, after,
        )

    mix0, prob0, inverse0 = attend(qkv0, [qkv1])
    f_far_core = [move(a, core) for a in f_far]
    feed_sources = [[f8[h], f_far[h], f_core[h], f_far_core[h]] for h in range(2)]
    mix1, prob1, inverse1 = attend(qkv1, [mix0])

    keeps = [struct((count * tall, width))] * 2
    low = lambda *shape: pltpu.VMEM(shape, bf16)
    dma = lambda *shape: pltpu.SemaphoreType.DMA(shape)
    local_rows = pltpu.VMEM((2, half_rows, features), f32)
    result_own, result_other, residual_grad, mix_grad, feed_sums, fk, fs = call(
        feed_kernel, me, (1,),
        [(a, HBM) for a in (latents_flat, x_other, cotangent_flat, cot_other, mix0, mix1)]
        + [(segment_column, whole((length, 1))), vec_op] + [(a, ANY) for a in feed_sources[0] + feed_sources[1]],
        [HBM] * 4 + [whole((8, features))] + [ANY] * 2,
        [struct((2, half_rows, features)), struct((half_rows, features)), struct((2, half_rows, features), f32),
         struct((length, features)), struct((8, features), f32)] + keeps,
        [low(3, features, features), low(2, half_rows, features), low(2, half_rows, features), low(length, features)]
        + [low(2, half_rows, features)] * 4 + [low(length, features), local_rows, local_rows]
        + [low(2, half_rows, features), local_rows, low(2, half_rows, features), low(2, 3, features, width)]
        + [dma(3), dma(6), dma(6), dma(2, 3)],
        9 * dense, 30e6,
    )
    f_c = move(fs, core)
    result_back = move(result_other, y)

    def attend_back(qkv, prob, mix, inverse, half, after):
        return call(
            lambda me_ref, *refs: attend_back_kernel(scale, *refs), me, (heads,),
            [(qkv, s) for s in head_specs] + [(prob, prob_block), (mix, column_block),
             (mix_grad, pl.BlockSpec((length, head_size), lambda h, me: (0, h + half * heads))), (inverse, inverse_block)],
            pl.BlockSpec((3, length, head_size), lambda h, me: (0, 0, h)), struct((3, length, width)),
            [pltpu.VMEM((length, head_size), f32)] * 2, 8 * dense, 30e6, after,
        )

    def project_back(grad, order, after):
        return call(
            functools.partial(project_back_kernel, order), me, (3,),
            [(normed_low, whole((length, features))), (grad, pl.BlockSpec((1, length, width), lambda i, me: (i, 0, 0)))],
            [ANY, ANY, pl.BlockSpec((1, 8, width), lambda i, me: (i, 0, 0))],
            [struct((count // 2 * tall, width))] * 2 + [struct((3, 8, width), f32)],
            [w_scratch, dma(3)], 1.5 * dense, 8e6, after,
        )

    def finish(rows, index, flip, out_spec, out_struct, after):
        block = lambda me: (me[0] & 1) ^ flip
        grad_spec = pl.BlockSpec((1, half_rows, width), lambda i, me: (i, block(me), 0))
        w_spec = pl.BlockSpec((1, features, width), lambda i, me: (i, 0, 0))
        return call(
            finish_kernel, me, (3,),
            [rows, (residual_grad, pl.BlockSpec((1, half_rows, features), lambda i, me: (index, 0, 0))),
             (qkv_grad0, grad_spec), (qkv_grad1, grad_spec), (weight0, w_spec), (weight1, w_spec), vec_op],
            [out_spec, whole((8, features))], [out_struct, struct((8, features), f32)],
            [pltpu.VMEM((half_rows, features), f32)], 8 * dense, 20e6, after,
        )

    half_count = count // 2
    blocks = lambda array, start, size: part(array, start, size, tall)
    vector_part = lambda array, row: (array, pl.BlockSpec((32, width), lambda i, me: (row // 32, 0)))
    feed_first = lambda start, size, h: [blocks(a, h * half_count + start, size) for a in (fk, f_c)]
    qkv_grad0 = attend_back(qkv0, prob0, mix0, inverse0, 0, [])
    fs0, fs1 = combine(me, [[feed_first(8, 8, 0)], [feed_first(8, 8, 1)]], [qkv_grad0])
    f_s2 = (move(fs0, x), move(fs1, z_near))
    ak0, as0, sums0 = project_back(qkv_grad0, ORDERS[0], [fs0, fs1])
    a0_c = move(as0, core)
    qkv_grad1 = attend_back(qkv1, prob1, mix1, inverse1, 1, [ak0])
    terms = [feed_first(4, 4, h) + [blocks(f_s2[h], 4, 4)] for h in range(2)]
    ft0, ft1, at0 = combine(me, [[terms[0]], [terms[1]], [[blocks(ak0, 8, 8), blocks(a0_c, 8, 8)]]], [qkv_grad1])
    f_s3 = (move(ft0, z_near), move(ft1, x))
    a0_s2 = move(at0, x)
    ak1, as1, sums1 = project_back(qkv_grad1, ORDERS[1], [ft0, ft1, at0, result_back])
    a1_c = move(as1, core)
    feed_terms = lambda start, size: [
        feed_first(start, size, h) + [blocks(f_s2[h], start, size), blocks(f_s3[h], start, size)] for h in range(2)
    ]
    fu, = combine(me, [feed_terms(2, 2)], [ak1])
    f_y = move(fu, y)
    latent_other, sums_other = finish((x_other, rows_spec), 1, 1, rows_spec, struct((half_rows, features)), [fu])
    latent_back = move(latent_other, y)
    at1, = combine(me, [[[blocks(ak1, 8, 8), blocks(a1_c, 8, 8)]]], [latent_other])
    a1_s2 = move(at1, z_near)
    latent_out, sums_own = finish((latents_flat, own), 0, 0, own, struct((2, half_rows, features), f32), [at1])
    vectors = call(
        vector_pack_kernel, me, (1,),
        [(a, whole((8, features))) for a in (feed_sums, sums_own, sums_other)]
        + [(a, whole((3, 8, width))) for a in (sums0, sums1)],
        whole((32, width)), struct((32, width)), [pltpu.VMEM((16, features), f32)], after=[f_y],
    )
    vectors_c = move(vectors, core)
    vector_terms = [vector_part(vectors, 0), vector_part(vectors_c, 0)]
    vectors_z = move(combine(me, [[vector_terms]])[0], z_near)
    vector_terms = vector_terms + [vector_part(vectors_z, 0)]
    au0, au1 = combine(
        me,
        [
            [[blocks(ak0, 4, 4), blocks(a0_c, 4, 4), blocks(a0_s2, 4, 4)]],
            [[blocks(ak1, 4, 4), blocks(a1_c, 4, 4), blocks(a1_s2, 4, 4)], vector_terms],
        ],
    )
    a0_s3 = move(au0, z_near)
    a1_s3 = move(au1, x)
    vector_terms = vector_terms + [vector_part(a1_s3, 4 * tall)]
    attn_terms = lambda start, size: [
        [blocks(a, start, size) for a in (ak0, a0_c, a0_s2, a0_s3)],
        [blocks(a, start, size) for a in (ak1, a1_c, a1_s2, a1_s3)],
    ]
    av, fv = combine(
        me,
        [
            attn_terms(2, 2) + [vector_terms],
            [t + [blocks(f_y, 2 * h + 1, 1)] for h, t in enumerate(feed_terms(1, 1))],
        ],
    )
    a_y = move(av, y)
    f_z = move(fv, z_far)
    vector_terms = vector_terms + [vector_part(a_y, 4 * tall)]
    aw, = combine(me, [[t + [blocks(a_y, 2 * h + 1, 1)] for h, t in enumerate(attn_terms(1, 1))] + [vector_terms]])
    a_z = move(aw, z_far)
    vector_terms = vector_terms + [vector_part(a_z, 2 * tall)]
    output_grad, hidden_grads = final(
        me, [t + [blocks(f_y, 2 * h, 1), blocks(f_z, h, 1)] for h, t in enumerate(feed_terms(0, 1))], depth, features,
        (1, 2),
    )
    attn_out, gain_grads, bias_grads = final(
        me, [t + [blocks(a_y, 2 * h, 1), blocks(a_z, h, 1)] for h, t in enumerate(attn_terms(0, 1))], depth, features,
        (3,), vector_terms,
    )

    latent_grads = lax.dynamic_update_slice_in_dim(latent_out, latent_back.astype(f32)[None], 1 - rank, 0)
    activations = lax.dynamic_update_slice_in_dim(result_own, result_back[None], 1 - rank, 0)
    return (
        activations[:, None],
        latent_grads[:, None],
        attn_out,
        output_grad[0],
        hidden_grads,
        gain_grads,
        bias_grads,
    )


def layer_norm(vector, gain_row, offset):
    centre = vector - jnp.mean(vector, axis=-1, keepdims=True)
    spread = jnp.mean(centre * centre, axis=-1, keepdims=True)
    return centre * lax.rsqrt(spread + EPSILON) * gain_row + offset


def on_device(
    latents, segments, attention_weights, output_weight, hidden_weights, gains, biases, cotangent
):
    micro_count = latents.shape[0]
    row_count = latents.shape[2]
    features = latents.shape[3]
    head_size = features // HEADS
    score_scale = 1.0 / math.sqrt(head_size)
    own_rank = lax.axis_index("row")
    attn_total = jnp.zeros((3, features, features), jnp.float32)
    output_total = jnp.zeros((features, features), jnp.float32)
    hidden_total = jnp.zeros((2, features, features), jnp.float32)
    gain_total = jnp.zeros((2, features), jnp.float32)
    bias_total = jnp.zeros((7, features), jnp.float32)
    outputs = []
    input_grads = []
    for micro_index in range(micro_count):
        gathered = (
            lax.all_gather(attention_weights, ("seq", "row"), axis=1, tiled=True),
            lax.all_gather(output_weight, ("seq", "row"), axis=0, tiled=True),
            lax.all_gather(hidden_weights, ("seq", "row"), axis=1, tiled=True),
            lax.all_gather(gains, ("seq", "row"), axis=1, tiled=True),
            lax.all_gather(biases, ("seq", "row"), axis=1, tiled=True),
        )
        attention_full, output_full, hidden_full, gain_full, bias_full = gathered
        gain_values = gain_full.astype(jnp.float32)
        bias_values = bias_full.astype(jnp.float32)
        inputs = latents[micro_index, 0].astype(jnp.float32)
        segment_all = segments[micro_index, 0]
        segment_own = lax.dynamic_slice_in_dim(segment_all, own_rank * row_count, row_count)
        normed_one, norm_one_pull = jax.vjp(layer_norm, inputs, gain_values[0], bias_values[0])
        normed_low = normed_one.astype(jnp.bfloat16)
        projected = jnp.einsum(
            "rd,cde->cre", normed_low, attention_full, preferred_element_type=jnp.float32
        )
        queries = (projected[0] + bias_values[2]).astype(jnp.bfloat16)
        own_keys = projected[1].astype(jnp.bfloat16)
        own_values = (projected[2] + bias_values[3]).astype(jnp.bfloat16)
        all_keys, all_values = (
            lax.all_gather(own_keys, "row", axis=0, tiled=True),
            lax.all_gather(own_values, "row", axis=0, tiled=True),
        )
        length = all_keys.shape[0]
        query_heads = queries.reshape(row_count, HEADS, head_size)
        key_heads = all_keys.reshape(length, HEADS, head_size)
        value_heads = all_values.reshape(length, HEADS, head_size)
        same_set = (segment_own[:, None] == segment_all[None, :])[None]
        raw_scores = (
            jnp.einsum("qhd,khd->hqk", query_heads, key_heads, preferred_element_type=jnp.float32)
            * score_scale
        )
        scores = jnp.where(same_set, raw_scores, -1e30)
        row_max = jnp.max(scores, axis=-1, keepdims=True)
        log_total = row_max + jnp.log(jnp.sum(jnp.exp(scores - row_max), axis=-1, keepdims=True))
        weights_low = jnp.exp(scores - log_total).astype(jnp.bfloat16)
        mixture = jnp.einsum(
            "hqk,khd->qhd", weights_low, value_heads, preferred_element_type=jnp.float32
        )
        mixture = mixture.reshape(row_count, features).astype(jnp.bfloat16)
        attended = (
            jnp.dot(mixture, output_full, preferred_element_type=jnp.float32) + bias_values[4]
        )
        residual_one = inputs + attended
        normed_two, norm_two_pull = jax.vjp(
            layer_norm, residual_one, gain_values[1], bias_values[1]
        )
        hidden_low = normed_two.astype(jnp.bfloat16)
        hidden_pre = (
            jnp.dot(hidden_low, hidden_full[0], preferred_element_type=jnp.float32) + bias_values[5]
        )
        activated, gelu_pull = jax.vjp(jax.nn.gelu, hidden_pre)
        active_low = activated.astype(jnp.bfloat16)
        result = residual_one + (
            jnp.dot(active_low, hidden_full[1], preferred_element_type=jnp.float32) + bias_values[6]
        )
        outputs.append(result.astype(jnp.bfloat16))
        live_rows = (segment_own >= 0).astype(jnp.bfloat16)[:, None]
        out_grad = cotangent[micro_index, 0] * live_rows
        out_grad_wide = out_grad.astype(jnp.float32)
        active_grad = jnp.dot(out_grad, hidden_full[1].T, preferred_element_type=jnp.float32)
        pre_grad = gelu_pull(active_grad)[0].astype(jnp.bfloat16)
        normed_two_grad = jnp.dot(pre_grad, hidden_full[0].T, preferred_element_type=jnp.float32)
        residual_part, gain_two, offset_two = norm_two_pull(normed_two_grad)
        residual_grad = out_grad_wide + residual_part
        residual_low = residual_grad.astype(jnp.bfloat16)
        mixture_grad = jnp.dot(residual_low, output_full.T, preferred_element_type=jnp.float32)
        mixture_grad = mixture_grad.astype(jnp.bfloat16).reshape(row_count, HEADS, head_size)
        raw_again = (
            jnp.einsum("qhd,khd->hqk", query_heads, key_heads, preferred_element_type=jnp.float32)
            * score_scale
        )
        weights_wide = jnp.exp(jnp.where(same_set, raw_again, -1e30) - log_total)
        weight_grads = jnp.einsum(
            "qhd,khd->hqk", mixture_grad, value_heads, preferred_element_type=jnp.float32
        )
        centred = jnp.sum(weights_wide * weight_grads, axis=-1, keepdims=True)
        score_grads = (weights_wide * (weight_grads - centred)).astype(jnp.bfloat16)
        query_grad = (
            jnp.einsum("hqk,khd->qhd", score_grads, key_heads, preferred_element_type=jnp.float32)
            * score_scale
        )
        query_grad = query_grad.astype(jnp.bfloat16).reshape(row_count, features)
        weights_again = weights_wide.astype(jnp.bfloat16)
        key_part = (
            jnp.einsum("hqk,qhd->khd", score_grads, query_heads, preferred_element_type=jnp.float32)
            * score_scale
        )
        value_part = jnp.einsum(
            "hqk,qhd->khd", weights_again, mixture_grad, preferred_element_type=jnp.float32
        )
        key_grad, value_grad = (
            lax.psum_scatter(
                key_part.reshape(length, features).astype(jnp.bfloat16),
                "row",
                scatter_dimension=0,
                tiled=True,
            ).astype(jnp.float32),
            lax.psum_scatter(
                value_part.reshape(length, features).astype(jnp.bfloat16),
                "row",
                scatter_dimension=0,
                tiled=True,
            ).astype(jnp.float32),
        )
        key_low = key_grad.astype(jnp.bfloat16)
        value_low = value_grad.astype(jnp.bfloat16)
        projection_grads = jnp.stack([query_grad, key_low, value_low])
        attn_total = attn_total + jnp.einsum(
            "rd,cre->cde", normed_low, projection_grads, preferred_element_type=jnp.float32
        )
        output_total = output_total + jnp.dot(
            mixture.T, residual_low, preferred_element_type=jnp.float32
        )
        hidden_total = hidden_total + jnp.stack(
            [
                jnp.dot(hidden_low.T, pre_grad, preferred_element_type=jnp.float32),
                jnp.dot(active_low.T, out_grad, preferred_element_type=jnp.float32),
            ]
        )
        normed_one_grad = jnp.einsum(
            "cre,cde->rd", projection_grads, attention_full, preferred_element_type=jnp.float32
        )
        input_part, gain_one, offset_one = norm_one_pull(normed_one_grad)
        input_grads.append(residual_grad + input_part)
        gain_total = gain_total + jnp.stack([gain_one, gain_two])
        bias_total = bias_total + jnp.stack(
            [
                offset_one,
                offset_two,
                jnp.sum(query_grad.astype(jnp.float32), axis=0),
                jnp.sum(value_low.astype(jnp.float32), axis=0),
                jnp.sum(residual_low.astype(jnp.float32), axis=0),
                jnp.sum(pre_grad.astype(jnp.float32), axis=0),
                jnp.sum(out_grad_wide, axis=0),
            ]
        )
    attn_grads, output_grads, hidden_grads, gain_grads, bias_grads = (
        lax.psum_scatter(attn_total, ("seq", "row"), scatter_dimension=1, tiled=True),
        lax.psum_scatter(output_total, ("seq", "row"), scatter_dimension=0, tiled=True),
        lax.psum_scatter(hidden_total, ("seq", "row"), scatter_dimension=1, tiled=True),
        lax.psum_scatter(gain_total, ("seq", "row"), scatter_dimension=1, tiled=True),
        lax.psum_scatter(bias_total, ("seq", "row"), scatter_dimension=1, tiled=True),
    )
    return (
        jnp.stack(outputs)[:, None],
        jnp.stack(input_grads)[:, None],
        attn_grads,
        output_grads,
        hidden_grads,
        gain_grads,
        bias_grads,
    )


def solution(mesh):
    def on_mesh(latents, *rest):
        shares_pair = mesh.shape["row"] == latents.shape[0] == 2
        fits = mesh.size == 1 << len(ORDERS[0]) and latents.shape[1] == mesh.shape["seq"]
        return shard_over(whole_sequence if shares_pair and fits else on_device)(latents, *rest)

    def shard_over(function):
        return jax.shard_map(
            function,
            mesh=mesh,
            in_specs=(
                P(None, "seq", "row", None),
                P(None, "seq", None),
                P(None, ("seq", "row"), None),
                P(("seq", "row"), None),
                P(None, ("seq", "row"), None),
                P(None, ("seq", "row")),
                P(None, ("seq", "row")),
                P(None, "seq", "row", None),
            ),
            out_specs=(
                P(None, "seq", "row", None),
                P(None, "seq", "row", None),
                P(None, ("seq", "row"), None),
                P(("seq", "row"), None),
                P(None, ("seq", "row"), None),
                P(None, ("seq", "row")),
                P(None, ("seq", "row")),
            ),
            check_vma=False,
        )

    return on_mesh
```

```python
import functools
import math

import jax
import jax.numpy as jnp
from jax import lax
from jax.experimental import pallas as pl
from jax.experimental.pallas import tpu as pltpu
from jax.sharding import PartitionSpec as P

HEADS = 8
EPSILON = 1e-05
AXES = ("seq", "row")
VMEM_LIMIT = 64 << 20
STEPS = 2
NN = (((1,), (0,)), ((), ()))
NT = (((1,), (1,)), ((), ()))
TN = (((0,), (0,)), ((), ()))
ORDERS = ((16, 1, 8, 4, 2), (16, 1, 4, 8, 2))


def offset_of(order, position):
    offset = 0
    for bit, mask in enumerate(order):
        if position >> bit & 1:
            offset ^= mask
    return offset


def dot(left, right, dims=NN):
    return lax.dot_general(left, right, dims, preferred_element_type=jnp.float32)


def shift(array, mask, count):
    return lax.ppermute(array, AXES, [(i, i ^ mask) for i in range(count)])


def place_weights(me, order, sources, weight_ref, column, sem):
    depth = weight_ref.shape[1] >> len(order)
    width = sources[0].shape[-1]
    held = sources[0].shape[0]
    for position in range(len(sources) * held):
        owner = me ^ offset_of(order, position)
        rows = pl.ds(pl.multiple_of(owner * depth, depth), depth)
        for matrix in range(3):
            pltpu.make_async_copy(
                sources[position // held].at[position % held, pl.ds(matrix * depth, depth), :],
                weight_ref.at[matrix, rows, pl.ds(column, width)],
                sem,
            ).start()


def normalize(rows):
    mean = jnp.mean(rows, axis=-1, keepdims=True)
    centre = rows - mean
    spread = jnp.mean(centre * centre, axis=-1, keepdims=True)
    scale = lax.rsqrt(spread + EPSILON)
    return centre * scale, scale


def column_sum(rows):
    return jnp.sum(rows.astype(jnp.float32), axis=0, keepdims=True)


def project(normed_ref, w_ref, vec_ref, qkv_ref, column):
    width = qkv_ref.shape[-1]
    for matrix, bias in ((0, 4), (1, None), (2, 5)):
        out = dot(normed_ref[...], w_ref[matrix])
        if bias is not None:
            out = out + vec_ref[bias : bias + 1, column : column + width]
        qkv_ref[matrix] = out.astype(jnp.bfloat16)


def project_first_kernel(me_ref, own_in, first_in, second_in, *refs):
    sources = refs[:4]
    normed_out, qkv_out, vec_ref, other_out, weight_out, *refs = refs[4:]
    x_ref, normed_ref, qkv_ref, w_ref, block_ref, x_sem, w_sem, v_sem, out_sem = refs
    me = me_ref[0]
    rank = me & 1
    half_rows, features = x_ref.shape[1:]
    width = w_ref.shape[2]
    depth = features >> len(ORDERS[0])
    count, rows = block_ref.shape[:2]
    held = sources[0].shape[0]
    for position in range(count):
        pltpu.make_async_copy(
            sources[position // held].at[position % held, pl.ds(3 * depth, rows), pl.ds(0, block_ref.shape[2])],
            block_ref.at[me ^ offset_of(ORDERS[0], position)],
            v_sem,
        ).start()
    x_in = [
        pltpu.make_async_copy(own_in.at[rank], x_ref.at[0], x_sem.at[0]),
        pltpu.make_async_copy(first_in, x_ref.at[1, pl.ds(0, first_in.shape[0])], x_sem.at[1]),
        pltpu.make_async_copy(second_in, x_ref.at[1, pl.ds(first_in.shape[0], second_in.shape[0])], x_sem.at[2]),
    ]
    for copy in x_in:
        copy.start()
    for matrix in range(3):
        place_matrix(me, ORDERS[0], sources, matrix, w_ref, 0, w_sem.at[matrix])
    outs = []

    def send(source, target):
        outs.append(pltpu.make_async_copy(source, target, out_sem.at[len(outs)]))
        outs[-1].start()

    def norm(half):
        normed, _ = normalize(x_ref[half].astype(jnp.float32))
        normed_ref[half] = (normed * vec_ref[0:1] + vec_ref[2:3]).astype(jnp.bfloat16)

    def product(half, matrix):
        out = dot(normed_ref[half], w_ref[matrix])
        if matrix != 1:
            bias = 4 + matrix // 2
            out = out + vec_ref[bias : bias + 1, 0:width]
        qkv_ref[half, matrix] = out.astype(jnp.bfloat16)

    def rows_of(half):
        return pl.ds(pl.multiple_of((half ^ rank) * half_rows, half_rows), half_rows)

    pltpu.make_async_copy(block_ref, block_ref, v_sem).wait()
    for owner in range(count):
        vec_ref[:, owner * depth : (owner + 1) * depth] = block_ref[owner, :, 0:depth].astype(jnp.float32)
    x_in[0].wait()
    norm(0)
    for matrix in range(3):
        pltpu.make_async_copy(w_ref.at[matrix], w_ref.at[matrix], w_sem.at[matrix]).wait()
    x_in[1].wait()
    x_in[2].wait()
    product(0, 0)
    norm(1)
    product(0, 1)
    product(0, 2)
    send(x_ref.at[1], other_out)
    send(w_ref, weight_out)
    send(normed_ref.at[0], normed_out.at[rows_of(0)])
    send(normed_ref.at[1], normed_out.at[rows_of(1)])
    send(qkv_ref.at[0], qkv_out.at[:, rows_of(0), :])
    for matrix in range(3):
        product(1, matrix)
    send(qkv_ref.at[1], qkv_out.at[:, rows_of(1), :])
    for copy in outs:
        copy.wait()


def project_next_kernel(me_ref, normed_ref, vec_ref, *refs):
    *sources, qkv_ref, weight_ref, w_ref, sem = refs
    step = pl.program_id(0)

    @pl.when(step == 0)
    def _():
        place_weights(me_ref[0], ORDERS[1], sources, w_ref, 0, sem)
        pltpu.make_async_copy(w_ref, w_ref, sem).wait()
        pltpu.make_async_copy(w_ref, weight_ref, sem).start()

    project(normed_ref, w_ref, vec_ref, qkv_ref, qkv_ref.shape[-1])

    @pl.when(step == 1)
    def _():
        pltpu.make_async_copy(w_ref, weight_ref, sem).wait()


def key_ranges(length):
    quarter = length // 4
    return ((0, 2 * quarter), (0, length), (quarter, length), (quarter, length))


def attend_kernel(scale, q_ref, k_ref, v_ref, column_ref, row_ref, mix_ref, prob_ref, inverse_ref):
    length = q_ref.shape[1]
    tile = length // 8
    ranges = [(row, *key_ranges(length)[2 * row // (length // 2)]) for row in range(0, length, tile)]

    def score(index):
        row, first, last = ranges[index]
        return dot(q_ref[0, row : row + tile, :], k_ref[0, first:last, :], NT)

    def mix(index, low, inverse):
        row, first, last = ranges[index]
        mix_ref[row : row + tile, :] = (dot(low, v_ref[0, first:last, :]) * inverse).astype(jnp.bfloat16)

    scores, before = score(0), None
    for index, (row, first, last) in enumerate(ranges):
        following = score(index + 1) if index + 1 < len(ranges) else None
        rows = slice(row, row + tile)
        same = column_ref[rows, :] == row_ref[0, :, first:last]
        scores = jnp.where(same, scores, -1e30)
        top = jnp.max(scores, axis=-1, keepdims=True)
        expo = jnp.exp2((scores - top) * (scale * math.log2(math.e)))
        low = expo.astype(jnp.bfloat16)
        inverse = 1.0 / jnp.sum(expo, axis=-1, keepdims=True)
        prob_ref[0, rows, first:last] = low
        inverse_ref[0, rows, :] = jnp.broadcast_to(inverse, (tile, inverse_ref.shape[2]))
        if before is not None:
            mix(*before)
        before, scores = (index, low, inverse), following
    mix(*before)


def attend_back_kernel(
    scale, q_ref, k_ref, v_ref, prob_ref, mix_ref, mixg_ref, inverse_ref, out_ref, sum_ref, key_acc, value_acc
):
    length = q_ref.shape[1]
    quarter = length // 4
    key_acc[...] = jnp.zeros_like(key_acc)
    value_acc[...] = jnp.zeros_like(value_acc)
    mix_grad = (mixg_ref[...].astype(jnp.float32) * inverse_ref[0]).astype(jnp.bfloat16)
    centred = jnp.sum(mix_grad.astype(jnp.float32) * mix_ref[...].astype(jnp.float32), axis=-1, keepdims=True)
    ranges = key_ranges(length)

    def grads_of(index):
        first, last = ranges[index]
        return dot(mix_grad[index * quarter : (index + 1) * quarter], v_ref[0, first:last, :], NT)

    def spread(index, score_grads, low):
        first, last = ranges[index]
        rows = slice(index * quarter, (index + 1) * quarter)
        out_ref[0, rows, :] = (dot(score_grads, k_ref[0, first:last, :]) * scale).astype(jnp.bfloat16)
        key_acc[first:last, :] += dot(score_grads, q_ref[0, rows, :], TN)
        value_acc[first:last, :] += dot(low, mix_grad[rows], TN)

    grads, before = grads_of(0), None
    for index, (first, last) in enumerate(ranges):
        following = grads_of(index + 1) if index + 1 < len(ranges) else None
        rows = slice(index * quarter, (index + 1) * quarter)
        low = prob_ref[0, rows, first:last]
        score_grads = (low.astype(jnp.float32) * (grads - centred[rows])).astype(jnp.bfloat16)
        if before is not None:
            spread(*before)
        before, grads = (index, score_grads, low), following
    spread(*before)
    out_ref[1] = (key_acc[...] * scale).astype(jnp.bfloat16)
    out_ref[2] = value_acc[...].astype(jnp.bfloat16)
    sum_ref[...] = jnp.zeros_like(sum_ref)
    sum_ref[0:1] = column_sum(out_ref[0])
    sum_ref[1:2] = column_sum(out_ref[2])


def project_back_kernel(order, me_ref, normed_ref, grad_ref, keep_ref, send_ref, stage_ref, sems):
    step = pl.program_id(0)
    stage_ref[step] = dot(normed_ref[...], grad_ref[0], TN).astype(jnp.bfloat16)
    for matrix in range(3):

        @pl.when(step == matrix)
        def _():
            stage = stage_ref.at[matrix]
            collect_matrix(me_ref[0], order, stage, matrix, keep_ref, send_ref, 0, sems.at[matrix])

    @pl.when(step == 2)
    def _():
        for matrix in range(3):
            stage = stage_ref.at[matrix]
            pltpu.make_async_copy(stage, stage, sems.at[matrix]).wait()


def place_matrix(me, order, sources, matrix, weight_ref, column, sem):
    depth = weight_ref.shape[1] >> len(order)
    width = sources[0].shape[-1]
    held = sources[0].shape[0]
    for position in range(len(sources) * held):
        owner = me ^ offset_of(order, position)
        rows = pl.ds(pl.multiple_of(owner * depth, depth), depth)
        pltpu.make_async_copy(
            sources[position // held].at[position % held, pl.ds(matrix * depth, depth), :],
            weight_ref.at[matrix, rows, pl.ds(column, width)],
            sem,
        ).start()


def collect_matrix(me, order, stage_ref, matrix, keep_ref, send_ref, base, sem):
    half = 1 << len(order) - 1
    depth = stage_ref.shape[0] >> len(order)
    for position in reversed(range(2 * half)):
        target = keep_ref if position < half else send_ref
        owner = me ^ offset_of(order, position)
        rows = pl.ds(pl.multiple_of(owner * depth, depth), depth)
        place = base + (position % half * 3 + matrix) * depth
        pltpu.make_async_copy(stage_ref.at[rows, :], target.at[pl.ds(place, depth), :], sem).start()


def feed_kernel(
    me_ref, x_own_ref, x_other_ref, cot_own_ref, cot_other_ref, mix0_ref, mix1_ref, column_ref, vec_ref, *refs
):
    sources = refs[:8]
    result_ref, result_other_ref, resg_ref, mixg_ref, sum_ref, keep_ref, send_ref, *refs = refs[8:]
    (
        w_ref, x_ref, cot_ref, mix_ref, hid_ref, act_ref, og_ref, pre_ref, res_ref, resid_ref, slope_ref,
        out_ref, resg_out, mixg_out, stage_ref, w_sem, in_sem, out_sem, g_sem,
    ) = refs
    me = me_ref[0]
    rank = me & 1
    half_rows, features = x_other_ref.shape
    width = features // 2
    places = [pl.multiple_of((half ^ rank) * half_rows, half_rows) for half in range(2)]
    rows = [pl.ds(place, half_rows) for place in places]

    def weights(matrix):
        for half in range(2):
            place_matrix(me, ORDERS[half], sources[4 * half : 4 * half + 4], matrix, w_ref, half * width, w_sem.at[matrix])

    def weights_here(matrix):
        pltpu.make_async_copy(w_ref.at[matrix], w_ref.at[matrix], w_sem.at[matrix]).wait()

    mix_in = [
        pltpu.make_async_copy(ref, mix_ref.at[:, pl.ds(half * width, width)], in_sem.at[half])
        for half, ref in enumerate((mix0_ref, mix1_ref))
    ]
    x_in = [
        pltpu.make_async_copy(ref, x_ref.at[half], in_sem.at[2 + half])
        for half, ref in enumerate((x_own_ref.at[rank], x_other_ref))
    ]
    cot_in = [
        pltpu.make_async_copy(ref, cot_ref.at[half], in_sem.at[4 + half])
        for half, ref in enumerate((cot_own_ref.at[rank], cot_other_ref))
    ]
    for copy in mix_in:
        copy.start()
    weights(0)
    x_in[0].start()
    x_in[1].start()
    weights(1)
    cot_in[0].start()
    cot_in[1].start()
    weights(2)
    sums = [jnp.zeros((1, features), jnp.float32)] * 5
    out_copies = []

    def attend_out(half):
        x_in[half].wait()
        resid_ref[half] = x_ref[half].astype(jnp.float32) + dot(mix_ref[rows[half], :], w_ref[0]) + vec_ref[6:7]

    def norm_two(half):
        normed, _ = normalize(resid_ref[half])
        hid_ref[half] = (normed * vec_ref[1:2] + vec_ref[3:4]).astype(jnp.bfloat16)

    def first(half):
        return dot(hid_ref[half], w_ref[1]) + vec_ref[7:8]

    def gelu(half, pre):
        square = pre * pre
        tanh = jnp.tanh(0.7978845608 * pre * (1.0 + 0.044715 * square))
        upper = 0.5 * (1.0 + tanh)
        act_ref[half] = (pre * upper).astype(jnp.bfloat16)
        slope_ref[half] = upper * (
            1.0 + pre * (1.0 - tanh) * (0.7978845608 + (3 * 0.044715 * 0.7978845608) * square)
        )

    def mask(half):
        cot_in[half].wait()
        live = (column_ref[rows[half], :] >= 0).astype(jnp.float32)
        og_ref[half] = (cot_ref[half].astype(jnp.float32) * live).astype(jnp.bfloat16)

    def second(half):
        result = resid_ref[half] + dot(act_ref[half], w_ref[2]) + vec_ref[8:9]
        out_ref[half] = result.astype(jnp.bfloat16)
        target = (result_ref.at[rank], result_other_ref)[half]
        out_copies.append(pltpu.make_async_copy(out_ref.at[half], target, out_sem.at[half]))
        out_copies[-1].start()

    def second_back(half):
        return dot(og_ref[half], w_ref[2], NT)

    def gelu_back(half, grad):
        pre_ref[half] = (grad * slope_ref[half]).astype(jnp.bfloat16)
        sums[3] = sums[3] + column_sum(pre_ref[half])
        sums[4] = sums[4] + column_sum(og_ref[half])

    def first_back(half):
        return dot(pre_ref[half], w_ref[1], NT)

    def norm_back(half, grad):
        normed, inverse = normalize(resid_ref[half])
        sums[0] = sums[0] + column_sum(grad * normed)
        sums[1] = sums[1] + column_sum(grad)
        scaled = grad * vec_ref[1:2]
        resg = og_ref[half].astype(jnp.float32) + inverse * (
            scaled
            - jnp.mean(scaled, axis=-1, keepdims=True)
            - normed * jnp.mean(scaled * normed, axis=-1, keepdims=True)
        )
        resg_out[half] = resg
        res_ref[rows[half], :] = resg.astype(jnp.bfloat16)
        sums[2] = sums[2] + column_sum(resg.astype(jnp.bfloat16))

    def out_back(half):
        mixg_out[half] = dot(res_ref[rows[half], :], w_ref[0], NT).astype(jnp.bfloat16)
        for source, target, number in (
            (resg_out.at[half], resg_ref.at[half], 2 + half), (mixg_out.at[half], mixg_ref.at[rows[half]], 4 + half)
        ):
            out_copies.append(pltpu.make_async_copy(source, target, out_sem.at[number]))
            out_copies[-1].start()

    def weight_grad(matrix, half):
        columns = slice(half * width, (half + 1) * width)
        if matrix == 0:
            total = dot(mix_ref[...], res_ref[:, columns], TN)
        else:
            left, right = ((hid_ref, pre_ref), (act_ref, og_ref))[matrix - 1]
            total = dot(left[0], right[0, :, columns], TN) + dot(left[1], right[1, :, columns], TN)
        stage = stage_ref.at[half, matrix]
        stage_ref[half, matrix] = total.astype(jnp.bfloat16)
        collect_matrix(
            me, ORDERS[half], stage, matrix, keep_ref, send_ref, half * keep_ref.shape[0] // 2, g_sem.at[half, matrix]
        )

    for copy in mix_in:
        copy.wait()
    weights_here(0)
    attend_out(0)
    attend_out(1)
    norm_two(0)
    weights_here(1)
    pre0 = first(0)
    norm_two(1)
    pre1 = first(1)
    gelu(0, pre0)
    mask(0)
    weights_here(2)
    second(0)
    grad0 = second_back(0)
    gelu(1, pre1)
    mask(1)
    second(1)
    grad1 = second_back(1)
    gelu_back(0, grad0)
    grad0 = first_back(0)
    gelu_back(1, grad1)
    weight_grad(2, 0)
    grad1 = first_back(1)
    norm_back(0, grad0)
    weight_grad(2, 1)
    out_back(0)
    weight_grad(1, 0)
    norm_back(1, grad1)
    weight_grad(1, 1)
    out_back(1)
    weight_grad(0, 0)
    weight_grad(0, 1)
    sum_ref[...] = jnp.zeros_like(sum_ref)
    for row, value in enumerate(sums):
        sum_ref[row : row + 1] = value
    for copy in out_copies:
        copy.wait()
    for half in range(2):
        for matrix in range(3):
            stage = stage_ref.at[half, matrix]
            pltpu.make_async_copy(stage, stage, g_sem.at[half, matrix]).wait()


def finish_kernel(
    flip, me_ref, x_in, resg_in, grad0_ref, grad1_ref, w0_ref, w1_ref, vec_ref, out_ref, sum_ref,
    x_ref, resg_ref, grad_ref, w_ref, in_sem, sems,
):
    rank = me_ref[0] & 1
    half_rows, features = x_ref.shape
    width = features // 2
    rows = pl.ds(pl.multiple_of((rank ^ flip) * half_rows, half_rows), half_rows)
    copies = []
    for matrix in range(3):
        for half, (grad, weight) in enumerate(((grad0_ref, w0_ref), (grad1_ref, w1_ref))):
            columns = pl.ds(half * width, width)
            copies.append([
                pltpu.make_async_copy(grad.at[matrix, rows, :], grad_ref.at[matrix, :, columns], sems.at[matrix, half]),
                pltpu.make_async_copy(weight.at[matrix], w_ref.at[matrix, :, columns], sems.at[matrix, 2 + half]),
            ])
    later = [
        pltpu.make_async_copy(x_in if flip else x_in.at[rank], x_ref, in_sem.at[0]),
        pltpu.make_async_copy(resg_in.at[flip], resg_ref, in_sem.at[1]),
    ]
    for copy in sum(copies, []) + later:
        copy.start()
    normed_grad = None
    for matrix in range(3):
        for copy in copies[2 * matrix] + copies[2 * matrix + 1]:
            copy.wait()
        term = dot(grad_ref[matrix], w_ref[matrix], NT)
        normed_grad = term if normed_grad is None else normed_grad + term
    for copy in later:
        copy.wait()
    normed, inverse = normalize(x_ref[...].astype(jnp.float32))
    sum_ref[...] = jnp.zeros_like(sum_ref)
    sum_ref[0:1] = column_sum(normed_grad * normed)
    sum_ref[1:2] = column_sum(normed_grad)
    scaled = normed_grad * vec_ref[0:1]
    total = resg_ref[...] + inverse * (
        scaled
        - jnp.mean(scaled, axis=-1, keepdims=True)
        - normed * jnp.mean(scaled * normed, axis=-1, keepdims=True)
    )
    out_ref[...] = total.reshape(out_ref.shape).astype(out_ref.dtype)


def double_first_kernel(me_ref, own_ref, own_vec_ref, got_ref, got_vec_ref, out_ref):
    matrices, depth, features = own_ref.shape
    width = features // 2
    base = matrices * depth
    out_ref[:, :, base:, :] = jnp.zeros_like(out_ref[:, :, base:, :])
    for block, (part, vectors) in enumerate(((own_ref, own_vec_ref), (got_ref, got_vec_ref))):
        for half in range(2):
            for matrix in range(matrices):
                rows = slice(matrix * depth, (matrix + 1) * depth)
                out_ref[block, half, rows, :] = part[matrix, :, half * width : (half + 1) * width]
        out_ref[block, 0, base : base + vectors.shape[0], 0:depth] = vectors[...]


def pack_next_kernel(me_ref, output_ref, hidden_ref, out_ref, sems):
    depth, features = output_ref.shape
    width = features // 2
    copies = []
    for half in range(2):
        columns = pl.ds(half * width, width)
        sources = [output_ref.at[:, columns]] + [hidden_ref.at[matrix, :, columns] for matrix in range(2)]
        for matrix, source in enumerate(sources):
            target = out_ref.at[0, half, pl.ds(matrix * depth, depth), :]
            copies.append(pltpu.make_async_copy(source, target, sems.at[len(copies)]))
    for copy in copies:
        copy.start()
    for copy in copies:
        copy.wait()


def join_kernel(moves, me_ref, *refs):
    for source, source_index, target, target_index in moves:
        refs[target][target_index] = refs[source][source_index]


def join_out_kernel(moves, me_ref, *refs):
    *refs, sems = refs
    copies = [
        pltpu.make_async_copy(refs[source].at[source_index], refs[target].at[target_index], sems.at[number])
        for number, (source, source_index, target, target_index) in enumerate(moves)
    ]
    for copy in copies:
        copy.start()
    for copy in copies:
        copy.wait()


def select_kernel(me_ref, rows_ref, *refs):
    row = 0
    for out_ref in refs[:-1]:
        out_ref[...] = rows_ref[0, row : row + out_ref.shape[0], :]
        row += out_ref.shape[0]
    refs[-1][...] = jnp.zeros_like(refs[-1])


def total_of(refs, width):
    total = None
    for ref in refs:
        term = ref[...].astype(jnp.float32).reshape(-1, width)
        total = term if total is None else total + term
    return total


def combine_kernel(sums, me_ref, *refs):
    for first, last, output, row in sums:
        out_ref = refs[output]
        total = total_of(refs[first:last], out_ref.shape[-1])
        out_ref[row : row + total.shape[0], :] = total.astype(out_ref.dtype)


def final_kernel(inputs, me_ref, *refs):
    outs = refs[2 * inputs :]
    depth, features = outs[0].shape[1:]
    width = features // 2
    for half in range(2):
        total = total_of(refs[half * inputs : (half + 1) * inputs], width)
        row = 0
        for out_ref in outs:
            matrices = out_ref.shape[0]
            piece = total[row : row + matrices * depth].reshape(matrices, depth, width)
            out_ref[:, :, half * width : (half + 1) * width] = piece
            row += matrices * depth


def final_vector_kernel(inputs, vectors, me_ref, *refs):
    blocks, terms = refs[: 2 * inputs], refs[2 * inputs : 2 * inputs + vectors]
    out_ref, gain_ref, bias_ref = refs[2 * inputs + vectors :]
    final_kernel(inputs, me_ref, *blocks, out_ref)
    picked = own_columns(me_ref, terms, gain_ref.shape[1])
    gains = gain_ref.shape[0]
    gain_ref[...] = picked[0:gains]
    bias_ref[...] = picked[gains : gains + bias_ref.shape[0]]


def own_columns(me_ref, terms, depth):
    rows = terms[0].shape[0] // 2
    width = terms[0].shape[-1]
    total = total_of(terms, width)
    lane = lax.broadcasted_iota(jnp.int32, (width, depth), 0)
    column = lax.broadcasted_iota(jnp.int32, (width, depth), 1)
    place = me_ref[0] * depth
    picked = None
    for half in range(2):
        choose = (lane + half * width == column + place).astype(jnp.float32)
        part = lax.dot_general(
            total[half * rows : (half + 1) * rows], choose, NN, precision=lax.Precision.HIGHEST,
            preferred_element_type=jnp.float32,
        )
        picked = part if picked is None else picked + part
    return picked


def vector_pack_kernel(me_ref, feed_ref, last0_ref, last1_ref, s0_ref, s1_ref, out_ref, row_ref):
    width = out_ref.shape[-1]
    row_ref[...] = jnp.zeros_like(row_ref)
    row_ref[0:1] = last0_ref[0:1] + last1_ref[0:1]
    row_ref[1:2] = feed_ref[0:1]
    row_ref[2:3] = last0_ref[1:2] + last1_ref[1:2]
    row_ref[3:4] = feed_ref[1:2]
    for half, sums in enumerate((s0_ref, s1_ref)):
        row_ref[4:6, half * width : (half + 1) * width] = sums[0:2]
    row_ref[6:9] = feed_ref[2:5]
    for half in range(2):
        out_ref[half * 16 : (half + 1) * 16, :] = row_ref[:, half * width : (half + 1) * width].astype(jnp.bfloat16)


ANY = pl.BlockSpec(memory_space=pl.ANY)
VMEM = pl.BlockSpec(memory_space=pltpu.VMEM)
HBM = pl.BlockSpec(memory_space=pltpu.HBM)
SMALL_LIMIT = 24 << 20


def call(kernel, me, grid, operands, out_specs, out_shape, scratch=(), flops=1e6, moved=1e6, after=(), limit=VMEM_LIMIT):
    taken = len(operands) + 1
    after = list(after)
    ordered = ANY if limit == SMALL_LIMIT else HBM

    def body(*refs):
        kernel(*refs[:taken], *refs[taken + len(after) :])

    return pl.pallas_call(
        body,
        grid_spec=pltpu.PrefetchScalarGridSpec(
            num_scalar_prefetch=1,
            grid=grid,
            in_specs=[spec for _, spec in operands] + [ordered] * len(after),
            out_specs=out_specs,
            scratch_shapes=list(scratch),
        ),
        out_shape=out_shape,
        compiler_params=pltpu.CompilerParams(
            dimension_semantics=("arbitrary",) * len(grid), vmem_limit_bytes=limit
        ),
        cost_estimate=pl.CostEstimate(flops=int(flops), bytes_accessed=int(moved), transcendentals=0),
    )(me, *[array for array, _ in operands], *after)


def struct(shape, dtype=jnp.bfloat16):
    return jax.ShapeDtypeStruct(shape, dtype)


def whole(shape):
    return pl.BlockSpec(shape, lambda *_: (0,) * len(shape))


def join(me, arrays, moves, shapes, after=(), kind="local"):
    moves = [(i, source, len(arrays) + o, target) for i, source, o, target in moves]
    place = whole if kind == "far" else lambda shape: VMEM
    kernel = functools.partial(join_out_kernel if kind == "out" else join_kernel, moves)
    return call(
        kernel, me, (1,), [(a, place(a.shape)) for a in arrays],
        [HBM if kind == "out" else place(s) for s in shapes], [struct(s) for s in shapes],
        [pltpu.SemaphoreType.DMA((len(moves),))] if kind == "out" else [], after=after,
        limit=VMEM_LIMIT if kind == "far" else SMALL_LIMIT,
    )


def part(array, start, size, tall):
    return array, pl.BlockSpec((size * tall, array.shape[-1]), lambda i, me: (start // size, 0))


def combine(me, outputs, after=(), flops=1e6, dtype=jnp.bfloat16):
    operands, sums, shapes = [], [], []
    count = sum(len(terms) for group in outputs for terms in group)
    for number, group in enumerate(outputs):
        row = 0
        for terms in group:
            first = len(operands)
            operands.extend(terms)
            sums.append((first, len(operands), count + number, row))
            row += terms[0][1].block_shape[0]
        shapes.append((row, group[0][0][0].shape[-1]))
    steps = STEPS if all(len(group) == 1 for group in outputs) else 1

    def cut_rows(spec):
        rows, columns = spec.block_shape
        index = spec.index_map(0, None)[0]
        return pl.BlockSpec((rows // steps, columns), lambda i, me: (index * steps + i, 0))

    return call(
        functools.partial(combine_kernel, sums), me, (steps,), [(array, cut_rows(spec)) for array, spec in operands],
        [pl.BlockSpec((rows // steps, columns), lambda i, me: (i, 0)) for rows, columns in shapes],
        [struct(shape, dtype) for shape in shapes], flops=flops, after=after,
    )


def final(me, halves, depth, features, counts, vectors=()):
    shapes = [(matrices, depth, features) for matrices in counts]
    kernel = functools.partial(final_kernel, len(halves[0]))
    if vectors:
        kernel = functools.partial(final_vector_kernel, len(halves[0]), len(vectors))
        shapes.extend([(2, depth), (7, depth)])
    return call(
        kernel, me, (1,), halves[0] + halves[1] + list(vectors), [whole(s) for s in shapes],
        [struct(s, jnp.float32) for s in shapes],
    )


def whole_sequence(
    latents, segments, attention_weights, output_weight, hidden_weights, gains, biases, cotangent
):
    half_rows, features = latents.shape[2:]
    length = 2 * half_rows
    head_size = features // HEADS
    scale = 1.0 / math.sqrt(head_size)
    width = features // 2
    count = 1 << len(ORDERS[0])
    depth = features // count
    rank = lax.axis_index("row")
    device = (lax.axis_index("seq") * 2 + rank).astype(jnp.int32)
    me = device.reshape(1)
    bf16, f32 = jnp.bfloat16, jnp.float32
    dense = 2.0 * length * features * features
    tall = 3 * depth
    vector_rows = gains.shape[0] + biases.shape[0]
    padded = tall + 16

    def move(array, mask):
        return shift(array, mask, count)

    def double(held, got, after=()):
        return join(me, [held, got], [(0, 0, 0, 0), (1, 0, 0, 1)], [(2,) + held.shape[1:]], after)[0]

    def split(held, got, rows, after=(), kind="local"):
        moves, shapes = [], []
        for half in range(2):
            for source in range(2):
                for block in range(2):
                    moves.append((source, (block, half, pl.ds(0, rows[half])), half, 2 * source + block))
            shapes.append((4, rows[half], width))
        return join(me, [held, got], moves, shapes, after, kind)

    def append(held, got, after=(), kind="out"):
        moves, shapes = [], []
        for half in range(2):
            for source in range(2):
                moves.append((2 * half + source, pl.ds(0, 4), half, pl.ds(4 * source, 4)))
            shapes.append((8,) + held[half].shape[1:])
        return join(me, [held[0], got[0], held[1], got[1]], moves, shapes, after, kind)

    z_far, y, z_near, x, core = 16, 1, 8, 4, 2
    def pack(kernel, arrays, rows, scratch, after=()):
        return call(
            kernel, me, (1,), [(a, HBM) for a in arrays], VMEM, struct((1, 2, rows, width)), scratch, after=after,
            limit=SMALL_LIMIT,
        )

    latents_flat = latents[:, 0]
    cotangent_flat = cotangent[:, 0]

    def select(array, parts, after):
        shapes = [(half_rows * share // sum(parts), features) for share in parts]
        return call(
            select_kernel, me, (1,),
            [(array, pl.BlockSpec((1, half_rows, features), lambda i, me: (1 - (me[0] & 1), 0, 0)))],
            [whole(shape) for shape in shapes] + [VMEM], [struct(shape) for shape in shapes] + [struct((8, 128), f32)],
            after=after, limit=SMALL_LIMIT,
        )

    sems = lambda number: pltpu.SemaphoreType.DMA((number,))
    vectors_own = jnp.concatenate([gains, biases], axis=0)
    a1_got = (move(attention_weights, z_far), move(vectors_own, z_far))
    *x_send, x_token = select(latents_flat, (5, 3), [])
    a2 = call(
        double_first_kernel, me, (1,),
        [(a, VMEM) for a in (attention_weights, vectors_own, *a1_got)], VMEM, struct((2, 2, padded, width)),
        after=[x_token], limit=SMALL_LIMIT,
    )
    f1 = pack(pack_next_kernel, [output_weight, hidden_weights], tall, [sems(6)], [a2])
    a4 = split(a2, move(a2, y), (padded, tall), [f1])
    x_first = move(x_send[0], y)
    cot_send, cot_token = select(cotangent_flat, (1,), a4)
    f2 = double(f1, move(f1, z_far), [a4[0], cot_token])
    a8 = append(a4, (move(a4[0], z_near), move(a4[1], x)), [f2, x_first])
    a_core = [move(a, core) for a in a8]
    x_second = move(x_send[1], y)
    f4 = split(f2, move(f2, y), (tall, tall), a8, "out")
    a_far = join(
        me, [move(a8[0], x), move(a8[1], z_near)], [(h, pl.ds(0, 8), h, pl.ds(0, 8)) for h in range(2)],
        [a.shape for a in a8], [f4[0], x_second], "out",
    )
    a_far_core = [move(a, core) for a in a_far]
    attn_sources = [[a8[h], a_far[h], a_core[h], a_far_core[h]] for h in range(2)]

    segment_row = segments
    segment_column = lax.dynamic_index_in_dim(segments[:, 0], rank, 0, keepdims=False)[:, None]

    own = pl.BlockSpec((1, half_rows, features), lambda i, me: (me[0] & 1, 0, 0))
    local = pl.BlockSpec((half_rows, features), lambda i, me: (i ^ (me[0] & 1), 0))
    local3 = pl.BlockSpec((3, half_rows, width), lambda i, me: (0, i ^ (me[0] & 1), 0))
    rows_spec = whole((half_rows, features))
    low = lambda *shape: pltpu.VMEM(shape, bf16)
    dma = lambda *shape: pltpu.SemaphoreType.DMA(shape)
    w_scratch = pltpu.VMEM((3, features, width), bf16)
    w_struct = struct((3, features, width))
    normed_low, qkv0, vec, x_other, weight0 = call(
        project_first_kernel, me, (1,),
        [(a, HBM) for a in (latents_flat, x_first, x_second)] + [(a, ANY) for a in attn_sources[0]],
        [HBM, HBM, whole((16, features)), HBM, HBM],
        [struct((length, features)), struct((3, length, width)), struct((16, features), f32),
         struct((half_rows, features)), w_struct],
        [low(2, half_rows, features), low(2, half_rows, features), low(2, 3, half_rows, width), w_scratch,
         low(count, 16, 128), dma(3), dma(3), pltpu.SemaphoreType.DMA(()), dma(6)],
        1.5 * dense, 16e6, f4,
    )
    vec_op = (vec, whole((16, features)))
    cot_other = move(cot_send, y)
    f8 = append(f4, (move(f4[0], z_near), move(f4[1], x)), [vec], "far")
    f_core = [move(a, core) for a in f8]
    f_far = (move(f8[0], x), move(f8[1], z_near))
    qkv1, weight1 = call(
        project_next_kernel, me, (2,),
        [(normed_low, pl.BlockSpec((half_rows, features), lambda i, me: (i, 0))), vec_op]
        + [(a, ANY) for a in attn_sources[1]],
        [pl.BlockSpec((3, half_rows, width), lambda i, me: (0, i, 0)), ANY], [struct((3, length, width)), w_struct],
        [w_scratch, pltpu.SemaphoreType.DMA(())], 1.5 * dense, 8e6, f8,
    )

    heads = width // head_size
    head_specs = [
        pl.BlockSpec((1, length, head_size), functools.partial(lambda c, h, me: (c, 0, h), c)) for c in range(3)
    ]
    column_block = pl.BlockSpec((length, head_size), lambda h, me: (0, h))
    prob_block = pl.BlockSpec((1, length, length), lambda h, me: (h, 0, 0))
    inverse_block = pl.BlockSpec((1, length, head_size), lambda h, me: (h, 0, 0))
    segment_spec = pl.BlockSpec((1, 1, length), lambda h, me: (me[0] & 1, 0, 0))

    def attend(qkv, after):
        return call(
            lambda me_ref, *refs: attend_kernel(scale, *refs), me, (heads,),
            [(qkv, s) for s in head_specs] + [(segment_column, whole((length, 1))), (segment_row, segment_spec)],
            [column_block, prob_block, inverse_block],
            [struct((length, width)), struct((heads, length, length)), struct((heads, length, head_size), f32)], [],
            4 * dense, 30e6, after,
        )

    mix0, prob0, inverse0 = attend(qkv0, [qkv1])
    f_far_core = [move(a, core) for a in f_far]
    feed_sources = [[f8[h], f_far[h], f_core[h], f_far_core[h]] for h in range(2)]
    mix1, prob1, inverse1 = attend(qkv1, [mix0])

    keeps = [struct((count * tall, width))] * 2
    local_rows = pltpu.VMEM((2, half_rows, features), f32)
    result_own, result_other, residual_grad, mix_grad, feed_sums, fk, fs = call(
        feed_kernel, me, (1,),
        [(a, HBM) for a in (latents_flat, x_other, cotangent_flat, cot_other, mix0, mix1)]
        + [(segment_column, whole((length, 1))), vec_op] + [(a, ANY) for a in feed_sources[0] + feed_sources[1]],
        [HBM] * 4 + [whole((8, features))] + [ANY] * 2,
        [struct((2, half_rows, features)), struct((half_rows, features)), struct((2, half_rows, features), f32),
         struct((length, features)), struct((8, features), f32)] + keeps,
        [low(3, features, features), low(2, half_rows, features), low(2, half_rows, features), low(length, features)]
        + [low(2, half_rows, features)] * 4 + [low(length, features), local_rows, local_rows]
        + [low(2, half_rows, features), local_rows, low(2, half_rows, features), low(2, 3, features, width)]
        + [dma(3), dma(6), dma(6), dma(2, 3)],
        9 * dense, 30e6,
    )
    f_c = move(fs, core)
    result_back = move(result_other, y)

    def attend_back(qkv, prob, mix, inverse, half, after):
        return call(
            lambda me_ref, *refs: attend_back_kernel(scale, *refs), me, (heads,),
            [(qkv, s) for s in head_specs] + [(prob, prob_block), (mix, column_block),
             (mix_grad, pl.BlockSpec((length, head_size), lambda h, me: (0, h + half * heads))), (inverse, inverse_block)],
            [pl.BlockSpec((3, length, head_size), lambda h, me: (0, 0, h)), pl.BlockSpec((8, head_size), lambda h, me: (0, h))],
            [struct((3, length, width)), struct((8, width), f32)], [pltpu.VMEM((length, head_size), f32)] * 2, 8 * dense, 30e6, after,
        )

    def project_back(grad, order, after):
        return call(
            functools.partial(project_back_kernel, order), me, (3,),
            [(normed_low, whole((length, features))), (grad, pl.BlockSpec((1, length, width), lambda i, me: (i, 0, 0)))],
            [ANY, ANY], [struct((count // 2 * tall, width))] * 2,
            [w_scratch, dma(3)], 1.5 * dense, 8e6, after,
        )

    def finish(rows, flip, out_spec, out_struct, after):
        return call(
            functools.partial(finish_kernel, flip), me, (1,),
            [(a, HBM) for a in (rows, residual_grad, qkv_grad0, qkv_grad1, weight0, weight1)] + [vec_op],
            [out_spec, whole((8, features))], [out_struct, struct((8, features), f32)],
            [low(half_rows, features), pltpu.VMEM((half_rows, features), f32), low(3, half_rows, features),
             low(3, features, features), dma(2), dma(3, 4)], 8 * dense, 20e6, after,
        )

    half_count = count // 2
    blocks = lambda array, start, size: part(array, start, size, tall)
    vector_part = lambda array, row: (array, pl.BlockSpec((32, width), lambda i, me: (row // 32, 0)))
    feed_first = lambda start, size, h: [blocks(a, h * half_count + start, size) for a in (fk, f_c)]
    qkv_grad0, sums0 = attend_back(qkv0, prob0, mix0, inverse0, 0, [])
    fs0, fs1 = combine(me, [[feed_first(8, 8, 0)], [feed_first(8, 8, 1)]], [qkv_grad0])
    f_s2 = (move(fs0, x), move(fs1, z_near))
    ak0, as0 = project_back(qkv_grad0, ORDERS[0], [fs0, fs1])
    a0_c = move(as0, core)
    qkv_grad1, sums1 = attend_back(qkv1, prob1, mix1, inverse1, 1, [ak0])
    terms = [feed_first(4, 4, h) + [blocks(f_s2[h], 4, 4)] for h in range(2)]
    ft0, ft1, at0 = combine(me, [[terms[0]], [terms[1]], [[blocks(ak0, 8, 8), blocks(a0_c, 8, 8)]]], [qkv_grad1])
    f_s3 = (move(ft0, z_near), move(ft1, x))
    a0_s2 = move(at0, x)
    ak1, as1 = project_back(qkv_grad1, ORDERS[1], [ft0, ft1, at0, result_back])
    a1_c = move(as1, core)
    feed_terms = lambda start, size: [
        feed_first(start, size, h) + [blocks(f_s2[h], start, size), blocks(f_s3[h], start, size)] for h in range(2)
    ]
    fu, = combine(me, [feed_terms(2, 2)], [ak1], 8 * dense)
    f_y = move(fu, y)
    at1, = combine(me, [[[blocks(ak1, 8, 8), blocks(a1_c, 8, 8)]]], [fu])
    a1_s2 = move(at1, z_near)
    latent_other, sums_other = finish(x_other, 1, rows_spec, struct((half_rows, features)), [at1])
    latent_back = move(latent_other, y)
    latent_out, sums_own = finish(latents_flat, 0, own, struct((2, half_rows, features), f32), [latent_other])
    vectors = call(
        vector_pack_kernel, me, (1,),
        [(a, whole((8, features))) for a in (feed_sums, sums_own, sums_other)]
        + [(a, whole((8, width))) for a in (sums0, sums1)],
        whole((32, width)), struct((32, width)), [pltpu.VMEM((16, features), f32)], after=[f_y],
    )
    vector_terms = [vector_part(vectors, 0)]
    vector_terms += [vector_part(move(vectors, mask), 0) for mask in (core, z_near, core ^ z_near)]
    au0, au1 = combine(
        me,
        [
            [[blocks(ak0, 4, 4), blocks(a0_c, 4, 4), blocks(a0_s2, 4, 4)]],
            [[blocks(ak1, 4, 4), blocks(a1_c, 4, 4), blocks(a1_s2, 4, 4)], vector_terms],
        ],
    )
    a0_s3 = move(au0, z_near)
    a1_s3 = move(au1, x)
    vector_terms = vector_terms + [vector_part(a1_s3, 4 * tall)]
    ar0, ar1, fr = combine(
        me,
        [
            [[blocks(a, 0, 4) for a in (ak0, a0_c, a0_s2)]],
            [[blocks(a, 0, 4) for a in (ak1, a1_c, a1_s2)]],
            [t + [blocks(f_y, 2 * h + 1, 1)] for h, t in enumerate(feed_terms(1, 1))],
        ],
        [au0], dtype=f32,
    )
    attn_terms = lambda start, size: [
        [blocks(a, start, size) for a in (ar0, a0_s3)], [blocks(a, start, size) for a in (ar1, a1_s3)]
    ]
    av, fv = combine(me, [attn_terms(2, 2) + [vector_terms], [[blocks(fr, 0, 2)]]])
    a_y = move(av, y)
    f_z = move(fv, z_far)
    vector_terms = vector_terms + [vector_part(a_y, 4 * tall)]
    aw, = combine(me, [[t + [blocks(a_y, 2 * h + 1, 1)] for h, t in enumerate(attn_terms(1, 1))] + [vector_terms]])
    a_z = move(aw, z_far)
    vector_terms = vector_terms + [vector_part(a_z, 2 * tall)]
    output_grad, hidden_grads = final(
        me, [t + [blocks(f_y, 2 * h, 1), blocks(f_z, h, 1)] for h, t in enumerate(feed_terms(0, 1))], depth, features,
        (1, 2),
    )
    attn_out, gain_grads, bias_grads = final(
        me, [t + [blocks(a_y, 2 * h, 1), blocks(a_z, h, 1)] for h, t in enumerate(attn_terms(0, 1))], depth, features,
        (3,), vector_terms,
    )

    latent_grads = lax.dynamic_update_slice_in_dim(latent_out, latent_back.astype(f32)[None], 1 - rank, 0)
    activations = lax.dynamic_update_slice_in_dim(result_own, result_back[None], 1 - rank, 0)
    return (
        activations[:, None],
        latent_grads[:, None],
        attn_out,
        output_grad[0],
        hidden_grads,
        gain_grads,
        bias_grads,
    )


def layer_norm(vector, gain_row, offset):
    centre = vector - jnp.mean(vector, axis=-1, keepdims=True)
    spread = jnp.mean(centre * centre, axis=-1, keepdims=True)
    return centre * lax.rsqrt(spread + EPSILON) * gain_row + offset


def on_device(
    latents, segments, attention_weights, output_weight, hidden_weights, gains, biases, cotangent
):
    micro_count = latents.shape[0]
    row_count = latents.shape[2]
    features = latents.shape[3]
    head_size = features // HEADS
    score_scale = 1.0 / math.sqrt(head_size)
    own_rank = lax.axis_index("row")
    attn_total = jnp.zeros((3, features, features), jnp.float32)
    output_total = jnp.zeros((features, features), jnp.float32)
    hidden_total = jnp.zeros((2, features, features), jnp.float32)
    gain_total = jnp.zeros((2, features), jnp.float32)
    bias_total = jnp.zeros((7, features), jnp.float32)
    outputs = []
    input_grads = []
    for micro_index in range(micro_count):
        gathered = (
            lax.all_gather(attention_weights, ("seq", "row"), axis=1, tiled=True),
            lax.all_gather(output_weight, ("seq", "row"), axis=0, tiled=True),
            lax.all_gather(hidden_weights, ("seq", "row"), axis=1, tiled=True),
            lax.all_gather(gains, ("seq", "row"), axis=1, tiled=True),
            lax.all_gather(biases, ("seq", "row"), axis=1, tiled=True),
        )
        attention_full, output_full, hidden_full, gain_full, bias_full = gathered
        gain_values = gain_full.astype(jnp.float32)
        bias_values = bias_full.astype(jnp.float32)
        inputs = latents[micro_index, 0].astype(jnp.float32)
        segment_all = segments[micro_index, 0]
        segment_own = lax.dynamic_slice_in_dim(segment_all, own_rank * row_count, row_count)
        normed_one, norm_one_pull = jax.vjp(layer_norm, inputs, gain_values[0], bias_values[0])
        normed_low = normed_one.astype(jnp.bfloat16)
        projected = jnp.einsum(
            "rd,cde->cre", normed_low, attention_full, preferred_element_type=jnp.float32
        )
        queries = (projected[0] + bias_values[2]).astype(jnp.bfloat16)
        own_keys = projected[1].astype(jnp.bfloat16)
        own_values = (projected[2] + bias_values[3]).astype(jnp.bfloat16)
        all_keys, all_values = (
            lax.all_gather(own_keys, "row", axis=0, tiled=True),
            lax.all_gather(own_values, "row", axis=0, tiled=True),
        )
        length = all_keys.shape[0]
        query_heads = queries.reshape(row_count, HEADS, head_size)
        key_heads = all_keys.reshape(length, HEADS, head_size)
        value_heads = all_values.reshape(length, HEADS, head_size)
        same_set = (segment_own[:, None] == segment_all[None, :])[None]
        raw_scores = (
            jnp.einsum("qhd,khd->hqk", query_heads, key_heads, preferred_element_type=jnp.float32)
            * score_scale
        )
        scores = jnp.where(same_set, raw_scores, -1e30)
        row_max = jnp.max(scores, axis=-1, keepdims=True)
        log_total = row_max + jnp.log(jnp.sum(jnp.exp(scores - row_max), axis=-1, keepdims=True))
        weights_low = jnp.exp(scores - log_total).astype(jnp.bfloat16)
        mixture = jnp.einsum(
            "hqk,khd->qhd", weights_low, value_heads, preferred_element_type=jnp.float32
        )
        mixture = mixture.reshape(row_count, features).astype(jnp.bfloat16)
        attended = (
            jnp.dot(mixture, output_full, preferred_element_type=jnp.float32) + bias_values[4]
        )
        residual_one = inputs + attended
        normed_two, norm_two_pull = jax.vjp(
            layer_norm, residual_one, gain_values[1], bias_values[1]
        )
        hidden_low = normed_two.astype(jnp.bfloat16)
        hidden_pre = (
            jnp.dot(hidden_low, hidden_full[0], preferred_element_type=jnp.float32) + bias_values[5]
        )
        activated, gelu_pull = jax.vjp(jax.nn.gelu, hidden_pre)
        active_low = activated.astype(jnp.bfloat16)
        result = residual_one + (
            jnp.dot(active_low, hidden_full[1], preferred_element_type=jnp.float32) + bias_values[6]
        )
        outputs.append(result.astype(jnp.bfloat16))
        live_rows = (segment_own >= 0).astype(jnp.bfloat16)[:, None]
        out_grad = cotangent[micro_index, 0] * live_rows
        out_grad_wide = out_grad.astype(jnp.float32)
        active_grad = jnp.dot(out_grad, hidden_full[1].T, preferred_element_type=jnp.float32)
        pre_grad = gelu_pull(active_grad)[0].astype(jnp.bfloat16)
        normed_two_grad = jnp.dot(pre_grad, hidden_full[0].T, preferred_element_type=jnp.float32)
        residual_part, gain_two, offset_two = norm_two_pull(normed_two_grad)
        residual_grad = out_grad_wide + residual_part
        residual_low = residual_grad.astype(jnp.bfloat16)
        mixture_grad = jnp.dot(residual_low, output_full.T, preferred_element_type=jnp.float32)
        mixture_grad = mixture_grad.astype(jnp.bfloat16).reshape(row_count, HEADS, head_size)
        raw_again = (
            jnp.einsum("qhd,khd->hqk", query_heads, key_heads, preferred_element_type=jnp.float32)
            * score_scale
        )
        weights_wide = jnp.exp(jnp.where(same_set, raw_again, -1e30) - log_total)
        weight_grads = jnp.einsum(
            "qhd,khd->hqk", mixture_grad, value_heads, preferred_element_type=jnp.float32
        )
        centred = jnp.sum(weights_wide * weight_grads, axis=-1, keepdims=True)
        score_grads = (weights_wide * (weight_grads - centred)).astype(jnp.bfloat16)
        query_grad = (
            jnp.einsum("hqk,khd->qhd", score_grads, key_heads, preferred_element_type=jnp.float32)
            * score_scale
        )
        query_grad = query_grad.astype(jnp.bfloat16).reshape(row_count, features)
        weights_again = weights_wide.astype(jnp.bfloat16)
        key_part = (
            jnp.einsum("hqk,qhd->khd", score_grads, query_heads, preferred_element_type=jnp.float32)
            * score_scale
        )
        value_part = jnp.einsum(
            "hqk,qhd->khd", weights_again, mixture_grad, preferred_element_type=jnp.float32
        )
        key_grad, value_grad = (
            lax.psum_scatter(
                key_part.reshape(length, features).astype(jnp.bfloat16),
                "row",
                scatter_dimension=0,
                tiled=True,
            ).astype(jnp.float32),
            lax.psum_scatter(
                value_part.reshape(length, features).astype(jnp.bfloat16),
                "row",
                scatter_dimension=0,
                tiled=True,
            ).astype(jnp.float32),
        )
        key_low = key_grad.astype(jnp.bfloat16)
        value_low = value_grad.astype(jnp.bfloat16)
        projection_grads = jnp.stack([query_grad, key_low, value_low])
        attn_total = attn_total + jnp.einsum(
            "rd,cre->cde", normed_low, projection_grads, preferred_element_type=jnp.float32
        )
        output_total = output_total + jnp.dot(
            mixture.T, residual_low, preferred_element_type=jnp.float32
        )
        hidden_total = hidden_total + jnp.stack(
            [
                jnp.dot(hidden_low.T, pre_grad, preferred_element_type=jnp.float32),
                jnp.dot(active_low.T, out_grad, preferred_element_type=jnp.float32),
            ]
        )
        normed_one_grad = jnp.einsum(
            "cre,cde->rd", projection_grads, attention_full, preferred_element_type=jnp.float32
        )
        input_part, gain_one, offset_one = norm_one_pull(normed_one_grad)
        input_grads.append(residual_grad + input_part)
        gain_total = gain_total + jnp.stack([gain_one, gain_two])
        bias_total = bias_total + jnp.stack(
            [
                offset_one,
                offset_two,
                jnp.sum(query_grad.astype(jnp.float32), axis=0),
                jnp.sum(value_low.astype(jnp.float32), axis=0),
                jnp.sum(residual_low.astype(jnp.float32), axis=0),
                jnp.sum(pre_grad.astype(jnp.float32), axis=0),
                jnp.sum(out_grad_wide, axis=0),
            ]
        )
    attn_grads, output_grads, hidden_grads, gain_grads, bias_grads = (
        lax.psum_scatter(attn_total, ("seq", "row"), scatter_dimension=1, tiled=True),
        lax.psum_scatter(output_total, ("seq", "row"), scatter_dimension=0, tiled=True),
        lax.psum_scatter(hidden_total, ("seq", "row"), scatter_dimension=1, tiled=True),
        lax.psum_scatter(gain_total, ("seq", "row"), scatter_dimension=1, tiled=True),
        lax.psum_scatter(bias_total, ("seq", "row"), scatter_dimension=1, tiled=True),
    )
    return (
        jnp.stack(outputs)[:, None],
        jnp.stack(input_grads)[:, None],
        attn_grads,
        output_grads,
        hidden_grads,
        gain_grads,
        bias_grads,
    )


def solution(mesh):
    def on_mesh(latents, *rest):
        shares_pair = mesh.shape["row"] == latents.shape[0] == 2
        fits = mesh.size == 1 << len(ORDERS[0]) and latents.shape[1] == mesh.shape["seq"]
        return shard_over(whole_sequence if shares_pair and fits else on_device)(latents, *rest)

    def shard_over(function):
        return jax.shard_map(
            function,
            mesh=mesh,
            in_specs=(
                P(None, "seq", "row", None),
                P(None, "seq", None),
                P(None, ("seq", "row"), None),
                P(("seq", "row"), None),
                P(None, ("seq", "row"), None),
                P(None, ("seq", "row")),
                P(None, ("seq", "row")),
                P(None, "seq", "row", None),
            ),
            out_specs=(
                P(None, "seq", "row", None),
                P(None, "seq", "row", None),
                P(None, ("seq", "row"), None),
                P(("seq", "row"), None),
                P(None, ("seq", "row"), None),
                P(None, ("seq", "row")),
                P(None, ("seq", "row")),
            ),
            check_vma=False,
        )

    return on_mesh
```

```python
import functools
import math

import jax
import jax.numpy as jnp
from jax import lax
from jax.experimental import pallas as pl
from jax.experimental.pallas import tpu as pltpu
from jax.sharding import PartitionSpec as P

HEADS = 8
EPSILON = 1e-05
AXES = ("seq", "row")
VMEM_LIMIT = 64 << 20
STEPS = 2
NN = (((1,), (0,)), ((), ()))
NT = (((1,), (1,)), ((), ()))
TN = (((0,), (0,)), ((), ()))
ORDERS = ((16, 1, 8, 4, 2), (16, 1, 4, 8, 2))


def offset_of(order, position):
    offset = 0
    for bit, mask in enumerate(order):
        if position >> bit & 1:
            offset ^= mask
    return offset


def dot(left, right, dims=NN):
    return lax.dot_general(left, right, dims, preferred_element_type=jnp.float32)


def shift(array, mask, count):
    return lax.ppermute(array, AXES, [(i, i ^ mask) for i in range(count)])


def place_weights(me, order, sources, weight_ref, column, sem):
    depth = weight_ref.shape[1] >> len(order)
    width = sources[0].shape[-1]
    held = sources[0].shape[0]
    for position in range(len(sources) * held):
        owner = me ^ offset_of(order, position)
        rows = pl.ds(pl.multiple_of(owner * depth, depth), depth)
        for matrix in range(3):
            pltpu.make_async_copy(
                sources[position // held].at[position % held, pl.ds(matrix * depth, depth), :],
                weight_ref.at[matrix, rows, pl.ds(column, width)],
                sem,
            ).start()


def normalize(rows):
    mean = jnp.mean(rows, axis=-1, keepdims=True)
    centre = rows - mean
    spread = jnp.mean(centre * centre, axis=-1, keepdims=True)
    scale = lax.rsqrt(spread + EPSILON)
    return centre * scale, scale


def column_sum(rows):
    return jnp.sum(rows.astype(jnp.float32), axis=0, keepdims=True)


def project(normed_ref, w_ref, vec_ref, qkv_ref, column):
    width = qkv_ref.shape[-1]
    for matrix, bias in ((0, 4), (1, None), (2, 5)):
        out = dot(normed_ref[...], w_ref[matrix])
        if bias is not None:
            out = out + vec_ref[bias : bias + 1, column : column + width]
        qkv_ref[matrix] = out.astype(jnp.bfloat16)


def project_first_kernel(me_ref, own_in, first_in, second_in, *refs):
    sources = refs[:4]
    normed_out, qkv_out, vec_ref, other_out, weight_out, *refs = refs[4:]
    x_ref, normed_ref, qkv_ref, w_ref, block_ref, x_sem, w_sem, v_sem, out_sem = refs
    me = me_ref[0]
    rank = me & 1
    half_rows, features = x_ref.shape[1:]
    width = w_ref.shape[2]
    depth = features >> len(ORDERS[0])
    count, rows = block_ref.shape[:2]
    held = sources[0].shape[0]
    for position in range(count):
        pltpu.make_async_copy(
            sources[position // held].at[position % held, pl.ds(3 * depth, rows), pl.ds(0, block_ref.shape[2])],
            block_ref.at[me ^ offset_of(ORDERS[0], position)],
            v_sem,
        ).start()
    x_in = [
        pltpu.make_async_copy(own_in.at[rank], x_ref.at[0], x_sem.at[0]),
        pltpu.make_async_copy(first_in, x_ref.at[1, pl.ds(0, first_in.shape[0])], x_sem.at[1]),
        pltpu.make_async_copy(second_in, x_ref.at[1, pl.ds(first_in.shape[0], second_in.shape[0])], x_sem.at[2]),
    ]
    for copy in x_in:
        copy.start()
    for matrix in range(3):
        place_matrix(me, ORDERS[0], sources, matrix, w_ref, 0, w_sem.at[matrix])
    outs = []

    def send(source, target):
        outs.append(pltpu.make_async_copy(source, target, out_sem.at[len(outs)]))
        outs[-1].start()

    def norm(half):
        normed, _ = normalize(x_ref[half].astype(jnp.float32))
        normed_ref[half] = (normed * vec_ref[0:1] + vec_ref[2:3]).astype(jnp.bfloat16)

    def product(half, matrix):
        out = dot(normed_ref[half], w_ref[matrix])
        if matrix != 1:
            bias = 4 + matrix // 2
            out = out + vec_ref[bias : bias + 1, 0:width]
        qkv_ref[half, matrix] = out.astype(jnp.bfloat16)

    def rows_of(half):
        return pl.ds(pl.multiple_of((half ^ rank) * half_rows, half_rows), half_rows)

    pltpu.make_async_copy(block_ref, block_ref, v_sem).wait()
    for owner in range(count):
        vec_ref[:, owner * depth : (owner + 1) * depth] = block_ref[owner, :, 0:depth].astype(jnp.float32)
    x_in[0].wait()
    norm(0)
    for matrix in range(3):
        pltpu.make_async_copy(w_ref.at[matrix], w_ref.at[matrix], w_sem.at[matrix]).wait()
    x_in[1].wait()
    x_in[2].wait()
    product(0, 0)
    norm(1)
    product(0, 1)
    product(0, 2)
    send(x_ref.at[1], other_out)
    send(w_ref, weight_out)
    send(normed_ref.at[0], normed_out.at[rows_of(0)])
    send(normed_ref.at[1], normed_out.at[rows_of(1)])
    send(qkv_ref.at[0], qkv_out.at[:, rows_of(0), :])
    for matrix in range(3):
        product(1, matrix)
    send(qkv_ref.at[1], qkv_out.at[:, rows_of(1), :])
    for copy in outs:
        copy.wait()


def project_next_kernel(me_ref, normed_ref, vec_ref, *refs):
    *sources, qkv_ref, weight_ref, w_ref, sem = refs
    step = pl.program_id(0)

    @pl.when(step == 0)
    def _():
        place_weights(me_ref[0], ORDERS[1], sources, w_ref, 0, sem)
        pltpu.make_async_copy(w_ref, w_ref, sem).wait()
        pltpu.make_async_copy(w_ref, weight_ref, sem).start()

    project(normed_ref, w_ref, vec_ref, qkv_ref, qkv_ref.shape[-1])

    @pl.when(step == 1)
    def _():
        pltpu.make_async_copy(w_ref, weight_ref, sem).wait()


def key_ranges(length):
    quarter = length // 4
    return ((0, 2 * quarter), (0, length), (quarter, length), (quarter, length))


def attend_kernel(scale, q_ref, k_ref, v_ref, column_ref, row_ref, mix_ref, prob_ref, inverse_ref):
    length = q_ref.shape[1]
    tile = length // 8
    ranges = [(row, *key_ranges(length)[2 * row // (length // 2)]) for row in range(0, length, tile)]

    def score(index):
        row, first, last = ranges[index]
        return dot(q_ref[0, row : row + tile, :], k_ref[0, first:last, :], NT)

    def mix(index, low, inverse):
        row, first, last = ranges[index]
        mix_ref[row : row + tile, :] = (dot(low, v_ref[0, first:last, :]) * inverse).astype(jnp.bfloat16)

    scores, before = score(0), None
    for index, (row, first, last) in enumerate(ranges):
        following = score(index + 1) if index + 1 < len(ranges) else None
        rows = slice(row, row + tile)
        same = column_ref[rows, :] == row_ref[0, :, first:last]
        scores = jnp.where(same, scores, -1e30)
        top = jnp.max(scores, axis=-1, keepdims=True)
        expo = jnp.exp2((scores - top) * (scale * math.log2(math.e)))
        low = expo.astype(jnp.bfloat16)
        inverse = 1.0 / jnp.sum(expo, axis=-1, keepdims=True)
        prob_ref[0, rows, first:last] = low
        inverse_ref[0, rows, :] = jnp.broadcast_to(inverse, (tile, inverse_ref.shape[2]))
        if before is not None:
            mix(*before)
        before, scores = (index, low, inverse), following
    mix(*before)


def attend_back_kernel(
    scale, q_ref, k_ref, v_ref, prob_ref, mix_ref, mixg_ref, inverse_ref, out_ref, sum_ref, key_acc, value_acc
):
    length = q_ref.shape[1]
    quarter = length // 4
    key_acc[...] = jnp.zeros_like(key_acc)
    value_acc[...] = jnp.zeros_like(value_acc)
    mix_grad = (mixg_ref[...].astype(jnp.float32) * inverse_ref[0]).astype(jnp.bfloat16)
    centred = jnp.sum(mix_grad.astype(jnp.float32) * mix_ref[...].astype(jnp.float32), axis=-1, keepdims=True)
    ranges = key_ranges(length)

    def grads_of(index):
        first, last = ranges[index]
        return dot(mix_grad[index * quarter : (index + 1) * quarter], v_ref[0, first:last, :], NT)

    def spread(index, score_grads, low):
        first, last = ranges[index]
        rows = slice(index * quarter, (index + 1) * quarter)
        out_ref[0, rows, :] = (dot(score_grads, k_ref[0, first:last, :]) * scale).astype(jnp.bfloat16)
        key_acc[first:last, :] += dot(score_grads, q_ref[0, rows, :], TN)
        value_acc[first:last, :] += dot(low, mix_grad[rows], TN)

    grads, before = grads_of(0), None
    for index, (first, last) in enumerate(ranges):
        following = grads_of(index + 1) if index + 1 < len(ranges) else None
        rows = slice(index * quarter, (index + 1) * quarter)
        low = prob_ref[0, rows, first:last]
        score_grads = (low.astype(jnp.float32) * (grads - centred[rows])).astype(jnp.bfloat16)
        if before is not None:
            spread(*before)
        before, grads = (index, score_grads, low), following
    spread(*before)
    out_ref[1] = (key_acc[...] * scale).astype(jnp.bfloat16)
    out_ref[2] = value_acc[...].astype(jnp.bfloat16)
    sum_ref[...] = jnp.zeros_like(sum_ref)
    sum_ref[0:1] = column_sum(out_ref[0])
    sum_ref[1:2] = column_sum(out_ref[2])


def project_back_kernel(order, me_ref, normed_ref, grad_ref, keep_ref, send_ref, stage_ref, sems):
    step = pl.program_id(0)
    stage_ref[step] = dot(normed_ref[...], grad_ref[0], TN).astype(jnp.bfloat16)
    for matrix in range(3):

        @pl.when(step == matrix)
        def _():
            stage = stage_ref.at[matrix]
            collect_matrix(me_ref[0], order, stage, matrix, keep_ref, send_ref, 0, sems.at[matrix])

    @pl.when(step == 2)
    def _():
        for matrix in range(3):
            stage = stage_ref.at[matrix]
            pltpu.make_async_copy(stage, stage, sems.at[matrix]).wait()


def place_matrix(me, order, sources, matrix, weight_ref, column, sem):
    depth = weight_ref.shape[1] >> len(order)
    width = sources[0].shape[-1]
    held = sources[0].shape[0]
    for position in range(len(sources) * held):
        owner = me ^ offset_of(order, position)
        rows = pl.ds(pl.multiple_of(owner * depth, depth), depth)
        pltpu.make_async_copy(
            sources[position // held].at[position % held, pl.ds(matrix * depth, depth), :],
            weight_ref.at[matrix, rows, pl.ds(column, width)],
            sem,
        ).start()


def collect_matrix(me, order, stage_ref, matrix, keep_ref, send_ref, base, sem):
    half = 1 << len(order) - 1
    depth = stage_ref.shape[0] >> len(order)
    for position in reversed(range(2 * half)):
        target = keep_ref if position < half else send_ref
        owner = me ^ offset_of(order, position)
        rows = pl.ds(pl.multiple_of(owner * depth, depth), depth)
        place = base + (position % half * 3 + matrix) * depth
        pltpu.make_async_copy(stage_ref.at[rows, :], target.at[pl.ds(place, depth), :], sem).start()


def feed_kernel(
    me_ref, x_own_ref, x_other_ref, cot_own_ref, cot_other_ref, mix0_ref, mix1_ref, column_ref, vec_ref, *refs
):
    sources = refs[:8]
    result_ref, result_other_ref, resg_ref, mixg_ref, sum_ref, keep_ref, send_ref, *refs = refs[8:]
    (
        w_ref, x_ref, cot_ref, mix_ref, hid_ref, act_ref, og_ref, pre_ref, res_ref, resid_ref, slope_ref,
        out_ref, resg_out, mixg_out, stage_ref, w_sem, in_sem, out_sem, g_sem,
    ) = refs
    me = me_ref[0]
    rank = me & 1
    half_rows, features = x_other_ref.shape
    width = features // 2
    places = [pl.multiple_of((half ^ rank) * half_rows, half_rows) for half in range(2)]
    rows = [pl.ds(place, half_rows) for place in places]

    def weights(matrix):
        for half in range(2):
            place_matrix(me, ORDERS[half], sources[4 * half : 4 * half + 4], matrix, w_ref, half * width, w_sem.at[matrix])

    def weights_here(matrix):
        pltpu.make_async_copy(w_ref.at[matrix], w_ref.at[matrix], w_sem.at[matrix]).wait()

    mix_in = [
        pltpu.make_async_copy(ref, mix_ref.at[:, pl.ds(half * width, width)], in_sem.at[half])
        for half, ref in enumerate((mix0_ref, mix1_ref))
    ]
    x_in = [
        pltpu.make_async_copy(ref, x_ref.at[half], in_sem.at[2 + half])
        for half, ref in enumerate((x_own_ref.at[rank], x_other_ref))
    ]
    cot_in = [
        pltpu.make_async_copy(ref, cot_ref.at[half], in_sem.at[4 + half])
        for half, ref in enumerate((cot_own_ref.at[rank], cot_other_ref))
    ]
    for copy in mix_in:
        copy.start()
    weights(0)
    x_in[0].start()
    x_in[1].start()
    weights(1)
    cot_in[0].start()
    cot_in[1].start()
    weights(2)
    sums = [jnp.zeros((1, features), jnp.float32)] * 5
    out_copies = []

    def attend_out(half):
        x_in[half].wait()
        resid_ref[half] = x_ref[half].astype(jnp.float32) + dot(mix_ref[rows[half], :], w_ref[0]) + vec_ref[6:7]

    def norm_two(half):
        normed, _ = normalize(resid_ref[half])
        hid_ref[half] = (normed * vec_ref[1:2] + vec_ref[3:4]).astype(jnp.bfloat16)

    def first(half):
        return dot(hid_ref[half], w_ref[1]) + vec_ref[7:8]

    def gelu(half, pre):
        square = pre * pre
        tanh = jnp.tanh(0.7978845608 * pre * (1.0 + 0.044715 * square))
        upper = 0.5 * (1.0 + tanh)
        act_ref[half] = (pre * upper).astype(jnp.bfloat16)
        slope_ref[half] = upper * (
            1.0 + pre * (1.0 - tanh) * (0.7978845608 + (3 * 0.044715 * 0.7978845608) * square)
        )

    def mask(half):
        cot_in[half].wait()
        live = (column_ref[rows[half], :] >= 0).astype(jnp.float32)
        og_ref[half] = (cot_ref[half].astype(jnp.float32) * live).astype(jnp.bfloat16)

    def second(half):
        result = resid_ref[half] + dot(act_ref[half], w_ref[2]) + vec_ref[8:9]
        out_ref[half] = result.astype(jnp.bfloat16)
        target = (result_ref.at[rank], result_other_ref)[half]
        out_copies.append(pltpu.make_async_copy(out_ref.at[half], target, out_sem.at[half]))
        out_copies[-1].start()

    def second_back(half):
        return dot(og_ref[half], w_ref[2], NT)

    def gelu_back(half, grad):
        pre_ref[half] = (grad * slope_ref[half]).astype(jnp.bfloat16)
        sums[3] = sums[3] + column_sum(pre_ref[half])
        sums[4] = sums[4] + column_sum(og_ref[half])

    def first_back(half):
        return dot(pre_ref[half], w_ref[1], NT)

    def norm_back(half, grad):
        normed, inverse = normalize(resid_ref[half])
        sums[0] = sums[0] + column_sum(grad * normed)
        sums[1] = sums[1] + column_sum(grad)
        scaled = grad * vec_ref[1:2]
        resg = og_ref[half].astype(jnp.float32) + inverse * (
            scaled
            - jnp.mean(scaled, axis=-1, keepdims=True)
            - normed * jnp.mean(scaled * normed, axis=-1, keepdims=True)
        )
        resg_out[half] = resg
        res_ref[rows[half], :] = resg.astype(jnp.bfloat16)
        sums[2] = sums[2] + column_sum(resg.astype(jnp.bfloat16))

    def out_back(half):
        mixg_out[half] = dot(res_ref[rows[half], :], w_ref[0], NT).astype(jnp.bfloat16)
        for source, target, number in (
            (resg_out.at[half], resg_ref.at[half], 2 + half), (mixg_out.at[half], mixg_ref.at[rows[half]], 4 + half)
        ):
            out_copies.append(pltpu.make_async_copy(source, target, out_sem.at[number]))
            out_copies[-1].start()

    def weight_grad(matrix, half):
        columns = slice(half * width, (half + 1) * width)
        if matrix == 0:
            total = dot(mix_ref[...], res_ref[:, columns], TN)
        else:
            left, right = ((hid_ref, pre_ref), (act_ref, og_ref))[matrix - 1]
            total = dot(left[0], right[0, :, columns], TN) + dot(left[1], right[1, :, columns], TN)
        stage = stage_ref.at[half, matrix]
        stage_ref[half, matrix] = total.astype(jnp.bfloat16)
        collect_matrix(
            me, ORDERS[half], stage, matrix, keep_ref, send_ref, half * keep_ref.shape[0] // 2, g_sem.at[half, matrix]
        )

    for copy in mix_in:
        copy.wait()
    weights_here(0)
    attend_out(0)
    attend_out(1)
    norm_two(0)
    weights_here(1)
    pre0 = first(0)
    norm_two(1)
    pre1 = first(1)
    gelu(0, pre0)
    mask(0)
    weights_here(2)
    second(0)
    grad0 = second_back(0)
    gelu(1, pre1)
    mask(1)
    second(1)
    grad1 = second_back(1)
    gelu_back(0, grad0)
    grad0 = first_back(0)
    gelu_back(1, grad1)
    weight_grad(2, 0)
    grad1 = first_back(1)
    norm_back(0, grad0)
    weight_grad(2, 1)
    out_back(0)
    weight_grad(1, 0)
    norm_back(1, grad1)
    weight_grad(1, 1)
    out_back(1)
    weight_grad(0, 0)
    weight_grad(0, 1)
    sum_ref[...] = jnp.zeros_like(sum_ref)
    for row, value in enumerate(sums):
        sum_ref[row : row + 1] = value
    for copy in out_copies:
        copy.wait()
    for half in range(2):
        for matrix in range(3):
            stage = stage_ref.at[half, matrix]
            pltpu.make_async_copy(stage, stage, g_sem.at[half, matrix]).wait()


def finish_kernel(
    flip, me_ref, x_in, resg_in, grad0_ref, grad1_ref, w0_ref, w1_ref, vec_ref, *refs
):
    earlier = refs[: 0 if flip else 4]
    out_ref, sum_ref, x_ref, resg_ref, grad_ref, w_ref, in_sem, sems, *row_refs = refs[len(earlier) :]
    rank = me_ref[0] & 1
    half_rows, features = x_ref.shape
    width = features // 2
    rows = pl.ds(pl.multiple_of((rank ^ flip) * half_rows, half_rows), half_rows)
    copies = []
    for matrix in range(3):
        for half, (grad, weight) in enumerate(((grad0_ref, w0_ref), (grad1_ref, w1_ref))):
            columns = pl.ds(half * width, width)
            copies.append([
                pltpu.make_async_copy(grad.at[matrix, rows, :], grad_ref.at[matrix, :, columns], sems.at[matrix, half]),
                pltpu.make_async_copy(weight.at[matrix], w_ref.at[matrix, :, columns], sems.at[matrix, 2 + half]),
            ])
    later = [
        pltpu.make_async_copy(x_in if flip else x_in.at[rank], x_ref, in_sem.at[0]),
        pltpu.make_async_copy(resg_in.at[flip], resg_ref, in_sem.at[1]),
    ]
    for copy in sum(copies, []) + later:
        copy.start()
    normed_grad = None
    for matrix in range(3):
        for copy in copies[2 * matrix] + copies[2 * matrix + 1]:
            copy.wait()
        term = dot(grad_ref[matrix], w_ref[matrix], NT)
        normed_grad = term if normed_grad is None else normed_grad + term
    for copy in later:
        copy.wait()
    normed, inverse = normalize(x_ref[...].astype(jnp.float32))
    gain_sum, bias_sum = column_sum(normed_grad * normed), column_sum(normed_grad)
    if flip:
        sum_ref[...] = jnp.zeros_like(sum_ref)
        sum_ref[0:1] = gain_sum
        sum_ref[1:2] = bias_sum
    else:
        feed_ref, other_ref, s0_ref, s1_ref = earlier
        (row_ref,) = row_refs
        row_ref[...] = jnp.zeros_like(row_ref)
        row_ref[0:1] = gain_sum + other_ref[0:1]
        row_ref[1:2] = feed_ref[0:1]
        row_ref[2:3] = bias_sum + other_ref[1:2]
        row_ref[3:4] = feed_ref[1:2]
        row_ref[6:9] = feed_ref[2:5]
        for half, sums in enumerate((s0_ref, s1_ref)):
            columns = slice(half * width, (half + 1) * width)
            row_ref[4:6, columns] = sums[0:2]
            sum_ref[half * 16 : (half + 1) * 16, :] = row_ref[:, columns].astype(jnp.bfloat16)
    scaled = normed_grad * vec_ref[0:1]
    total = resg_ref[...] + inverse * (
        scaled
        - jnp.mean(scaled, axis=-1, keepdims=True)
        - normed * jnp.mean(scaled * normed, axis=-1, keepdims=True)
    )
    out_ref[...] = total.reshape(out_ref.shape).astype(out_ref.dtype)


def double_first_kernel(me_ref, own_ref, own_vec_ref, got_ref, got_vec_ref, out_ref):
    matrices, depth, features = own_ref.shape
    width = features // 2
    base = matrices * depth
    out_ref[:, :, base:, :] = jnp.zeros_like(out_ref[:, :, base:, :])
    for block, (part, vectors) in enumerate(((own_ref, own_vec_ref), (got_ref, got_vec_ref))):
        for half in range(2):
            for matrix in range(matrices):
                rows = slice(matrix * depth, (matrix + 1) * depth)
                out_ref[block, half, rows, :] = part[matrix, :, half * width : (half + 1) * width]
        out_ref[block, 0, base : base + vectors.shape[0], 0:depth] = vectors[...]


def pack_next_kernel(me_ref, output_ref, hidden_ref, out_ref, sems):
    depth, features = output_ref.shape
    width = features // 2
    copies = []
    for half in range(2):
        columns = pl.ds(half * width, width)
        sources = [output_ref.at[:, columns]] + [hidden_ref.at[matrix, :, columns] for matrix in range(2)]
        for matrix, source in enumerate(sources):
            target = out_ref.at[0, half, pl.ds(matrix * depth, depth), :]
            copies.append(pltpu.make_async_copy(source, target, sems.at[len(copies)]))
    for copy in copies:
        copy.start()
    for copy in copies:
        copy.wait()


def join_kernel(moves, me_ref, *refs):
    for source, source_index, target, target_index in moves:
        refs[target][target_index] = refs[source][source_index]


def join_out_kernel(moves, me_ref, *refs):
    *refs, sems = refs
    copies = [
        pltpu.make_async_copy(refs[source].at[source_index], refs[target].at[target_index], sems.at[number])
        for number, (source, source_index, target, target_index) in enumerate(moves)
    ]
    for copy in copies:
        copy.start()
    for copy in copies:
        copy.wait()


def select_kernel(me_ref, rows_ref, *refs):
    row = 0
    for out_ref in refs[:-1]:
        out_ref[...] = rows_ref[0, row : row + out_ref.shape[0], :]
        row += out_ref.shape[0]
    refs[-1][...] = jnp.zeros_like(refs[-1])


def total_of(refs, width):
    total = None
    for ref in refs:
        term = ref[...].astype(jnp.float32).reshape(-1, width)
        total = term if total is None else total + term
    return total


def combine_kernel(sums, me_ref, *refs):
    for first, last, output, row in sums:
        out_ref = refs[output]
        total = total_of(refs[first:last], out_ref.shape[-1])
        out_ref[row : row + total.shape[0], :] = total.astype(out_ref.dtype)


def final_kernel(inputs, me_ref, *refs):
    outs = refs[2 * inputs :]
    depth, features = outs[0].shape[1:]
    width = features // 2
    for half in range(2):
        total = total_of(refs[half * inputs : (half + 1) * inputs], width)
        row = 0
        for out_ref in outs:
            matrices = out_ref.shape[0]
            piece = total[row : row + matrices * depth].reshape(matrices, depth, width)
            out_ref[:, :, half * width : (half + 1) * width] = piece
            row += matrices * depth


def final_vector_kernel(inputs, vectors, me_ref, *refs):
    blocks, terms = refs[: 2 * inputs], refs[2 * inputs : 2 * inputs + vectors]
    out_ref, gain_ref, bias_ref = refs[2 * inputs + vectors :]
    final_kernel(inputs, me_ref, *blocks, out_ref)
    picked = own_columns(me_ref, terms, gain_ref.shape[1])
    gains = gain_ref.shape[0]
    gain_ref[...] = picked[0:gains]
    bias_ref[...] = picked[gains : gains + bias_ref.shape[0]]


def own_columns(me_ref, terms, depth):
    rows = terms[0].shape[0] // 2
    width = terms[0].shape[-1]
    total = total_of(terms, width)
    lane = lax.broadcasted_iota(jnp.int32, (width, depth), 0)
    column = lax.broadcasted_iota(jnp.int32, (width, depth), 1)
    place = me_ref[0] * depth
    picked = None
    for half in range(2):
        choose = (lane + half * width == column + place).astype(jnp.float32)
        part = lax.dot_general(
            total[half * rows : (half + 1) * rows], choose, NN, precision=lax.Precision.HIGHEST,
            preferred_element_type=jnp.float32,
        )
        picked = part if picked is None else picked + part
    return picked


ANY = pl.BlockSpec(memory_space=pl.ANY)
VMEM = pl.BlockSpec(memory_space=pltpu.VMEM)
HBM = pl.BlockSpec(memory_space=pltpu.HBM)
SMALL_LIMIT = 24 << 20


def call(kernel, me, grid, operands, out_specs, out_shape, scratch=(), flops=1e6, moved=1e6, after=(), limit=VMEM_LIMIT):
    taken = len(operands) + 1
    after = list(after)
    ordered = ANY if limit == SMALL_LIMIT else HBM

    def body(*refs):
        kernel(*refs[:taken], *refs[taken + len(after) :])

    return pl.pallas_call(
        body,
        grid_spec=pltpu.PrefetchScalarGridSpec(
            num_scalar_prefetch=1,
            grid=grid,
            in_specs=[spec for _, spec in operands] + [ordered] * len(after),
            out_specs=out_specs,
            scratch_shapes=list(scratch),
        ),
        out_shape=out_shape,
        compiler_params=pltpu.CompilerParams(
            dimension_semantics=("arbitrary",) * len(grid), vmem_limit_bytes=limit
        ),
        cost_estimate=pl.CostEstimate(flops=int(flops), bytes_accessed=int(moved), transcendentals=0),
    )(me, *[array for array, _ in operands], *after)


def struct(shape, dtype=jnp.bfloat16):
    return jax.ShapeDtypeStruct(shape, dtype)


def whole(shape):
    return pl.BlockSpec(shape, lambda *_: (0,) * len(shape))


def join(me, arrays, moves, shapes, after=(), kind="local"):
    moves = [(i, source, len(arrays) + o, target) for i, source, o, target in moves]
    place = whole if kind == "far" else lambda shape: VMEM
    kernel = functools.partial(join_out_kernel if kind == "out" else join_kernel, moves)
    return call(
        kernel, me, (1,), [(a, place(a.shape)) for a in arrays],
        [HBM if kind == "out" else place(s) for s in shapes], [struct(s) for s in shapes],
        [pltpu.SemaphoreType.DMA((len(moves),))] if kind == "out" else [], after=after,
        limit=VMEM_LIMIT if kind == "far" else SMALL_LIMIT,
    )


def part(array, start, size, tall):
    return array, pl.BlockSpec((size * tall, array.shape[-1]), lambda i, me: (start // size, 0))


def combine(me, outputs, after=(), flops=1e6, dtype=jnp.bfloat16):
    operands, sums, shapes = [], [], []
    count = sum(len(terms) for group in outputs for terms in group)
    for number, group in enumerate(outputs):
        row = 0
        for terms in group:
            first = len(operands)
            operands.extend(terms)
            sums.append((first, len(operands), count + number, row))
            row += terms[0][1].block_shape[0]
        shapes.append((row, group[0][0][0].shape[-1]))
    steps = STEPS if all(len(group) == 1 for group in outputs) else 1

    def cut_rows(spec):
        rows, columns = spec.block_shape
        index = spec.index_map(0, None)[0]
        return pl.BlockSpec((rows // steps, columns), lambda i, me: (index * steps + i, 0))

    return call(
        functools.partial(combine_kernel, sums), me, (steps,), [(array, cut_rows(spec)) for array, spec in operands],
        [pl.BlockSpec((rows // steps, columns), lambda i, me: (i, 0)) for rows, columns in shapes],
        [struct(shape, dtype) for shape in shapes], flops=flops, after=after,
    )


def final(me, halves, depth, features, counts, vectors=()):
    shapes = [(matrices, depth, features) for matrices in counts]
    kernel = functools.partial(final_kernel, len(halves[0]))
    if vectors:
        kernel = functools.partial(final_vector_kernel, len(halves[0]), len(vectors))
        shapes.extend([(2, depth), (7, depth)])
    return call(
        kernel, me, (1,), halves[0] + halves[1] + list(vectors), [whole(s) for s in shapes],
        [struct(s, jnp.float32) for s in shapes],
    )


def whole_sequence(
    latents, segments, attention_weights, output_weight, hidden_weights, gains, biases, cotangent
):
    half_rows, features = latents.shape[2:]
    length = 2 * half_rows
    head_size = features // HEADS
    scale = 1.0 / math.sqrt(head_size)
    width = features // 2
    count = 1 << len(ORDERS[0])
    depth = features // count
    rank = lax.axis_index("row")
    device = (lax.axis_index("seq") * 2 + rank).astype(jnp.int32)
    me = device.reshape(1)
    bf16, f32 = jnp.bfloat16, jnp.float32
    dense = 2.0 * length * features * features
    tall = 3 * depth
    vector_rows = gains.shape[0] + biases.shape[0]
    padded = tall + 16

    def move(array, mask):
        return shift(array, mask, count)

    def double(held, got, after=()):
        return join(me, [held, got], [(0, 0, 0, 0), (1, 0, 0, 1)], [(2,) + held.shape[1:]], after)[0]

    def split(held, got, rows, after=(), kind="local"):
        moves, shapes = [], []
        for half in range(2):
            for source in range(2):
                for block in range(2):
                    moves.append((source, (block, half, pl.ds(0, rows[half])), half, 2 * source + block))
            shapes.append((4, rows[half], width))
        return join(me, [held, got], moves, shapes, after, kind)

    def append(held, got, after=(), kind="out"):
        moves, shapes = [], []
        for half in range(2):
            for source in range(2):
                moves.append((2 * half + source, pl.ds(0, 4), half, pl.ds(4 * source, 4)))
            shapes.append((8,) + held[half].shape[1:])
        return join(me, [held[0], got[0], held[1], got[1]], moves, shapes, after, kind)

    z_far, y, z_near, x, core = 16, 1, 8, 4, 2
    def pack(kernel, arrays, rows, scratch, after=()):
        return call(
            kernel, me, (1,), [(a, HBM) for a in arrays], VMEM, struct((1, 2, rows, width)), scratch, after=after,
            limit=SMALL_LIMIT,
        )

    latents_flat = latents[:, 0]
    cotangent_flat = cotangent[:, 0]

    def select(array, parts, after):
        shapes = [(half_rows * share // sum(parts), features) for share in parts]
        return call(
            select_kernel, me, (1,),
            [(array, pl.BlockSpec((1, half_rows, features), lambda i, me: (1 - (me[0] & 1), 0, 0)))],
            [whole(shape) for shape in shapes] + [VMEM], [struct(shape) for shape in shapes] + [struct((8, 128), f32)],
            after=after, limit=SMALL_LIMIT,
        )

    sems = lambda number: pltpu.SemaphoreType.DMA((number,))
    vectors_own = jnp.concatenate([gains, biases], axis=0)
    a1_got = (move(attention_weights, z_far), move(vectors_own, z_far))
    *x_send, x_token = select(latents_flat, (5, 3), [])
    a2 = call(
        double_first_kernel, me, (1,),
        [(a, VMEM) for a in (attention_weights, vectors_own, *a1_got)], VMEM, struct((2, 2, padded, width)),
        after=[x_token], limit=SMALL_LIMIT,
    )
    f1 = pack(pack_next_kernel, [output_weight, hidden_weights], tall, [sems(6)], [a2])
    a4 = split(a2, move(a2, y), (padded, tall), [f1])
    x_first = move(x_send[0], y)
    cot_send, cot_token = select(cotangent_flat, (1,), a4)
    f2 = double(f1, move(f1, z_far), [a4[0], cot_token])
    a8 = append(a4, (move(a4[0], z_near), move(a4[1], x)), [f2, x_first])
    a_core = [move(a, core) for a in a8]
    x_second = move(x_send[1], y)
    f4 = split(f2, move(f2, y), (tall, tall), a8, "out")
    a_far = join(
        me, [move(a8[0], x), move(a8[1], z_near)], [(h, pl.ds(0, 8), h, pl.ds(0, 8)) for h in range(2)],
        [a.shape for a in a8], [f4[0], x_second], "out",
    )
    a_far_core = [move(a, core) for a in a_far]
    attn_sources = [[a8[h], a_far[h], a_core[h], a_far_core[h]] for h in range(2)]

    segment_row = segments
    segment_column = lax.dynamic_index_in_dim(segments[:, 0], rank, 0, keepdims=False)[:, None]

    own = pl.BlockSpec((1, half_rows, features), lambda i, me: (me[0] & 1, 0, 0))
    local = pl.BlockSpec((half_rows, features), lambda i, me: (i ^ (me[0] & 1), 0))
    local3 = pl.BlockSpec((3, half_rows, width), lambda i, me: (0, i ^ (me[0] & 1), 0))
    rows_spec = whole((half_rows, features))
    low = lambda *shape: pltpu.VMEM(shape, bf16)
    dma = lambda *shape: pltpu.SemaphoreType.DMA(shape)
    w_scratch = pltpu.VMEM((3, features, width), bf16)
    w_struct = struct((3, features, width))
    normed_low, qkv0, vec, x_other, weight0 = call(
        project_first_kernel, me, (1,),
        [(a, HBM) for a in (latents_flat, x_first, x_second)] + [(a, ANY) for a in attn_sources[0]],
        [HBM, HBM, whole((16, features)), HBM, HBM],
        [struct((length, features)), struct((3, length, width)), struct((16, features), f32),
         struct((half_rows, features)), w_struct],
        [low(2, half_rows, features), low(2, half_rows, features), low(2, 3, half_rows, width), w_scratch,
         low(count, 16, 128), dma(3), dma(3), pltpu.SemaphoreType.DMA(()), dma(6)],
        1.5 * dense, 16e6, f4,
    )
    vec_op = (vec, whole((16, features)))
    cot_other = move(cot_send, y)
    f8 = append(f4, (move(f4[0], z_near), move(f4[1], x)), [vec], "far")
    f_core = [move(a, core) for a in f8]
    f_far = (move(f8[0], x), move(f8[1], z_near))
    qkv1, weight1 = call(
        project_next_kernel, me, (2,),
        [(normed_low, pl.BlockSpec((half_rows, features), lambda i, me: (i, 0))), vec_op]
        + [(a, ANY) for a in attn_sources[1]],
        [pl.BlockSpec((3, half_rows, width), lambda i, me: (0, i, 0)), ANY], [struct((3, length, width)), w_struct],
        [w_scratch, pltpu.SemaphoreType.DMA(())], 1.5 * dense, 8e6, f8,
    )

    heads = width // head_size
    head_specs = [
        pl.BlockSpec((1, length, head_size), functools.partial(lambda c, h, me: (c, 0, h), c)) for c in range(3)
    ]
    column_block = pl.BlockSpec((length, head_size), lambda h, me: (0, h))
    prob_block = pl.BlockSpec((1, length, length), lambda h, me: (h, 0, 0))
    inverse_block = pl.BlockSpec((1, length, head_size), lambda h, me: (h, 0, 0))
    segment_spec = pl.BlockSpec((1, 1, length), lambda h, me: (me[0] & 1, 0, 0))

    def attend(qkv, after):
        return call(
            lambda me_ref, *refs: attend_kernel(scale, *refs), me, (heads,),
            [(qkv, s) for s in head_specs] + [(segment_column, whole((length, 1))), (segment_row, segment_spec)],
            [column_block, prob_block, inverse_block],
            [struct((length, width)), struct((heads, length, length)), struct((heads, length, head_size), f32)], [],
            4 * dense, 30e6, after,
        )

    mix0, prob0, inverse0 = attend(qkv0, [qkv1])
    f_far_core = [move(a, core) for a in f_far]
    feed_sources = [[f8[h], f_far[h], f_core[h], f_far_core[h]] for h in range(2)]
    mix1, prob1, inverse1 = attend(qkv1, [mix0])

    keeps = [struct((count * tall, width))] * 2
    local_rows = pltpu.VMEM((2, half_rows, features), f32)
    result_own, result_other, residual_grad, mix_grad, feed_sums, fk, fs = call(
        feed_kernel, me, (1,),
        [(a, HBM) for a in (latents_flat, x_other, cotangent_flat, cot_other, mix0, mix1)]
        + [(segment_column, whole((length, 1))), vec_op] + [(a, ANY) for a in feed_sources[0] + feed_sources[1]],
        [HBM] * 4 + [whole((8, features))] + [ANY] * 2,
        [struct((2, half_rows, features)), struct((half_rows, features)), struct((2, half_rows, features), f32),
         struct((length, features)), struct((8, features), f32)] + keeps,
        [low(3, features, features), low(2, half_rows, features), low(2, half_rows, features), low(length, features)]
        + [low(2, half_rows, features)] * 4 + [low(length, features), local_rows, local_rows]
        + [low(2, half_rows, features), local_rows, low(2, half_rows, features), low(2, 3, features, width)]
        + [dma(3), dma(6), dma(6), dma(2, 3)],
        9 * dense, 30e6,
    )
    f_c = move(fs, core)
    result_back = move(result_other, y)

    def attend_back(qkv, prob, mix, inverse, half, after):
        return call(
            lambda me_ref, *refs: attend_back_kernel(scale, *refs), me, (heads,),
            [(qkv, s) for s in head_specs] + [(prob, prob_block), (mix, column_block),
             (mix_grad, pl.BlockSpec((length, head_size), lambda h, me: (0, h + half * heads))), (inverse, inverse_block)],
            [pl.BlockSpec((3, length, head_size), lambda h, me: (0, 0, h)), pl.BlockSpec((8, head_size), lambda h, me: (0, h))],
            [struct((3, length, width)), struct((8, width), f32)], [pltpu.VMEM((length, head_size), f32)] * 2, 8 * dense, 30e6, after,
        )

    def project_back(grad, order, after):
        return call(
            functools.partial(project_back_kernel, order), me, (3,),
            [(normed_low, whole((length, features))), (grad, pl.BlockSpec((1, length, width), lambda i, me: (i, 0, 0)))],
            [ANY, ANY], [struct((count // 2 * tall, width))] * 2,
            [w_scratch, dma(3)], 1.5 * dense, 8e6, after,
        )

    def finish(rows, flip, out_spec, out_struct, after, earlier=()):
        sum_struct = struct((8, features), f32) if flip else struct((32, width))
        return call(
            functools.partial(finish_kernel, flip), me, (1,),
            [(a, HBM) for a in (rows, residual_grad, qkv_grad0, qkv_grad1, weight0, weight1)] + [vec_op]
            + [(a, whole(a.shape)) for a in earlier],
            [out_spec, whole(sum_struct.shape)], [out_struct, sum_struct],
            [low(half_rows, features), pltpu.VMEM((half_rows, features), f32), low(3, half_rows, features),
             low(3, features, features), dma(2), dma(3, 4)] + [pltpu.VMEM((16, features), f32)] * (1 - flip),
            8 * dense, 20e6, after,
        )

    half_count = count // 2
    blocks = lambda array, start, size: part(array, start, size, tall)
    vector_part = lambda array, row: (array, pl.BlockSpec((32, width), lambda i, me: (row // 32, 0)))
    feed_first = lambda start, size, h: [blocks(a, h * half_count + start, size) for a in (fk, f_c)]
    qkv_grad0, sums0 = attend_back(qkv0, prob0, mix0, inverse0, 0, [])
    fs0, fs1 = combine(me, [[feed_first(8, 8, 0)], [feed_first(8, 8, 1)]], [qkv_grad0])
    f_s2 = (move(fs0, x), move(fs1, z_near))
    ak0, as0 = project_back(qkv_grad0, ORDERS[0], [fs0, fs1])
    a0_c = move(as0, core)
    qkv_grad1, sums1 = attend_back(qkv1, prob1, mix1, inverse1, 1, [ak0])
    terms = [feed_first(4, 4, h) + [blocks(f_s2[h], 4, 4)] for h in range(2)]
    ft0, ft1, at0 = combine(me, [[terms[0]], [terms[1]], [[blocks(ak0, 8, 8), blocks(a0_c, 8, 8)]]], [qkv_grad1])
    f_s3 = (move(ft0, z_near), move(ft1, x))
    a0_s2 = move(at0, x)
    ak1, as1 = project_back(qkv_grad1, ORDERS[1], [ft0, ft1, at0, result_back])
    a1_c = move(as1, core)
    feed_terms = lambda start, size: [
        feed_first(start, size, h) + [blocks(f_s2[h], start, size), blocks(f_s3[h], start, size)] for h in range(2)
    ]
    fu, = combine(me, [feed_terms(2, 2)], [ak1], 8 * dense)
    f_y = move(fu, y)
    at1, = combine(me, [[[blocks(ak1, 8, 8), blocks(a1_c, 8, 8)]]], [fu])
    a1_s2 = move(at1, z_near)
    latent_other, sums_other = finish(x_other, 1, rows_spec, struct((half_rows, features)), [at1])
    latent_back = move(latent_other, y)
    latent_out, vectors = finish(
        latents_flat, 0, own, struct((2, half_rows, features), f32), [latent_other, f_y],
        (feed_sums, sums_other, sums0, sums1),
    )
    vector_terms = [vector_part(vectors, 0)]
    vector_terms += [vector_part(move(vectors, mask), 0) for mask in (core, z_near, core ^ z_near)]
    au0, au1 = combine(
        me,
        [
            [[blocks(ak0, 4, 4), blocks(a0_c, 4, 4), blocks(a0_s2, 4, 4)]],
            [[blocks(ak1, 4, 4), blocks(a1_c, 4, 4), blocks(a1_s2, 4, 4)], vector_terms],
        ],
    )
    a0_s3 = move(au0, z_near)
    a1_s3 = move(au1, x)
    vector_terms = vector_terms + [vector_part(a1_s3, 4 * tall)]
    ar0, ar1, fr = combine(
        me,
        [
            [[blocks(a, 0, 4) for a in (ak0, a0_c, a0_s2)]],
            [[blocks(a, 0, 4) for a in (ak1, a1_c, a1_s2)]],
            [t + [blocks(f_y, 2 * h + 1, 1)] for h, t in enumerate(feed_terms(1, 1))],
        ],
        [au0], dtype=f32,
    )
    attn_terms = lambda start, size: [
        [blocks(a, start, size) for a in (ar0, a0_s3)], [blocks(a, start, size) for a in (ar1, a1_s3)]
    ]
    av, fv = combine(me, [attn_terms(2, 2) + [vector_terms], [[blocks(fr, 0, 2)]]])
    a_y = move(av, y)
    f_z = move(fv, z_far)
    vector_terms = vector_terms + [vector_part(a_y, 4 * tall)]
    aw, = combine(me, [[t + [blocks(a_y, 2 * h + 1, 1)] for h, t in enumerate(attn_terms(1, 1))] + [vector_terms]])
    a_z = move(aw, z_far)
    vector_terms = vector_terms + [vector_part(a_z, 2 * tall)]
    output_grad, hidden_grads = final(
        me, [t + [blocks(f_y, 2 * h, 1), blocks(f_z, h, 1)] for h, t in enumerate(feed_terms(0, 1))], depth, features,
        (1, 2),
    )
    attn_out, gain_grads, bias_grads = final(
        me, [t + [blocks(a_y, 2 * h, 1), blocks(a_z, h, 1)] for h, t in enumerate(attn_terms(0, 1))], depth, features,
        (3,), vector_terms,
    )

    latent_grads = lax.dynamic_update_slice_in_dim(latent_out, latent_back.astype(f32)[None], 1 - rank, 0)
    activations = lax.dynamic_update_slice_in_dim(result_own, result_back[None], 1 - rank, 0)
    return (
        activations[:, None],
        latent_grads[:, None],
        attn_out,
        output_grad[0],
        hidden_grads,
        gain_grads,
        bias_grads,
    )


def layer_norm(vector, gain_row, offset):
    centre = vector - jnp.mean(vector, axis=-1, keepdims=True)
    spread = jnp.mean(centre * centre, axis=-1, keepdims=True)
    return centre * lax.rsqrt(spread + EPSILON) * gain_row + offset


def on_device(
    latents, segments, attention_weights, output_weight, hidden_weights, gains, biases, cotangent
):
    micro_count = latents.shape[0]
    row_count = latents.shape[2]
    features = latents.shape[3]
    head_size = features // HEADS
    score_scale = 1.0 / math.sqrt(head_size)
    own_rank = lax.axis_index("row")
    attn_total = jnp.zeros((3, features, features), jnp.float32)
    output_total = jnp.zeros((features, features), jnp.float32)
    hidden_total = jnp.zeros((2, features, features), jnp.float32)
    gain_total = jnp.zeros((2, features), jnp.float32)
    bias_total = jnp.zeros((7, features), jnp.float32)
    outputs = []
    input_grads = []
    for micro_index in range(micro_count):
        gathered = (
            lax.all_gather(attention_weights, ("seq", "row"), axis=1, tiled=True),
            lax.all_gather(output_weight, ("seq", "row"), axis=0, tiled=True),
            lax.all_gather(hidden_weights, ("seq", "row"), axis=1, tiled=True),
            lax.all_gather(gains, ("seq", "row"), axis=1, tiled=True),
            lax.all_gather(biases, ("seq", "row"), axis=1, tiled=True),
        )
        attention_full, output_full, hidden_full, gain_full, bias_full = gathered
        gain_values = gain_full.astype(jnp.float32)
        bias_values = bias_full.astype(jnp.float32)
        inputs = latents[micro_index, 0].astype(jnp.float32)
        segment_all = segments[micro_index, 0]
        segment_own = lax.dynamic_slice_in_dim(segment_all, own_rank * row_count, row_count)
        normed_one, norm_one_pull = jax.vjp(layer_norm, inputs, gain_values[0], bias_values[0])
        normed_low = normed_one.astype(jnp.bfloat16)
        projected = jnp.einsum(
            "rd,cde->cre", normed_low, attention_full, preferred_element_type=jnp.float32
        )
        queries = (projected[0] + bias_values[2]).astype(jnp.bfloat16)
        own_keys = projected[1].astype(jnp.bfloat16)
        own_values = (projected[2] + bias_values[3]).astype(jnp.bfloat16)
        all_keys, all_values = (
            lax.all_gather(own_keys, "row", axis=0, tiled=True),
            lax.all_gather(own_values, "row", axis=0, tiled=True),
        )
        length = all_keys.shape[0]
        query_heads = queries.reshape(row_count, HEADS, head_size)
        key_heads = all_keys.reshape(length, HEADS, head_size)
        value_heads = all_values.reshape(length, HEADS, head_size)
        same_set = (segment_own[:, None] == segment_all[None, :])[None]
        raw_scores = (
            jnp.einsum("qhd,khd->hqk", query_heads, key_heads, preferred_element_type=jnp.float32)
            * score_scale
        )
        scores = jnp.where(same_set, raw_scores, -1e30)
        row_max = jnp.max(scores, axis=-1, keepdims=True)
        log_total = row_max + jnp.log(jnp.sum(jnp.exp(scores - row_max), axis=-1, keepdims=True))
        weights_low = jnp.exp(scores - log_total).astype(jnp.bfloat16)
        mixture = jnp.einsum(
            "hqk,khd->qhd", weights_low, value_heads, preferred_element_type=jnp.float32
        )
        mixture = mixture.reshape(row_count, features).astype(jnp.bfloat16)
        attended = (
            jnp.dot(mixture, output_full, preferred_element_type=jnp.float32) + bias_values[4]
        )
        residual_one = inputs + attended
        normed_two, norm_two_pull = jax.vjp(
            layer_norm, residual_one, gain_values[1], bias_values[1]
        )
        hidden_low = normed_two.astype(jnp.bfloat16)
        hidden_pre = (
            jnp.dot(hidden_low, hidden_full[0], preferred_element_type=jnp.float32) + bias_values[5]
        )
        activated, gelu_pull = jax.vjp(jax.nn.gelu, hidden_pre)
        active_low = activated.astype(jnp.bfloat16)
        result = residual_one + (
            jnp.dot(active_low, hidden_full[1], preferred_element_type=jnp.float32) + bias_values[6]
        )
        outputs.append(result.astype(jnp.bfloat16))
        live_rows = (segment_own >= 0).astype(jnp.bfloat16)[:, None]
        out_grad = cotangent[micro_index, 0] * live_rows
        out_grad_wide = out_grad.astype(jnp.float32)
        active_grad = jnp.dot(out_grad, hidden_full[1].T, preferred_element_type=jnp.float32)
        pre_grad = gelu_pull(active_grad)[0].astype(jnp.bfloat16)
        normed_two_grad = jnp.dot(pre_grad, hidden_full[0].T, preferred_element_type=jnp.float32)
        residual_part, gain_two, offset_two = norm_two_pull(normed_two_grad)
        residual_grad = out_grad_wide + residual_part
        residual_low = residual_grad.astype(jnp.bfloat16)
        mixture_grad = jnp.dot(residual_low, output_full.T, preferred_element_type=jnp.float32)
        mixture_grad = mixture_grad.astype(jnp.bfloat16).reshape(row_count, HEADS, head_size)
        raw_again = (
            jnp.einsum("qhd,khd->hqk", query_heads, key_heads, preferred_element_type=jnp.float32)
            * score_scale
        )
        weights_wide = jnp.exp(jnp.where(same_set, raw_again, -1e30) - log_total)
        weight_grads = jnp.einsum(
            "qhd,khd->hqk", mixture_grad, value_heads, preferred_element_type=jnp.float32
        )
        centred = jnp.sum(weights_wide * weight_grads, axis=-1, keepdims=True)
        score_grads = (weights_wide * (weight_grads - centred)).astype(jnp.bfloat16)
        query_grad = (
            jnp.einsum("hqk,khd->qhd", score_grads, key_heads, preferred_element_type=jnp.float32)
            * score_scale
        )
        query_grad = query_grad.astype(jnp.bfloat16).reshape(row_count, features)
        weights_again = weights_wide.astype(jnp.bfloat16)
        key_part = (
            jnp.einsum("hqk,qhd->khd", score_grads, query_heads, preferred_element_type=jnp.float32)
            * score_scale
        )
        value_part = jnp.einsum(
            "hqk,qhd->khd", weights_again, mixture_grad, preferred_element_type=jnp.float32
        )
        key_grad, value_grad = (
            lax.psum_scatter(
                key_part.reshape(length, features).astype(jnp.bfloat16),
                "row",
                scatter_dimension=0,
                tiled=True,
            ).astype(jnp.float32),
            lax.psum_scatter(
                value_part.reshape(length, features).astype(jnp.bfloat16),
                "row",
                scatter_dimension=0,
                tiled=True,
            ).astype(jnp.float32),
        )
        key_low = key_grad.astype(jnp.bfloat16)
        value_low = value_grad.astype(jnp.bfloat16)
        projection_grads = jnp.stack([query_grad, key_low, value_low])
        attn_total = attn_total + jnp.einsum(
            "rd,cre->cde", normed_low, projection_grads, preferred_element_type=jnp.float32
        )
        output_total = output_total + jnp.dot(
            mixture.T, residual_low, preferred_element_type=jnp.float32
        )
        hidden_total = hidden_total + jnp.stack(
            [
                jnp.dot(hidden_low.T, pre_grad, preferred_element_type=jnp.float32),
                jnp.dot(active_low.T, out_grad, preferred_element_type=jnp.float32),
            ]
        )
        normed_one_grad = jnp.einsum(
            "cre,cde->rd", projection_grads, attention_full, preferred_element_type=jnp.float32
        )
        input_part, gain_one, offset_one = norm_one_pull(normed_one_grad)
        input_grads.append(residual_grad + input_part)
        gain_total = gain_total + jnp.stack([gain_one, gain_two])
        bias_total = bias_total + jnp.stack(
            [
                offset_one,
                offset_two,
                jnp.sum(query_grad.astype(jnp.float32), axis=0),
                jnp.sum(value_low.astype(jnp.float32), axis=0),
                jnp.sum(residual_low.astype(jnp.float32), axis=0),
                jnp.sum(pre_grad.astype(jnp.float32), axis=0),
                jnp.sum(out_grad_wide, axis=0),
            ]
        )
    attn_grads, output_grads, hidden_grads, gain_grads, bias_grads = (
        lax.psum_scatter(attn_total, ("seq", "row"), scatter_dimension=1, tiled=True),
        lax.psum_scatter(output_total, ("seq", "row"), scatter_dimension=0, tiled=True),
        lax.psum_scatter(hidden_total, ("seq", "row"), scatter_dimension=1, tiled=True),
        lax.psum_scatter(gain_total, ("seq", "row"), scatter_dimension=1, tiled=True),
        lax.psum_scatter(bias_total, ("seq", "row"), scatter_dimension=1, tiled=True),
    )
    return (
        jnp.stack(outputs)[:, None],
        jnp.stack(input_grads)[:, None],
        attn_grads,
        output_grads,
        hidden_grads,
        gain_grads,
        bias_grads,
    )


def solution(mesh):
    def on_mesh(latents, *rest):
        shares_pair = mesh.shape["row"] == latents.shape[0] == 2
        fits = mesh.size == 1 << len(ORDERS[0]) and latents.shape[1] == mesh.shape["seq"]
        return shard_over(whole_sequence if shares_pair and fits else on_device)(latents, *rest)

    def shard_over(function):
        return jax.shard_map(
            function,
            mesh=mesh,
            in_specs=(
                P(None, "seq", "row", None),
                P(None, "seq", None),
                P(None, ("seq", "row"), None),
                P(("seq", "row"), None),
                P(None, ("seq", "row"), None),
                P(None, ("seq", "row")),
                P(None, ("seq", "row")),
                P(None, "seq", "row", None),
            ),
            out_specs=(
                P(None, "seq", "row", None),
                P(None, "seq", "row", None),
                P(None, ("seq", "row"), None),
                P(("seq", "row"), None),
                P(None, ("seq", "row"), None),
                P(None, ("seq", "row")),
                P(None, ("seq", "row")),
            ),
            check_vma=False,
        )

    return on_mesh
```
